32 devices in a mesh: frames: 16 (over z, y, x), dp: 2 (over core).
Axes of the slice: x: 2, y: 2, z: 4, core: 2. Of those that a mesh axis runs over, the one named last changes fastest.
Arguments:
- latents: bfloat16 [2, 16, 1024, 4], P('dp', 'frames'), may hold values from -6 to 6
- noise: bfloat16 [2, 16, 1024, 4], P('dp', 'frames'), may hold values from -6 to 6
- timesteps: int32 [2, 1], P('dp'), may hold values from 0 to 999
- image_flags: int32 [2, 1], P('dp'), may hold values 0 or 1
- frame_counts: int32 [2, 1], replicated, may hold values from 1 to 16, as said below
- text: bfloat16 [2, 1, 77, 768], P('dp'), may hold values from -6 to 6
- conv_in: bfloat16 [3, 3, 4, 320], replicated, may hold values from -1 to 1
- res_convs: bfloat16 [2, 3, 3, 320, 320], replicated, may hold values from -0.109375 to 0.109375
- conv_out: bfloat16 [3, 3, 320, 4], replicated, may hold values from -0.109375 to 0.109375
- time_w1: bfloat16 [320, 1280], replicated, may hold values from -0.3125 to 0.3125
- time_w2: bfloat16 [1280, 1280], replicated, may hold values from -0.15625 to 0.15625
- temb_w: bfloat16 [1280, 320], replicated, may hold values from -0.15625 to 0.15625
- spatial_squares: bfloat16 [8, 320, 320], replicated, may hold values from -0.3125 to 0.3125
- cross_kv: bfloat16 [768, 640], replicated, may hold values from -0.21875 to 0.21875
- spatial_up: bfloat16 [320, 2560], replicated, may hold values from -0.3125 to 0.3125
- spatial_down: bfloat16 [1280, 320], replicated, may hold values from -0.15625 to 0.15625
- frozen_vectors: float32 [23, 320], replicated
- motion_squares: float32 [10, 320, 320], replicated, may hold values from -0.3125 to 0.3125
- motion_up: float32 [320, 2560], replicated, may hold values from -0.3125 to 0.3125
- motion_down: float32 [1280, 320], replicated, may hold values from -0.15625 to 0.15625
- motion_vectors: float32 [13, 320], replicated
- square_moment: float32 [10, 320, 320], P('dp'), may hold values from -0.0048828125 to 0.0048828125
- up_moment: float32 [320, 2560], P(None, 'dp'), may hold values from -0.0048828125 to 0.0048828125
- down_moment: float32 [1280, 320], P('dp'), may hold values from -0.0048828125 to 0.0048828125
- vector_moment1: float32 [13, 320], replicated, may hold values from -0.00048828125 to 0.00048828125
- vector_moment2: float32 [13, 320], replicated, may hold values from 1.0986328e-10 to 4.394531e-10
- square_ema: float32 [10, 320, 320], P('dp'), may hold values from -0.3125 to 0.3125
- up_ema: float32 [320, 2560], P(None, 'dp'), may hold values from -0.3125 to 0.3125
- down_ema: float32 [1280, 320], P('dp'), may hold values from -0.15625 to 0.15625
- vector_ema: float32 [13, 320], replicated, may hold values from 0.5 to 1.5
Outputs:
- loss_sum: float32 [], replicated
- frame_total: float32 [], replicated
- square_weights_new: float32 [10, 320, 320], replicated
- square_moment_new: float32 [10, 320, 320], P('dp')
- square_ema_new: float32 [10, 320, 320], P('dp')
- up_weights_new: float32 [320, 2560], replicated
- up_moment_new: float32 [320, 2560], P(None, 'dp')
- up_ema_new: float32 [320, 2560], P(None, 'dp')
- down_weights_new: float32 [1280, 320], replicated
- down_moment_new: float32 [1280, 320], P('dp')
- down_ema_new: float32 [1280, 320], P('dp')
- vector_moment1_new: float32 [13, 320], replicated
- vector_moment2_new: float32 [13, 320], replicated
- vector_weights_new: float32 [13, 320], replicated
- vector_ema_new: float32 [13, 320], replicated
The draws below stay inside these ranges and needn't reach their ends.
Inputs may be any that keep to these rules, and one draw needn't show every extreme that they name: `frame_counts`: the first that many of a sample's 16 frames are valid; in each group one sample has all 16 frames valid.
All inputs are finite; a program needn't handle non-finite values. No bound on the sum of `image_flags` on one device may be relied on, other than what follows from the above.
Results may differ from the reference program's by a relative error of at most 0.0094.
Values may be sent and summed in bfloat16 or wider, within the bound.
No kernel may reach another device: no remote copies, remote signals or barrier semaphores. Data moves between devices by JAX's collectives and lax.ppermute only.
A program may use at most 256 MiB of HBM per device.

```python
import math
import jax
import jax.numpy as jnp
from jax import lax

WIDTH = 320
HEADS = 8
HEAD_DIM = 40
FF_INNER = 1280
TEXT_LEN = 77
TEXT_DIM = 768
TIME_DIM = 1280
GN_GROUPS = 32
CLIP = 16
LATENT = 32
F_DEV = 1
STEP = 10
NVEC = 13
NFROZEN = 23
PIX = 1024
GROUPS = 2
GFRAMES = 16
GSAMPLES = 1
N_FRAMES = 16
N_DP = 2


def vector_rows(key, count, gain_rows):
    noise_rows = 0.15 * jax.random.normal(key, (count, WIDTH), jnp.float32)
    positions = jnp.arange(count)[:, None]
    marks = jnp.zeros((count, 1), jnp.float32)
    for row_id in gain_rows:
        marks = marks + (positions == row_id).astype(jnp.float32)
    return noise_rows + marks


def draw_motion_vectors(key, part):
    key = jax.random.fold_in(key, 7)
    return vector_rows(key, NVEC, (0, 3, 6, 9))


def draw_frozen_vectors(key, part):
    key = jax.random.fold_in(key, 8)
    return vector_rows(key, NFROZEN, (1, 4, 7, 10, 13, 16, 20))


def draw_frame_counts(key, part):
    key = jax.random.fold_in(key, 9)
    full_key, count_key = jax.random.split(key)
    order = jnp.arange(GSAMPLES, dtype=jnp.int32)[None, :]
    span = max(GSAMPLES - 1, 1)
    lowest = 1 + (CLIP // 2 - 1) * order // span
    raw = jax.random.randint(count_key, (GROUPS, GSAMPLES), 0, 1 << 20, dtype=jnp.int32)
    counts = lowest + raw % (CLIP + 1 - lowest)
    chosen = jax.random.randint(full_key, (GROUPS, 1), 0, GSAMPLES, dtype=jnp.int32)
    counts = jnp.where(order == chosen, CLIP, counts)
    return counts.astype(jnp.int32)


def touch_ends(values, rng, smallest, high):
    shape = values.shape
    spot = [jax.random.randint(jax.random.fold_in(rng, axis), (), 0, shape[axis]) for axis in range(len(shape))]
    values = values.at[tuple(spot)].set(smallest)
    longest = shape.index(max(shape))
    spot[longest] = (spot[longest] + 1) % shape[longest]
    return values.at[tuple(spot)].set(high)


def steps_of(own_key, shape, shards, least, top_value):
    def one(axis_at, parts):
        draws = jax.random.uniform(jax.random.fold_in(jax.random.fold_in(own_key, 6), axis_at), (parts,), jnp.float32, least / len(shards), top_value / len(shards))
        return jnp.repeat(jnp.exp(draws), shape[axis_at] // parts).reshape((-1,) + (1,) * (len(shape) - axis_at - 1))

    gain = one(*shards[0])
    for cut in shards[1:]:
        gain = gain * one(*cut)
    return gain


def scatter_about(stream_key, dims, width, limit, pieces=(), kind=jnp.bfloat16):
    array = width * jax.random.normal(stream_key, dims, jnp.float32)
    if pieces:
        array = array * steps_of(stream_key, dims, pieces, -0.22, 0.18)
    return jnp.clip(array, -limit, limit).astype(kind)


def setup_inputs(seed: int = 0) -> dict:
    arg_keys = jax.random.split(jax.random.key(seed), 31)
    latents = scatter_about(arg_keys[0], (GROUPS, GFRAMES, PIX, 4), 1.0, 6.0, ((0, 2), (1, 16)))
    noise = scatter_about(arg_keys[1], (GROUPS, GFRAMES, PIX, 4), 1.0, 6.0, ((0, 2), (1, 16)))
    timesteps = jax.random.randint(arg_keys[2], (GROUPS, GSAMPLES), 0, 1000).astype(jnp.int32)
    image_flags = touch_ends((jax.random.randint(arg_keys[3], (GROUPS, GSAMPLES), 0, 4) < 1).astype(jnp.int32), jax.random.fold_in(arg_keys[3], 1), 0, 1)
    frame_counts = draw_frame_counts(jax.random.fold_in(arg_keys[30], 71), 0)
    text = scatter_about(arg_keys[5], (GROUPS, GSAMPLES, TEXT_LEN, TEXT_DIM), 1.0, 6.0, ((0, 2),))
    conv_in = scatter_about(arg_keys[6], (3, 3, 4, WIDTH), 36 ** -0.5, 1.0)
    res_convs = scatter_about(arg_keys[7], (2, 3, 3, WIDTH, WIDTH), (9 * WIDTH) ** -0.5, 0.109375)
    conv_out = scatter_about(arg_keys[8], (3, 3, WIDTH, 4), (9 * WIDTH) ** -0.5, 0.109375)
    time_w1 = scatter_about(arg_keys[9], (WIDTH, TIME_DIM), WIDTH ** -0.5, 0.3125)
    time_w2 = scatter_about(arg_keys[10], (TIME_DIM, TIME_DIM), TIME_DIM ** -0.5, 0.15625)
    temb_w = scatter_about(arg_keys[11], (TIME_DIM, WIDTH), TIME_DIM ** -0.5, 0.15625)
    spatial_squares = scatter_about(arg_keys[12], (8, WIDTH, WIDTH), WIDTH ** -0.5, 0.3125)
    cross_kv = scatter_about(arg_keys[13], (TEXT_DIM, 2 * WIDTH), TEXT_DIM ** -0.5, 0.21875)
    spatial_up = scatter_about(arg_keys[14], (WIDTH, 2 * FF_INNER), WIDTH ** -0.5, 0.3125)
    spatial_down = scatter_about(arg_keys[15], (FF_INNER, WIDTH), FF_INNER ** -0.5, 0.15625)
    frozen_vectors = draw_frozen_vectors(jax.random.fold_in(arg_keys[30], 71), 0)
    motion_squares = scatter_about(arg_keys[17], (10, WIDTH, WIDTH), WIDTH ** -0.5, 0.3125, (), jnp.float32)
    motion_up = scatter_about(arg_keys[18], (WIDTH, 2 * FF_INNER), WIDTH ** -0.5, 0.3125, (), jnp.float32)
    motion_down = scatter_about(arg_keys[19], (FF_INNER, WIDTH), FF_INNER ** -0.5, 0.15625, (), jnp.float32)
    motion_vectors = draw_motion_vectors(jax.random.fold_in(arg_keys[30], 71), 0)
    square_moment = scatter_about(arg_keys[21], (10, WIDTH, WIDTH), (0.06 / (N_DP * F_DEV * N_FRAMES * PIX) ** 0.5), 0.0048828125, ((0, 2),), jnp.float32)
    up_moment = scatter_about(arg_keys[22], (WIDTH, 2 * FF_INNER), (0.06 / (N_DP * F_DEV * N_FRAMES * PIX) ** 0.5), 0.0048828125, ((1, 2),), jnp.float32)
    down_moment = scatter_about(arg_keys[23], (FF_INNER, WIDTH), (0.06 / (N_DP * F_DEV * N_FRAMES * PIX) ** 0.5), 0.0048828125, ((0, 2),), jnp.float32)
    vector_moment1 = scatter_about(arg_keys[24], (NVEC, WIDTH), (0.0066 / (N_DP * F_DEV * N_FRAMES * PIX) ** 0.5), 0.00048828125, (), jnp.float32)
    vector_moment2 = jnp.clip(jnp.exp(jax.random.uniform(arg_keys[25], (NVEC, WIDTH), jnp.float32, math.log(1.0986327819706432e-10), math.log(4.3945311278825727e-10))), 1.0986327819706432e-10, 4.3945311278825727e-10)
    square_ema = scatter_about(arg_keys[26], (10, WIDTH, WIDTH), WIDTH ** -0.5, 0.3125, ((0, 2),), jnp.float32)
    up_ema = scatter_about(arg_keys[27], (WIDTH, 2 * FF_INNER), WIDTH ** -0.5, 0.3125, ((1, 2),), jnp.float32)
    down_ema = scatter_about(arg_keys[28], (FF_INNER, WIDTH), FF_INNER ** -0.5, 0.15625, ((0, 2),), jnp.float32)
    vector_ema = jnp.clip(1.0 + 0.1 * jax.random.normal(arg_keys[29], (NVEC, WIDTH), jnp.float32), 0.5, 1.5)
    return {"latents": latents, "noise": noise, "timesteps": timesteps, "image_flags": image_flags, "frame_counts": frame_counts, "text": text, "conv_in": conv_in, "res_convs": res_convs, "conv_out": conv_out, "time_w1": time_w1, "time_w2": time_w2, "temb_w": temb_w, "spatial_squares": spatial_squares, "cross_kv": cross_kv, "spatial_up": spatial_up, "spatial_down": spatial_down, "frozen_vectors": frozen_vectors, "motion_squares": motion_squares, "motion_up": motion_up, "motion_down": motion_down, "motion_vectors": motion_vectors, "square_moment": square_moment, "up_moment": up_moment, "down_moment": down_moment, "vector_moment1": vector_moment1, "vector_moment2": vector_moment2, "square_ema": square_ema, "up_ema": up_ema, "down_ema": down_ema, "vector_ema": vector_ema}


PRECISE = lax.Precision.HIGHEST
MUON_RATE = 0.2
ADAM_RATE = 0.4
DECAY = 0.01
AVERAGE = 0.75

@jax.custom_vjp
def low(v):
    return lax.optimization_barrier(v.astype(jnp.bfloat16)).astype(jnp.float32)

@jax.custom_vjp
def low_back(v):
    return v

def low_keep(v):
    return (low(v), None)

def low_pass(kept, grad):
    return (grad,)

def back_keep(v):
    return (v, None)

def back_low(kept, grad):
    return (low(grad),)
low.defvjp(low_keep, low_pass)
low_back.defvjp(back_keep, back_low)

def unchanged(values):
    return values

def matmul(left, right):
    return jnp.einsum('...i,ij->...j', left, right, precision=PRECISE)

def convolve(values, kernel):
    leading = values.shape[:-2]
    images = values.reshape((-1, LATENT, LATENT, values.shape[-1]))
    result = lax.conv_general_dilated(images, kernel, (1, 1), 'SAME', dimension_numbers=('NHWC', 'HWIO', 'NHWC'), precision=PRECISE)
    return result.reshape(leading + (PIX, kernel.shape[-1]))

def group_norm(values, scaling, offset):
    full_shape = values.shape
    grouped = values.reshape(full_shape[:-1] + (GN_GROUPS, full_shape[-1] // GN_GROUPS))
    centre = lax.optimization_barrier(jnp.mean(grouped, axis=(-3, -1), keepdims=True))
    spread = lax.optimization_barrier(jnp.mean(jnp.square(grouped - centre), axis=(-3, -1), keepdims=True))
    return ((grouped - centre) * lax.rsqrt(spread + 1e-05)).reshape(full_shape) * scaling + offset

def layer_norm(values, scaling, offset):
    centre = lax.optimization_barrier(jnp.mean(values, axis=-1, keepdims=True))
    spread = lax.optimization_barrier(jnp.mean(jnp.square(values - centre), axis=-1, keepdims=True))
    return (values - centre) * lax.rsqrt(spread + 1e-05) * scaling + offset

def gated_gelu(gate_up):
    return gate_up[..., :FF_INNER] * jax.nn.gelu(gate_up[..., FF_INNER:], approximate=False)

def frame_codes():
    positions = jnp.arange(CLIP, dtype=jnp.float32)[:, None]
    column = jnp.arange(WIDTH)
    frequency = jnp.exp(-math.log(10000.0) * (2 * (column // 2)).astype(jnp.float32) / WIDTH)
    angles = positions * frequency
    return jnp.where(column % 2 == 0, jnp.sin(angles), jnp.cos(angles))

def attend(queries, key_vecs, values, masking, rounding):
    leading = queries.shape[:-2]
    query_heads = queries.reshape(leading + (queries.shape[-2], HEADS, HEAD_DIM))
    key_heads = key_vecs.reshape(leading + (key_vecs.shape[-2], HEADS, HEAD_DIM))
    value_heads = values.reshape(leading + (values.shape[-2], HEADS, HEAD_DIM))
    scores = rounding(jnp.einsum('...qhd,...khd->...hqk', query_heads, key_heads, precision=PRECISE) / math.sqrt(HEAD_DIM)) + masking
    probs_low = low(jax.nn.softmax(scores, axis=-1))
    mixture = jnp.einsum('...hqk,...khd->...qhd', probs_low, value_heads, precision=PRECISE)
    return low(rounding(mixture.reshape(leading + (queries.shape[-2], WIDTH))))

def time_embed(step_values, time_w1, time_w2, temb_w, temb_bias):
    half_width = WIDTH // 2
    frequency = jnp.exp(-math.log(10000.0) * jnp.arange(half_width, dtype=jnp.float32) / half_width)
    angles = step_values[..., None] * frequency
    encoding = jnp.concatenate([jnp.cos(angles), jnp.sin(angles)], axis=-1)
    hidden = matmul(low(encoding), time_w1)
    hidden = matmul(low(jax.nn.silu(hidden)), time_w2)
    return matmul(low(jax.nn.silu(hidden)), temb_w) + temb_bias

def frame_forward(noisy_frame, temb_row, text_rows, frozen):
    conv_in, res_convs, squares, cross_kv, spatial_up, spatial_down, vectors = frozen
    first_conv = convolve(low(noisy_frame), conv_in) + vectors[0]
    inner_act = convolve(low(jax.nn.silu(group_norm(first_conv, vectors[1], vectors[2]))), res_convs[0]) + vectors[3] + temb_row
    inner_act = convolve(low(jax.nn.silu(group_norm(inner_act, vectors[4], vectors[5]))), res_convs[1]) + vectors[6]
    resnet = first_conv + inner_act
    tokens = matmul(low(group_norm(resnet, vectors[7], vectors[8])), squares[0]) + vectors[9]
    normal_a = low(layer_norm(tokens, vectors[10], vectors[11]))
    mixture = attend(low(matmul(normal_a, squares[1])), low(matmul(normal_a, squares[2])), low(matmul(normal_a, squares[3])), 0.0, unchanged)
    tokens = tokens + (matmul(mixture, squares[4]) + vectors[12])
    normal_c = low(layer_norm(tokens, vectors[13], vectors[14]))
    text_kv = low(matmul(text_rows, cross_kv))
    mixture = attend(low(matmul(normal_c, squares[5])), text_kv[:, :WIDTH], text_kv[:, WIDTH:], 0.0, unchanged)
    tokens = tokens + (matmul(mixture, squares[6]) + vectors[15])
    normal_f = low(layer_norm(tokens, vectors[16], vectors[17]))
    tokens = tokens + (matmul(low(gated_gelu(matmul(normal_f, spatial_up))), spatial_down) + vectors[18])
    return resnet + (matmul(low(tokens), squares[7]) + vectors[19])

def motion_branch(normed, masking, keep_video, params):
    squares, up_weight, down_weight, vectors = params
    squares_low, up_low, down_low = (low(squares), low(up_weight), low(down_weight))
    inputs = low(normed * vectors[0] + vectors[1])
    stream = low_back(matmul(inputs, squares_low[0]) + vectors[2])
    for first, vec in ((1, 3), (5, 6)):
        normal_a = low(layer_norm(stream, vectors[vec], vectors[vec + 1]) + frame_codes())
        queries = low(low_back(matmul(normal_a, squares_low[first])))
        key_vecs = low(low_back(matmul(normal_a, squares_low[first + 1])))
        values = low(low_back(matmul(normal_a, squares_low[first + 2])))
        mixture = attend(queries, key_vecs, values, masking, low_back)
        stream = stream + low_back(matmul(mixture, squares_low[first + 3]) + vectors[vec + 2])
    normal_c = low(layer_norm(stream, vectors[9], vectors[10]))
    gate_up = low_back(matmul(normal_c, up_low))
    final_u = stream + low_back(matmul(low(gated_gelu(gate_up)), down_low) + vectors[11])
    return low(low_back((matmul(low(final_u), squares_low[9]) + vectors[12]) * keep_video))

def orthogonalize(matrix):
    is_tall = matrix.shape[0] > matrix.shape[1]
    current = matrix.T if is_tall else matrix
    current = current / (jnp.sqrt(jnp.sum(current * current)) + 1e-07)
    for _ in range(5):
        gram_matrix = jnp.dot(current, current.T, precision=PRECISE)
        polynomial = -4.775 * gram_matrix + 2.0315 * jnp.dot(gram_matrix, gram_matrix, precision=PRECISE)
        current = 3.4445 * current + jnp.dot(polynomial, current, precision=PRECISE)
    return current.T if is_tall else current

def muon_step(weight, moment, gradient):
    moment_new = 0.95 * moment + gradient
    direction = orthogonalize(gradient + 0.95 * moment_new)
    step_scale = MUON_RATE * 0.2 * math.sqrt(max(weight.shape))
    return (weight * (1.0 - MUON_RATE * DECAY) - step_scale * direction, moment_new)

def reference(latents, noise, timesteps, image_flags, frame_counts, text, conv_in, res_convs, conv_out, time_w1, time_w2, temb_w, spatial_squares, cross_kv, spatial_up, spatial_down, frozen_vectors, motion_squares, motion_up, motion_down, motion_vectors, square_moment, up_moment, down_moment, vector_moment1, vector_moment2, square_ema, up_ema, down_ema, vector_ema):
    single = jnp.float32
    frozen = tuple((member.astype(single) for member in (conv_in, res_convs, spatial_squares, cross_kv, spatial_up, spatial_down, frozen_vectors)))
    vectors = frozen[6]
    step_values = timesteps.astype(single)
    phases = (step_values / 1000.0 + 0.008) / 1.008 * (math.pi / 2)
    keep_rate = jnp.repeat(jnp.cos(phases), CLIP, axis=1)[:, :, None, None]
    noise_rate = jnp.repeat(jnp.sin(phases), CLIP, axis=1)[:, :, None, None]
    clean_latent = latents.astype(single)
    drawn_noise = noise.astype(single)
    noisy = keep_rate * clean_latent + noise_rate * drawn_noise
    target = keep_rate * drawn_noise - noise_rate * clean_latent
    temb_res = time_embed(step_values, time_w1.astype(single), time_w2.astype(single), temb_w.astype(single), vectors[22])
    temb_frames = jnp.repeat(temb_res, CLIP, axis=1).reshape(-1, WIDTH)
    text_frames = jnp.repeat(text.astype(single), CLIP, axis=1).reshape(-1, TEXT_LEN, TEXT_DIM)
    hidden = lax.map(lambda bundle: frame_forward(bundle[0], bundle[1], bundle[2], frozen), (noisy.reshape(-1, PIX, 4), temb_frames, text_frames))
    normed = low(group_norm(hidden, 1.0, 0.0))
    samples = GROUPS * GSAMPLES
    valid_frames = (jnp.arange(CLIP)[None, :] < frame_counts.reshape(samples, 1)).astype(single)
    masking = jnp.where(valid_frames > 0.5, 0.0, -1e+30).astype(single)
    keep_video = 1.0 - image_flags.reshape(samples).astype(single)
    total_count = 4.0 * PIX * jnp.sum(frame_counts).astype(single)
    conv_head = conv_out.astype(single)

    def sample_loss(params, bundle):
        normed_s, hidden_s, target_s, valid_s, masking_s, keep_s = bundle
        branch = motion_branch(jnp.swapaxes(normed_s, 0, 1), masking_s, keep_s, params)
        mixed_h = hidden_s + jnp.swapaxes(branch, 0, 1)
        activation = low(jax.nn.silu(group_norm(mixed_h, vectors[20], vectors[21])))
        predicted = low_back(convolve(activation, conv_head))
        return jnp.sum(valid_s[:, None, None] * jnp.square(predicted - target_s))
    checked = jax.checkpoint(sample_loss)
    data = (normed.reshape(samples, CLIP, PIX, WIDTH), hidden.reshape(samples, CLIP, PIX, WIDTH), target.reshape(samples, CLIP, PIX, 4), valid_frames, masking, keep_video)

    def objective(params):
        return jnp.sum(lax.map(lambda bundle: checked(params, bundle), data))
    params = (motion_squares, motion_up, motion_down, motion_vectors)
    loss_sum, pullback = jax.vjp(objective, params)
    grad_sq, grad_up, grad_down, grad_vec = pullback(jnp.ones_like(loss_sum) / total_count)[0]
    outcomes = [muon_step(motion_squares[matrix_id], square_moment[matrix_id], grad_sq[matrix_id]) for matrix_id in range(10)]
    square_new = jnp.stack([outcome[0] for outcome in outcomes])
    square_moment_new = jnp.stack([outcome[1] for outcome in outcomes])
    up_new, up_moment_new = muon_step(motion_up, up_moment, grad_up)
    down_new, down_moment_new = muon_step(motion_down, down_moment, grad_down)
    moment_first = 0.9 * vector_moment1 + 0.1 * grad_vec
    moment_second = 0.999 * vector_moment2 + 0.001 * jnp.square(grad_vec)
    adjusted = moment_first / (1.0 - 0.9 ** STEP) / (jnp.sqrt(moment_second / (1.0 - 0.999 ** STEP)) + 1e-08)
    vector_new = motion_vectors - ADAM_RATE * (adjusted + DECAY * motion_vectors)
    return (loss_sum, total_count, square_new, square_moment_new, AVERAGE * square_ema + (1.0 - AVERAGE) * square_new, up_new, up_moment_new, AVERAGE * up_ema + (1.0 - AVERAGE) * up_new, down_new, down_moment_new, AVERAGE * down_ema + (1.0 - AVERAGE) * down_new, moment_first, moment_second, vector_new, AVERAGE * vector_ema + (1.0 - AVERAGE) * vector_new)
```

```python
import math

import jax
import jax.numpy as jnp
from jax import lax
from jax.experimental import pallas as pl
from jax.experimental.pallas import tpu as pltpu
from jax.sharding import PartitionSpec as P

WIDTH = 320
HEADS = 8
HEAD_DIM = 40
FF_INNER = 1280
TEXT_LEN = 77
TEXT_DIM = 768
GN_GROUPS = 32
CLIP = 16
LATENT = 32
STEP = 10
PIX = 1024


PRECISE = lax.Precision.HIGHEST
MUON_RATE = 0.2
ADAM_RATE = 0.4
DECAY = 0.01
AVERAGE = 0.75


def to_low(values):
    return values.astype(jnp.bfloat16)


def product(left, right):
    return jnp.einsum("...i,ij->...j", left, right, preferred_element_type=jnp.float32)


def product_back(left, right):
    return jnp.einsum("...j,ij->...i", left, right, preferred_element_type=jnp.float32)


def convolve(values, kernel):
    leading = values.shape[:-2]
    images = values.reshape((-1, LATENT, LATENT, values.shape[-1]))
    result = lax.conv_general_dilated(
        images,
        kernel,
        (1, 1),
        "SAME",
        dimension_numbers=("NHWC", "HWIO", "NHWC"),
        preferred_element_type=jnp.float32,
    )
    return result.reshape(leading + (PIX, kernel.shape[-1]))


def group_norm(values, scaling, offset):
    full_shape = values.shape
    grouped = values.reshape(full_shape[:-1] + (GN_GROUPS, full_shape[-1] // GN_GROUPS))
    centre = jnp.mean(grouped, axis=(-3, -1), keepdims=True)
    spread = jnp.mean(jnp.square(grouped - centre), axis=(-3, -1), keepdims=True)
    return ((grouped - centre) * lax.rsqrt(spread + 1e-05)).reshape(full_shape) * scaling + offset


def layer_norm(values, scaling, offset):
    centre = jnp.mean(values, axis=-1, keepdims=True)
    spread = jnp.mean(jnp.square(values - centre), axis=-1, keepdims=True)
    return (values - centre) * lax.rsqrt(spread + 1e-05) * scaling + offset


def gated_gelu(gate_up):
    return gate_up[..., :FF_INNER] * jax.nn.gelu(gate_up[..., FF_INNER:], approximate=False)


def frame_codes():
    positions = jnp.arange(CLIP, dtype=jnp.float32)[:, None]
    column = jnp.arange(WIDTH)
    frequency = jnp.exp(-math.log(10000.0) * (2 * (column // 2)).astype(jnp.float32) / WIDTH)
    angles = positions * frequency
    return jnp.where(column % 2 == 0, jnp.sin(angles), jnp.cos(angles))


def spatial_attend(queries, key_vecs, values):
    query_heads = queries.reshape(queries.shape[0], HEADS, HEAD_DIM)
    key_heads = key_vecs.reshape(key_vecs.shape[0], HEADS, HEAD_DIM)
    value_heads = values.reshape(values.shape[0], HEADS, HEAD_DIM)
    scores = jnp.einsum(
        "qhd,khd->hqk", query_heads, key_heads, preferred_element_type=jnp.float32
    ) / math.sqrt(HEAD_DIM)
    probs_low = to_low(jax.nn.softmax(scores, axis=-1))
    mixture = jnp.einsum("hqk,khd->qhd", probs_low, value_heads, preferred_element_type=jnp.float32)
    return to_low(mixture.reshape(queries.shape[0], WIDTH))


def time_embed(step_values, time_w1, time_w2, temb_w, temb_bias):
    half_width = WIDTH // 2
    frequency = jnp.exp(-math.log(10000.0) * jnp.arange(half_width, dtype=jnp.float32) / half_width)
    angles = step_values[..., None] * frequency
    encoding = jnp.concatenate([jnp.cos(angles), jnp.sin(angles)], axis=-1)
    hidden = product(to_low(encoding), time_w1)
    hidden = product(to_low(jax.nn.silu(hidden)), time_w2)
    return product(to_low(jax.nn.silu(hidden)), temb_w) + temb_bias


def frame_forward(noisy_frame, temb_row, text_rows, frozen):
    conv_in, res_convs, squares, cross_kv, spatial_up, spatial_down, vectors = frozen
    first_conv = convolve(to_low(noisy_frame), conv_in) + vectors[0]
    inner_act = (
        convolve(to_low(jax.nn.silu(group_norm(first_conv, vectors[1], vectors[2]))), res_convs[0])
        + vectors[3]
        + temb_row
    )
    inner_act = (
        convolve(to_low(jax.nn.silu(group_norm(inner_act, vectors[4], vectors[5]))), res_convs[1])
        + vectors[6]
    )
    resnet = first_conv + inner_act
    tokens = product(to_low(group_norm(resnet, vectors[7], vectors[8])), squares[0]) + vectors[9]
    normal_a = to_low(layer_norm(tokens, vectors[10], vectors[11]))
    mixture = spatial_attend(
        to_low(product(normal_a, squares[1])),
        to_low(product(normal_a, squares[2])),
        to_low(product(normal_a, squares[3])),
    )
    tokens = tokens + (product(mixture, squares[4]) + vectors[12])
    normal_c = to_low(layer_norm(tokens, vectors[13], vectors[14]))
    text_kv = to_low(product(text_rows, cross_kv))
    mixture = spatial_attend(
        to_low(product(normal_c, squares[5])), text_kv[:, :WIDTH], text_kv[:, WIDTH:]
    )
    tokens = tokens + (product(mixture, squares[6]) + vectors[15])
    normal_f = to_low(layer_norm(tokens, vectors[16], vectors[17]))
    tokens = tokens + (
        product(to_low(gated_gelu(product(normal_f, spatial_up))), spatial_down) + vectors[18]
    )
    return resnet + (product(to_low(tokens), squares[7]) + vectors[19])


def temporal_forward(stream, squares, first, gain, offset, masking):
    normal_a = to_low(layer_norm(stream, gain, offset) + frame_codes())
    queries = to_low(product(normal_a, squares[first]))
    key_vecs = to_low(product(normal_a, squares[first + 1]))
    values = to_low(product(normal_a, squares[first + 2]))
    head_shape = queries.shape[:-1] + (HEADS, HEAD_DIM)
    scores = (
        jnp.einsum(
            "psfhd,psehd->pshfe",
            queries.reshape(head_shape),
            key_vecs.reshape(head_shape),
            preferred_element_type=jnp.float32,
        )
        / math.sqrt(HEAD_DIM)
        + masking[None, :, None, None, :]
    )
    softmaxed = jax.nn.softmax(scores, axis=-1)
    probs_low = to_low(softmaxed)
    mixture = to_low(
        jnp.einsum(
            "pshfe,psehd->psfhd",
            probs_low,
            values.reshape(head_shape),
            preferred_element_type=jnp.float32,
        ).reshape(queries.shape)
    )
    return (mixture, (normal_a, queries, key_vecs, values, softmaxed, probs_low, mixture))


def motion_forward(arrived, masking, keep_video, low_weights, vectors):
    squares, up_weight, down_weight = low_weights
    inputs = to_low(arrived.astype(jnp.float32) * vectors[0] + vectors[1])
    motion_u = product(inputs, squares[0]) + vectors[2]
    mixture, kept_first = temporal_forward(motion_u, squares, 1, vectors[3], vectors[4], masking)
    middle = motion_u + (product(mixture, squares[4]) + vectors[5])
    mixture, kept_second = temporal_forward(middle, squares, 5, vectors[6], vectors[7], masking)
    upper = middle + (product(mixture, squares[8]) + vectors[8])
    normal_c = to_low(layer_norm(upper, vectors[9], vectors[10]))
    gate_up = product(normal_c, up_weight)
    inner_act = to_low(gated_gelu(gate_up))
    final_u = upper + (product(inner_act, down_weight) + vectors[11])
    final_low = to_low(final_u)
    branch = to_low((product(final_low, squares[9]) + vectors[12]) * keep_video)
    saved = (
        inputs,
        motion_u,
        kept_first,
        middle,
        kept_second,
        upper,
        normal_c,
        gate_up,
        inner_act,
        final_low,
    )
    return (branch, saved)


def contract(left, right):
    return jnp.einsum("psfi,psfj->ij", left, right, preferred_element_type=jnp.float32)


def column_sum(values):
    return jnp.sum(values.astype(jnp.float32), axis=(0, 1, 2))


def temporal_backward(grad_stream, stream, squares, first, gain, offset, kept):
    normal_a, queries, key_vecs, values, softmaxed, probs_low, mixture = kept
    head_shape = queries.shape[:-1] + (HEADS, HEAD_DIM)
    grad_attn = to_low(grad_stream)
    w_o_grad = contract(mixture, grad_attn)
    b_o_grad = column_sum(grad_attn)
    grad_mixture = to_low(product_back(grad_attn, squares[first + 3])).reshape(head_shape)
    grad_values = jnp.einsum(
        "pshfe,psfhd->psehd", probs_low, grad_mixture, preferred_element_type=jnp.float32
    )
    grad_probs = jnp.einsum(
        "psfhd,psehd->pshfe",
        grad_mixture,
        values.reshape(head_shape),
        preferred_element_type=jnp.float32,
    )
    grad_scores = to_low(
        softmaxed * (grad_probs - jnp.sum(softmaxed * grad_probs, axis=-1, keepdims=True))
    )
    grad_queries = to_low(
        (
            jnp.einsum(
                "pshfe,psehd->psfhd",
                grad_scores,
                key_vecs.reshape(head_shape),
                preferred_element_type=jnp.float32,
            )
            / math.sqrt(HEAD_DIM)
        ).reshape(queries.shape)
    )
    grad_keys = to_low(
        (
            jnp.einsum(
                "pshfe,psfhd->psehd",
                grad_scores,
                queries.reshape(head_shape),
                preferred_element_type=jnp.float32,
            )
            / math.sqrt(HEAD_DIM)
        ).reshape(queries.shape)
    )
    grad_values_low = to_low(grad_values.reshape(queries.shape))
    w_q_grad = contract(normal_a, grad_queries)
    w_k_grad = contract(normal_a, grad_keys)
    w_v_grad = contract(normal_a, grad_values_low)
    grad_normal_a = (
        product_back(grad_queries, squares[first])
        + product_back(grad_keys, squares[first + 1])
        + product_back(grad_values_low, squares[first + 2])
    )
    grad_ln, gain_grad, offset_grad = jax.vjp(layer_norm, stream, gain, offset)[1](grad_normal_a)
    return (
        grad_stream + grad_ln,
        (w_q_grad, w_k_grad, w_v_grad, w_o_grad),
        (gain_grad, offset_grad, b_o_grad),
    )


def motion_backward(grad_in, arrived, keep_video, low_weights, vectors, saved):
    squares, up_weight, down_weight = low_weights
    (
        inputs,
        motion_u,
        kept_first,
        middle,
        kept_second,
        upper,
        normal_c,
        gate_up,
        inner_act,
        final_low,
    ) = saved
    grad_branch = grad_in * to_low(keep_video)
    w_out_grad = contract(final_low, grad_branch)
    b_out_grad = column_sum(grad_branch)
    grad_last = product_back(grad_branch, squares[9])
    grad_ffn = to_low(grad_last)
    w_down_grad = contract(inner_act, grad_ffn)
    b_down_grad = column_sum(grad_ffn)
    grad_inner = product_back(grad_ffn, down_weight)
    grad_gate_up = to_low(jax.vjp(gated_gelu, gate_up)[1](grad_inner)[0])
    w_up_grad = contract(normal_c, grad_gate_up)
    grad_normal_c = product_back(grad_gate_up, up_weight)
    grad_upper_ln, g_ln3, b_ln3 = jax.vjp(layer_norm, upper, vectors[9], vectors[10])[1](
        grad_normal_c
    )
    grad_upper = grad_last + grad_upper_ln
    grad_middle, second_w, second_v = temporal_backward(
        grad_upper, middle, squares, 5, vectors[6], vectors[7], kept_second
    )
    grad_u_sum, first_w, first_v = temporal_backward(
        grad_middle, motion_u, squares, 1, vectors[3], vectors[4], kept_first
    )
    grad_motion_u = to_low(grad_u_sum)
    w_in_grad = contract(inputs, grad_motion_u)
    b_in_grad = column_sum(grad_motion_u)
    grad_inputs = product_back(grad_motion_u, squares[0])
    g_norm = jnp.sum(grad_inputs * arrived.astype(jnp.float32), axis=(0, 1, 2))
    b_norm = jnp.sum(grad_inputs, axis=(0, 1, 2))
    square_grads = jnp.stack(
        [
            w_in_grad,
            first_w[0],
            first_w[1],
            first_w[2],
            first_w[3],
            second_w[0],
            second_w[1],
            second_w[2],
            second_w[3],
            w_out_grad,
        ]
    )
    vector_grads = jnp.stack(
        [
            g_norm,
            b_norm,
            b_in_grad,
            first_v[0],
            first_v[1],
            first_v[2],
            second_v[0],
            second_v[1],
            second_v[2],
            g_ln3,
            b_ln3,
            b_down_grad,
            b_out_grad,
        ]
    )
    return (square_grads, w_up_grad, w_down_grad, vector_grads)


F32 = jnp.float32
BF16 = jnp.bfloat16
VMEM_LIMIT = 56 * 2**20
HALF = CLIP // 2


def in_vmem():
    return pl.BlockSpec(memory_space=pltpu.VMEM)


def halves(values):
    high = values.astype(BF16)
    return (high, (values - high.astype(F32)).astype(BF16))


def triple(left, right, transposed=False):
    stacked = jnp.concatenate([left[0], left[0], left[1]], axis=1)
    if transposed:
        other = jnp.concatenate([right[0], right[1], right[0]], axis=1)
        dims = (((1,), (1,)), ((), ()))
    else:
        other = jnp.concatenate([right[0], right[1], right[0]], axis=0)
        dims = (((1,), (0,)), ((), ()))
    return lax.dot_general(stacked, other, dims, preferred_element_type=F32)


def scaled_to_unit(matrix):
    return matrix * (1.0 / (jnp.sqrt(jnp.sum(matrix * matrix, keepdims=True)) + 1e-07))


def square_directions_kernel(x_ref, o_ref):
    count = x_ref.shape[0]
    for index in range(count):
        o_ref[index] = scaled_to_unit(x_ref[index])

    def step(_, carry):
        for index in range(count):
            current = o_ref[index]
            parts = halves(current)
            gram = triple(parts, parts, True)
            gram_parts = halves(gram)
            polynomial = -4.775 * gram + 2.0315 * triple(gram_parts, gram_parts)
            o_ref[index] = 3.4445 * current + triple(halves(polynomial), parts)
        return carry

    lax.fori_loop(0, 5, step, 0)


def square_directions(matrices):
    return pl.pallas_call(
        square_directions_kernel,
        out_shape=jax.ShapeDtypeStruct(matrices.shape, F32),
        in_specs=[in_vmem()],
        out_specs=in_vmem(),
        compiler_params=pltpu.CompilerParams(vmem_limit_bytes=VMEM_LIMIT),
        name="square_directions",
    )(matrices)


def wide_direction_kernel(x_ref, o_ref):
    parts = halves(scaled_to_unit(x_ref[...]))
    gram = triple(parts, parts, True)
    size = gram.shape[0]
    total = None
    for step in range(5):
        gram_parts = halves(gram)
        polynomial = -4.775 * gram + 2.0315 * triple(gram_parts, gram_parts)
        poly_parts = halves(polynomial)
        if total is None:
            row = lax.broadcasted_iota(jnp.int32, (size, size), 0)
            column = lax.broadcasted_iota(jnp.int32, (size, size), 1)
            total = polynomial + jnp.where(row == column, 3.4445, 0.0)
        else:
            total = 3.4445 * total + triple(poly_parts, halves(total))
        if step < 4:
            once = 3.4445 * gram + triple(poly_parts, gram_parts)
            gram = 3.4445 * once + triple(halves(once), poly_parts)
    o_ref[...] = triple(halves(total), parts)


def wide_direction(matrix):
    return pl.pallas_call(
        wide_direction_kernel,
        out_shape=jax.ShapeDtypeStruct(matrix.shape, F32),
        in_specs=[in_vmem()],
        out_specs=in_vmem(),
        compiler_params=pltpu.CompilerParams(vmem_limit_bytes=VMEM_LIMIT),
        name="wide_direction",
    )(matrix)


def swap_cores(values):
    return lax.ppermute(values, "dp", [(0, 1), (1, 0)])


def frames_bit(bit):
    return (lax.axis_index("frames") // bit) % 2


def swap_frames(values, bit):
    size = lax.axis_size("frames")
    return lax.ppermute(values, "frames", [(i, i ^ bit) for i in range(size)])


def sum_over_frames(values, order):
    for bit in order:
        rows = values.shape[0] // 2
        mine = frames_bit(bit)
        own = lax.dynamic_slice_in_dim(values, mine * rows, rows, 0)
        other = lax.dynamic_slice_in_dim(values, (1 - mine) * rows, rows, 0)
        values = own + swap_frames(other, bit)
    for bit in reversed(order):
        got = swap_frames(values, bit)
        values = jnp.where(
            frames_bit(bit) == 0,
            jnp.concatenate([values, got], 0),
            jnp.concatenate([got, values], 0),
        )
    return values


def sum_rows(values):
    size = lax.axis_size("frames")
    bits = []
    bit = 1
    while bit < size:
        bits.append(bit)
        bit *= 2
    unit = 8 * size
    rows = values.shape[0]
    padded = -(-rows // unit) * unit
    values = jnp.pad(values, ((0, padded - rows), (0, 0)))
    cut = (padded // unit + 1) // 2 * unit
    first = sum_over_frames(values[:cut], bits)
    second = sum_over_frames(values[cut:], [bits[1], bits[0]] + bits[2:])
    return jnp.concatenate([first, second], 0)[:rows]


def sample_groups():
    groups = []
    for block in range(lax.axis_size("frames") // CLIP):
        for half in range(2):
            groups.append(
                [
                    2 * (block * CLIP + half * HALF + place) + core
                    for core in range(2)
                    for place in range(HALF)
                ]
            )
    return groups


def swap_samples(values):
    size = lax.axis_size("frames")
    pairs = []
    for frame in range(size):
        half = (frame % CLIP) // HALF
        pairs.append((2 * frame + 1 - half, 2 * (frame ^ HALF) + half))
    return lax.ppermute(values, ("frames", "dp"), pairs)


def shards(
    latents,
    noise,
    timesteps,
    image_flags,
    frame_counts,
    text,
    conv_in,
    res_convs,
    conv_out,
    time_w1,
    time_w2,
    temb_w,
    spatial_squares,
    cross_kv,
    spatial_up,
    spatial_down,
    frozen_vectors,
    motion_squares,
    motion_up,
    motion_down,
    motion_vectors,
    square_moment,
    up_moment,
    down_moment,
    vector_moment1,
    vector_moment2,
    square_ema,
    up_ema,
    down_ema,
    vector_ema,
):
    dp_index = lax.axis_index("dp")
    place = lax.axis_index("frames")
    block = place // CLIP
    place = place % CLIP
    half = place // HALF
    stays = half == dp_index
    frame = jnp.where(stays, place, (place + HALF) % CLIP)
    pair = jnp.concatenate([latents.reshape(64, 64), noise.reshape(64, 64)], axis=1)
    pair = jnp.where(stays, pair, swap_samples(pair))
    clean_latent = pair[:, :64].reshape(1, PIX, 4).astype(jnp.float32)
    drawn_noise = pair[:, 64:].reshape(1, PIX, 4).astype(jnp.float32)

    def of_block(values):
        return lax.dynamic_index_in_dim(values[0], block, 0, keepdims=False)

    step_count = of_block(timesteps)
    facts = jnp.stack([step_count // 32, step_count % 32, of_block(image_flags)])
    facts = jnp.pad(facts.astype(jnp.bfloat16)[None, :], ((0, 0), (0, TEXT_DIM - 3)))
    text_facts = jnp.concatenate([of_block(text), facts], axis=0)
    text_facts = jnp.where(stays, text_facts, swap_cores(text_facts))
    text_rows = text_facts[None, :TEXT_LEN]
    facts = text_facts[TEXT_LEN].astype(jnp.float32)
    step_values = (facts[0] * 32.0 + facts[1])[None]
    flag = facts[2]
    phases = (step_values / 1000.0 + 0.008) / 1.008 * (math.pi / 2)
    keep_rate = jnp.cos(phases)[:, None, None]
    noise_rate = jnp.sin(phases)[:, None, None]
    noisy = keep_rate * clean_latent + noise_rate * drawn_noise
    target = keep_rate * drawn_noise - noise_rate * clean_latent
    temb_res = time_embed(step_values, time_w1, time_w2, temb_w, frozen_vectors[22])
    frozen = (
        conv_in,
        res_convs,
        spatial_squares,
        cross_kv,
        spatial_up,
        spatial_down,
        frozen_vectors,
    )
    hidden = frame_forward(noisy[0], temb_res, text_rows[0], frozen)[None]
    normed = to_low(group_norm(hidden, 1.0, 0.0))
    groups = sample_groups()

    def to_positions(values):
        return lax.all_to_all(
            jnp.swapaxes(values, 0, 1),
            ("frames", "dp"),
            split_axis=0,
            concat_axis=1,
            tiled=True,
            axis_index_groups=groups,
        )

    arrived = to_positions(normed)
    pixels_dev = arrived.shape[0]
    arrived = arrived.reshape(pixels_dev, 1, CLIP, WIDTH)
    count = lax.dynamic_slice(frame_counts, (half, block), (1, 1))[0, 0].astype(jnp.float32)
    valid_frames = (jnp.arange(CLIP, dtype=jnp.float32)[None, :] < count).astype(jnp.float32)
    masking = jnp.where(valid_frames > 0.5, 0.0, -1e30).astype(jnp.float32)
    keep_video = jnp.full((1, 1, 1, 1), 1.0 - flag)
    low_weights = (to_low(motion_squares), to_low(motion_up), to_low(motion_down))
    branch, saved = motion_forward(arrived, masking, keep_video, low_weights, motion_vectors)
    returned = lax.all_to_all(
        branch.reshape(pixels_dev, CLIP, WIDTH),
        ("frames", "dp"),
        split_axis=1,
        concat_axis=0,
        tiled=True,
        axis_index_groups=groups,
    )
    mixed_h = hidden + jnp.swapaxes(returned, 0, 1).astype(jnp.float32)

    def head_norm(values):
        return jax.nn.silu(group_norm(values, frozen_vectors[20], frozen_vectors[21]))

    activation, head_back = jax.vjp(head_norm, mixed_h)
    predicted = convolve(to_low(activation), conv_out)
    frame_valid = (frame.astype(jnp.float32) < count).astype(jnp.float32)
    total_count = 4.0 * PIX * jnp.sum(frame_counts).astype(jnp.float32)
    residual = predicted - target
    loss_part = jnp.sum(frame_valid * jnp.square(residual))
    grad_pred = to_low(2.0 * (frame_valid * residual) / total_count)
    flipped = jnp.swapaxes(conv_out[::-1, ::-1], 2, 3)
    grad_mixed = head_back(convolve(grad_pred, flipped))[0]
    grad_in = to_positions(to_low(grad_mixed))
    grad_in = grad_in.reshape(pixels_dev, 1, CLIP, WIDTH)
    grad_sq, grad_up, grad_down, grad_vec = motion_backward(
        grad_in, arrived, keep_video, low_weights, motion_vectors, saved
    )
    half_sq = square_moment.shape[0]
    half_up = up_moment.shape[1]
    half_down = down_moment.shape[0]
    vector_part = jnp.concatenate([grad_vec.reshape(-1), loss_part[None]])
    vector_part = jnp.pad(vector_part, (0, 64 * 128 - vector_part.shape[0])).reshape(64, 128)

    def half_of(core):
        return jnp.concatenate(
            [
                lax.dynamic_slice_in_dim(grad_sq, core * half_sq, half_sq, 0).reshape(-1, 128),
                lax.dynamic_slice_in_dim(grad_up, core * half_up, half_up, 1).reshape(-1, 128),
                lax.dynamic_slice_in_dim(grad_down, core * half_down, half_down, 0).reshape(-1, 128),
                vector_part,
            ],
            axis=0,
        )

    summed = sum_rows(half_of(dp_index) + swap_cores(half_of(1 - dp_index)))
    rows_sq = half_sq * WIDTH * WIDTH // 128
    rows_up = WIDTH * half_up // 128
    rows_down = WIDTH * half_down // 128
    sum_sq = summed[:rows_sq].reshape(square_moment.shape)
    sum_up = summed[rows_sq : rows_sq + rows_up].reshape(up_moment.shape)
    sum_down = summed[rows_sq + rows_up : rows_sq + rows_up + rows_down].reshape(down_moment.shape)
    vector_part = summed[rows_sq + rows_up + rows_down :].reshape(-1)
    grad_vec = vector_part[: grad_vec.size].reshape(grad_vec.shape)
    loss_sum = vector_part[grad_vec.size]
    sq_moment_new = 0.95 * square_moment + sum_sq
    up_moment_new = 0.95 * up_moment + sum_up
    down_moment_new = 0.95 * down_moment + sum_down
    own_up = sum_up + 0.95 * up_moment_new
    own_down = jnp.pad((sum_down + 0.95 * down_moment_new).T, ((0, 0), (0, half_up - half_down)))
    first_core = dp_index == 0
    kept = jnp.where(first_core, own_up, own_down)
    got = swap_cores(jnp.where(first_core, own_down, own_up))
    wide = jnp.where(
        first_core, jnp.concatenate([kept, got], 1), jnp.concatenate([got, kept], 1)
    )
    wide = wide_direction(wide)
    low_wide = to_low(wide)
    other_wide = swap_cores(low_wide)
    direct_up = jnp.where(first_core, low_wide, other_wide).astype(jnp.float32)
    direct_down = jnp.where(first_core, other_wide, low_wide)
    direct_down = (
        jnp.concatenate(
            [direct_down[:, :half_down], direct_down[:, half_up : half_up + half_down]], 1
        )
        .astype(jnp.float32)
        .T
    )
    low_sq = to_low(square_directions(sum_sq + 0.95 * sq_moment_new))
    other_sq = swap_cores(low_sq)
    direct_sq = jnp.where(
        first_core,
        jnp.concatenate([low_sq, other_sq], 0),
        jnp.concatenate([other_sq, low_sq], 0),
    ).astype(jnp.float32)
    directions = (direct_sq, direct_up, direct_down)
    shrink = 1.0 - MUON_RATE * DECAY
    square_new = motion_squares * shrink - MUON_RATE * 0.2 * math.sqrt(WIDTH) * directions[0]
    up_new = (
        motion_up * shrink - MUON_RATE * 0.2 * math.sqrt(max(WIDTH, 2 * FF_INNER)) * directions[1]
    )
    down_new = (
        motion_down * shrink - MUON_RATE * 0.2 * math.sqrt(max(FF_INNER, WIDTH)) * directions[2]
    )
    square_ema_new = AVERAGE * square_ema + (1.0 - AVERAGE) * lax.dynamic_slice_in_dim(
        square_new, dp_index * half_sq, half_sq, 0
    )
    up_ema_new = AVERAGE * up_ema + (1.0 - AVERAGE) * lax.dynamic_slice_in_dim(
        up_new, dp_index * half_up, half_up, 1
    )
    down_ema_new = AVERAGE * down_ema + (1.0 - AVERAGE) * lax.dynamic_slice_in_dim(
        down_new, dp_index * half_down, half_down, 0
    )
    moment_first = 0.9 * vector_moment1 + 0.1 * grad_vec
    moment_second = 0.999 * vector_moment2 + 0.001 * jnp.square(grad_vec)
    adjusted = (
        moment_first / (1.0 - 0.9**STEP) / (jnp.sqrt(moment_second / (1.0 - 0.999**STEP)) + 1e-08)
    )
    vector_new = motion_vectors - ADAM_RATE * (adjusted + DECAY * motion_vectors)
    return (
        loss_sum,
        total_count,
        square_new,
        sq_moment_new,
        square_ema_new,
        up_new,
        up_moment_new,
        up_ema_new,
        down_new,
        down_moment_new,
        down_ema_new,
        moment_first,
        moment_second,
        vector_new,
        AVERAGE * vector_ema + (1.0 - AVERAGE) * vector_new,
    )


def solution(mesh):
    return jax.shard_map(
        shards,
        mesh=mesh,
        in_specs=(
            P("dp", "frames", None, None),
            P("dp", "frames", None, None),
            P("dp", None),
            P("dp", None),
            P(),
            P("dp", None, None, None),
            P(),
            P(),
            P(),
            P(),
            P(),
            P(),
            P(),
            P(),
            P(),
            P(),
            P(),
            P(),
            P(),
            P(),
            P(),
            P("dp", None, None),
            P(None, "dp"),
            P("dp", None),
            P(),
            P(),
            P("dp", None, None),
            P(None, "dp"),
            P("dp", None),
            P(),
        ),
        out_specs=(
            P(),
            P(),
            P(),
            P("dp", None, None),
            P("dp", None, None),
            P(),
            P(None, "dp"),
            P(None, "dp"),
            P(),
            P("dp", None),
            P("dp", None),
            P(),
            P(),
            P(),
            P(),
        ),
        check_vma=False,
    )
```

```python
import math

import jax
import jax.numpy as jnp
import numpy as np
from jax import lax
from jax.experimental import pallas as pl
from jax.experimental.pallas import tpu as pltpu
from jax.sharding import PartitionSpec as P

WIDTH = 320
HEADS = 8
HEAD_DIM = 40
FF_INNER = 1280
CLIP = 16
HALF = 8
PIX = 1024
LATENT = 32
TEXT_LEN = 77
TEXT_DIM = 768
GN_GROUPS = 32
F32 = jnp.float32
BF16 = jnp.bfloat16
VMEM_LIMIT = 60 * 2**20
OWN = PIX // CLIP
SLOT = 64
SLOTS = HEADS * SLOT
CHUNK = 256
CHUNKS = PIX // CHUNK
GROUP = 128
SCALE = 1.0 / math.sqrt(HEAD_DIM)


def to_low(values):
    return values.astype(BF16)


def dot(left, right):
    return lax.dot_general(left, right, (((1,), (0,)), ((), ())), preferred_element_type=F32)


def dot_nt(left, right):
    return lax.dot_general(left, right, (((1,), (1,)), ((), ())), preferred_element_type=F32)


def dot_tn(left, right):
    return lax.dot_general(left, right, (((0,), (0,)), ((), ())), preferred_element_type=F32)


def in_vmem():
    return pl.BlockSpec(memory_space=pltpu.VMEM)


def in_smem():
    return pl.BlockSpec(memory_space=pltpu.SMEM)


def whole(shape):
    return pl.BlockSpec(shape, lambda *_: (0,) * len(shape))


def rows_of(width):
    return pl.BlockSpec((CHUNK, width), lambda c: (c, 0))


def slot_selector():
    out = np.zeros((WIDTH, SLOTS), np.float32)
    for head in range(HEADS):
        for j in range(HEAD_DIM):
            out[head * HEAD_DIM + j, head * SLOT + j] = 1.0
    return jnp.asarray(out, BF16)


def frame_codes():
    positions = np.arange(CLIP, dtype=np.float32)[:, None]
    column = np.arange(WIDTH)
    frequency = np.exp(np.float32(-math.log(10000.0)) * (2 * (column // 2)).astype(np.float32) / WIDTH)
    angles = positions * frequency.astype(np.float32)
    codes = np.where(column % 2 == 0, np.sin(angles), np.cos(angles)).astype(np.float32)
    return jnp.asarray(np.tile(np.repeat(codes, 8, axis=0), (CHUNK // GROUP, 1)))


def unpack_positions(packed_ref, wide_ref):
    wide_ref[:, :, 0:128] = packed_ref[:, 0:64, :].astype(F32)
    wide_ref[:, :, 128:256] = packed_ref[:, 64:128, :].astype(F32)
    last = packed_ref[:, 128:160, :].astype(F32)
    wide_ref[:, 0:32, 256:320] = last[:, :, 0:64]
    wide_ref[:, 32:64, 256:320] = last[:, :, 64:128]


def pack_positions(wide_ref, packed_ref):
    packed_ref[:, 0:64, :] = to_low(wide_ref[:, :, 0:128])
    packed_ref[:, 64:128, :] = to_low(wide_ref[:, :, 128:256])
    last = jnp.concatenate([wide_ref[:, 0:32, 256:320], wide_ref[:, 32:64, 256:320]], axis=2)
    packed_ref[:, 128:160, :] = to_low(last)


def chunk_tokens(wide_ref, step):
    parts = []
    for group in range(CHUNK // GROUP):
        start = pl.multiple_of(step * (CHUNK // CLIP) + 8 * group, 8)
        parts.append(wide_ref[:, pl.ds(start, 8), :].reshape(GROUP, WIDTH))
    return jnp.concatenate(parts, axis=0)


def put_chunk_tokens(wide_ref, step, tokens):
    for group in range(CHUNK // GROUP):
        start = pl.multiple_of(step * (CHUNK // CLIP) + 8 * group, 8)
        part = tokens[group * GROUP : (group + 1) * GROUP].reshape(CLIP, 8, WIDTH)
        wide_ref[:, pl.ds(start, 8), :] = part


def normal_parts(values):
    centre = jnp.mean(values, axis=-1, keepdims=True)
    shifted = values - centre
    scale = lax.rsqrt(jnp.mean(shifted * shifted, axis=-1, keepdims=True) + 1e-05)
    return shifted * scale, scale


def normal_back(grad, normal, scale, gain):
    inner = grad * gain
    return scale * (
        inner
        - jnp.mean(inner, axis=-1, keepdims=True)
        - normal * jnp.mean(inner * normal, axis=-1, keepdims=True)
    )


def erf_parts(gate):
    bell = jnp.exp(-0.5 * gate * gate)
    size = jnp.abs(gate) * (1.0 / math.sqrt(2.0))
    t = 1.0 / (1.0 + 0.3275911 * size)
    poly = t * (
        0.254829592
        + t * (-0.284496736 + t * (1.421413741 + t * (-1.453152027 + t * 1.061405429)))
    )
    tail = poly * bell
    return jnp.where(gate < 0.0, tail - 1.0, 1.0 - tail), bell


def gelu_parts(gate):
    erf, bell = erf_parts(gate)
    share = 0.5 + 0.5 * erf
    return gate * share, share + gate * bell * (1.0 / math.sqrt(2.0 * math.pi))


def lane_halves(values):
    lane = lax.broadcasted_iota(jnp.int32, values.shape, 1)
    zero = jnp.zeros_like(values)
    return jnp.concatenate(
        [jnp.where(lane < SLOT, values, zero), jnp.where(lane < SLOT, zero, values)], axis=0
    )


def key_bias(count, queries_first):
    shape = (GROUP, 2 * GROUP) if queries_first else (2 * GROUP, GROUP)
    row = lax.broadcasted_iota(jnp.int32, shape, 0)
    column = lax.broadcasted_iota(jnp.int32, shape, 1)
    key = (column if queries_first else row) % GROUP
    valid = (row % 8 == column % 8) & (key // 8 < count)
    return jnp.where(valid, 0.0, -1e30).astype(F32)


def attend_chunk(qkv, bias):
    out = []
    for group in range(CHUNK // GROUP):
        rows = slice(group * GROUP, (group + 1) * GROUP)
        pairs = []
        for pair in range(HEADS // 2):
            lanes = pair * 2 * SLOT
            queries = qkv[rows, lanes : lanes + GROUP]
            keys = lane_halves(qkv[rows, SLOTS + lanes : SLOTS + lanes + GROUP])
            values = lane_halves(qkv[rows, 2 * SLOTS + lanes : 2 * SLOTS + lanes + GROUP])
            scores = dot_nt(queries, keys) * SCALE + bias
            probs = []
            for part in (scores[:, :GROUP], scores[:, GROUP:]):
                raised = jnp.exp(part - jnp.max(part, axis=1, keepdims=True))
                probs.append(raised * (1.0 / jnp.sum(raised, axis=1, keepdims=True)))
            pairs.append(to_low(dot(to_low(jnp.concatenate(probs, axis=1)), values)))
        out.append(jnp.concatenate(pairs, axis=1))
    return jnp.concatenate(out, axis=0)


def motion_forward_kernel(
    count_ref, keep_ref, arrived_ref, codes_ref, vec_ref, w_in_ref, w_qkv_ref, w_o_ref, w_up_ref, w_down_ref, w_out_ref,
    branch_ref, u_ref, u2_ref, u3_ref, qkv1_ref, qkv2_ref, o1_ref, o2_ref, last_ref,
    wide, back,
):
    step = pl.program_id(0)

    @pl.when(step == 0)
    def _():
        unpack_positions(arrived_ref, wide)

    def vec(i):
        return vec_ref[i : i + 1, :]

    bias = key_bias(count_ref[0], True)
    normed = chunk_tokens(wide, step)
    inputs = to_low(normed * vec(0) + vec(1))
    stream = dot(inputs, w_in_ref[...]) + vec(2)
    for index, (first, x_ref, qkv_ref, o_ref) in enumerate(((3, u_ref, qkv1_ref, o1_ref), (6, u2_ref, qkv2_ref, o2_ref))):
        x_ref[...] = stream
        normal = normal_parts(stream)[0]
        a = to_low(normal * vec(first) + vec(first + 1) + codes_ref[...])
        qkv = to_low(dot(a, w_qkv_ref[index]))
        qkv_ref[...] = qkv
        mixture = attend_chunk(qkv, bias)
        o_ref[...] = mixture
        stream = stream + (dot(mixture, w_o_ref[index]) + vec(first + 2))
    u3_ref[...] = stream
    c = to_low(normal_parts(stream)[0] * vec(9) + vec(10))
    gate_up = dot(c, w_up_ref[...])
    inner = to_low(gate_up[:, :FF_INNER] * gelu_parts(gate_up[:, FF_INNER:])[0])
    last = to_low(stream + (dot(inner, w_down_ref[...]) + vec(11)))
    last_ref[...] = last
    put_chunk_tokens(back, step, (dot(last, w_out_ref[...]) + vec(12)) * keep_ref[0])

    @pl.when(step == CHUNKS - 1)
    def _():
        pack_positions(back, branch_ref)


def motion_forward(arrived, count, keep, weights, vectors):
    outs = [
        ((CLIP, 160, 128), BF16, None),
        ((PIX, WIDTH), F32, WIDTH), ((PIX, WIDTH), F32, WIDTH), ((PIX, WIDTH), F32, WIDTH),
        ((PIX, 3 * SLOTS), BF16, 3 * SLOTS), ((PIX, 3 * SLOTS), BF16, 3 * SLOTS),
        ((PIX, SLOTS), BF16, SLOTS), ((PIX, SLOTS), BF16, SLOTS),
        ((PIX, WIDTH), BF16, WIDTH),
    ]
    operands = (arrived, frame_codes(), vectors, weights["in"], weights["qkv"], weights["o"], weights["up"], weights["down"], weights["out"])
    return pl.pallas_call(
        motion_forward_kernel,
        grid=(CHUNKS,),
        in_specs=[in_smem(), in_smem()] + [whole(x.shape) for x in operands],
        out_specs=[whole(s) if w is None else rows_of(w) for s, _, w in outs],
        out_shape=[jax.ShapeDtypeStruct(s, d) for s, d, _ in outs],
        scratch_shapes=[pltpu.VMEM((CLIP, OWN, WIDTH), F32), pltpu.VMEM((CLIP, OWN, WIDTH), F32)],
        compiler_params=pltpu.CompilerParams(vmem_limit_bytes=VMEM_LIMIT),
        name="motion_forward",
    )(count, keep, *operands)


def prepare_kernel(sq_ref, up_ref, down_ref, sel_ref, w_in, w_qkv, w_o, w_up, w_down, w_out, t_in, t_qkv, t_o, t_up, t_down, t_out):
    sel = sel_ref[...]
    low = [to_low(sq_ref[i]) for i in range(10)]
    w_in[...] = low[0]
    t_in[...] = low[0].T
    w_out[...] = low[9]
    t_out[...] = low[9].T
    for index, first in enumerate((1, 5)):
        for j in range(3):
            padded = to_low(dot(low[first + j], sel))
            w_qkv[index, :, j * SLOTS : (j + 1) * SLOTS] = padded
            t_qkv[index, j * SLOTS : (j + 1) * SLOTS, :] = padded.T
        padded = to_low(dot_nt(low[first + 3].T, sel.T))
        t_o[index] = padded
        w_o[index] = padded.T
    up = to_low(up_ref[...])
    w_up[...] = up
    t_up[...] = up.T
    down = to_low(down_ref[...])
    w_down[...] = down
    t_down[...] = down.T


def prepare(squares, up, down):
    shapes = {
        "in": (WIDTH, WIDTH), "qkv": (2, WIDTH, 3 * SLOTS), "o": (2, SLOTS, WIDTH), "up": (WIDTH, 2 * FF_INNER),
        "down": (FF_INNER, WIDTH), "out": (WIDTH, WIDTH),
        "in_t": (WIDTH, WIDTH), "qkv_t": (2, 3 * SLOTS, WIDTH), "o_t": (2, WIDTH, SLOTS), "up_t": (2 * FF_INNER, WIDTH),
        "down_t": (WIDTH, FF_INNER), "out_t": (WIDTH, WIDTH),
    }
    made = pl.pallas_call(
        prepare_kernel,
        in_specs=[in_vmem()] * 4,
        out_specs=[in_vmem()] * len(shapes),
        out_shape=[jax.ShapeDtypeStruct(s, BF16) for s in shapes.values()],
        compiler_params=pltpu.CompilerParams(vmem_limit_bytes=VMEM_LIMIT),
        name="motion_weights",
    )(squares, up, down, slot_selector())
    return dict(zip(shapes, made))


def add_to(ref, step, value):
    @pl.when(step == 0)
    def _():
        ref[...] = value

    @pl.when(step > 0)
    def _():
        ref[...] += value


def column_sum(values):
    return jnp.sum(values, axis=0, keepdims=True)


def feed_backward_kernel(
    keep_ref, grad_ref, u3_ref, last_ref, vec_ref, w_up_ref, t_up_ref, t_down_ref, t_out_ref,
    du3_ref, g_wide_ref, g_out_ref, g_vec_ref,
    wide,
):
    step = pl.program_id(0)

    @pl.when(step == 0)
    def _():
        unpack_positions(grad_ref, wide)
        g_wide_ref[...] = jnp.zeros_like(g_wide_ref)

    gain = vec_ref[9:10, :]
    dbranch = to_low(chunk_tokens(wide, step) * keep_ref[0])
    add_to(g_out_ref, step, dot_tn(last_ref[...], dbranch))
    du4 = dot(dbranch, t_out_ref[...])
    d4 = to_low(du4)
    normal, scale = normal_parts(u3_ref[...])
    c = to_low(normal * gain + vec_ref[10:11, :])
    z = dot(c, w_up_ref[...])
    value = z[:, :FF_INNER]
    gelu, slope = gelu_parts(z[:, FF_INNER:])
    inner = to_low(value * gelu)
    dinner = dot(d4, t_down_ref[...])
    dz = to_low(jnp.concatenate([dinner * gelu, dinner * value * slope], axis=1))
    g_down = dot_tn(d4, inner)
    g_up = dot_tn(c, dz)
    for half in range(2):
        for tile in range(10):
            start = half * FF_INNER + tile * 128
            g_wide_ref[half, tile_rows(tile)] += g_up[:, start : start + 128]
        for tile in range(5):
            start = half * (FF_INNER // 2) + tile * 128
            g_wide_ref[half, tile_rows(10 + tile)] += g_down[:, start : start + 128]
    dc = dot(dz, t_up_ref[...])
    du3_ref[...] = du4 + normal_back(dc, normal, scale, gain)
    rows = [column_sum(dc * normal), column_sum(dc), column_sum(d4.astype(F32)), column_sum(dbranch.astype(F32))]
    add_to(g_vec_ref, step, jnp.concatenate(rows + [jnp.zeros((4, WIDTH), F32)], axis=0))


def feed_backward(grad, keep, weights, vectors, u3, last):
    operands = (grad, u3, last, vectors, weights["up"], weights["up_t"], weights["down_t"], weights["out_t"])
    specs = [whole(x.shape) for x in operands]
    specs[1] = rows_of(WIDTH)
    specs[2] = rows_of(WIDTH)
    outs = [(PIX, WIDTH), (2, EARLY_ROWS, 128), (WIDTH, WIDTH), (8, WIDTH)]
    return pl.pallas_call(
        feed_backward_kernel,
        grid=(CHUNKS,),
        in_specs=[in_smem()] + specs,
        out_specs=[rows_of(WIDTH)] + [whole(s) for s in outs[1:]],
        out_shape=[jax.ShapeDtypeStruct(s, F32) for s in outs],
        scratch_shapes=[pltpu.VMEM((CLIP, OWN, WIDTH), F32)],
        compiler_params=pltpu.CompilerParams(vmem_limit_bytes=VMEM_LIMIT),
        name="feed_backward",
    )(keep, *operands)


def attend_back_chunk(qkv, d_mixture, bias):
    out = []
    for group in range(CHUNK // GROUP):
        rows = slice(group * GROUP, (group + 1) * GROUP)
        grads = [[], [], []]
        for pair in range(HEADS // 2):
            lanes = pair * 2 * SLOT
            queries = qkv[rows, lanes : lanes + GROUP]
            keys = lane_halves(qkv[rows, SLOTS + lanes : SLOTS + lanes + GROUP])
            values = lane_halves(qkv[rows, 2 * SLOTS + lanes : 2 * SLOTS + lanes + GROUP])
            d_out = d_mixture[rows, lanes : lanes + GROUP]
            scores = dot_nt(keys, queries) * SCALE + bias
            d_probs = dot_nt(values, d_out)
            low_probs = []
            d_scores = []
            for head in range(2):
                part = scores[head * GROUP : (head + 1) * GROUP]
                d_part = d_probs[head * GROUP : (head + 1) * GROUP]
                raised = jnp.exp(part - jnp.max(part, axis=0, keepdims=True))
                probs = raised * (1.0 / jnp.sum(raised, axis=0, keepdims=True))
                low_probs.append(to_low(probs))
                d_scores.append(to_low(probs * (d_part - jnp.sum(probs * d_part, axis=0, keepdims=True))))
            low_probs = jnp.concatenate(low_probs, axis=0)
            d_scores = jnp.concatenate(d_scores, axis=0)
            d_values = dot(low_probs, d_out)
            d_keys = dot(d_scores, queries) * SCALE
            d_queries = dot_tn(d_scores, keys) * SCALE
            lane = lax.broadcasted_iota(jnp.int32, (GROUP, GROUP), 1)
            grads[0].append(to_low(d_queries))
            grads[1].append(to_low(jnp.where(lane < SLOT, d_keys[:GROUP], d_keys[GROUP:])))
            grads[2].append(to_low(jnp.where(lane < SLOT, d_values[:GROUP], d_values[GROUP:])))
        out.append(jnp.concatenate(grads[0] + grads[1] + grads[2], axis=1))
    return jnp.concatenate(out, axis=0)


def attention_backward_step(step, count, grad, stream, qkv, mixture, codes, gain, offset, t_o, t_qkv, sel_t, g_refs):
    bias = key_bias(count, False)
    d_out = to_low(grad)
    padded = dot_tn(mixture, d_out)
    w_o_grad = jnp.concatenate([padded[head * SLOT : head * SLOT + HEAD_DIM] for head in range(HEADS)], axis=0)
    add_to(g_refs[3], step, w_o_grad)
    d_mixture = to_low(dot(d_out, t_o))
    d_qkv = attend_back_chunk(qkv, d_mixture, bias)
    normal, scale = normal_parts(stream)
    a = to_low(normal * gain + offset + codes)
    for j in range(3):
        tight = to_low(dot(d_qkv[:, j * SLOTS : (j + 1) * SLOTS], sel_t))
        add_to(g_refs[j], step, dot_tn(a, tight))
    d_a = dot(d_qkv, t_qkv)
    rows = [column_sum(d_a * normal), column_sum(d_a), column_sum(d_out.astype(F32))]
    return grad + normal_back(d_a, normal, scale, gain), rows


def second_backward_kernel(
    count_ref, grad_ref, u2_ref, qkv_ref, o_ref, codes_ref, vec_ref, t_o_ref, t_qkv_ref, sel_t_ref,
    du2_ref, gq_ref, gk_ref, gv_ref, go_ref, g_vec_ref,
):
    step = pl.program_id(0)
    du2, rows = attention_backward_step(
        step, count_ref[0], grad_ref[...], u2_ref[...], qkv_ref[...], o_ref[...], codes_ref[...],
        vec_ref[6:7, :], vec_ref[7:8, :], t_o_ref[...], t_qkv_ref[...], sel_t_ref[...], (gq_ref, gk_ref, gv_ref, go_ref),
    )
    du2_ref[...] = du2
    add_to(g_vec_ref, step, jnp.concatenate(rows + [jnp.zeros((5, WIDTH), F32)], axis=0))


def second_backward(grad, count, weights, vectors, u2, qkv, mixture):
    operands = (grad, u2, qkv, mixture, frame_codes(), vectors, weights["o_t"][1], weights["qkv_t"][1], slot_selector().T)
    specs = [rows_of(WIDTH), rows_of(WIDTH), rows_of(3 * SLOTS), rows_of(SLOTS)] + [whole(x.shape) for x in operands[4:]]
    outs = [(PIX, WIDTH)] + [(WIDTH, WIDTH)] * 4 + [(8, WIDTH)]
    return pl.pallas_call(
        second_backward_kernel,
        grid=(CHUNKS,),
        in_specs=[in_smem()] + specs,
        out_specs=[rows_of(WIDTH)] + [whole(s) for s in outs[1:]],
        out_shape=[jax.ShapeDtypeStruct(s, F32) for s in outs],
        compiler_params=pltpu.CompilerParams(vmem_limit_bytes=VMEM_LIMIT),
        name="second_backward",
    )(count, *operands)


def first_backward_kernel(
    count_ref, loss_ref, grad_ref, u_ref, qkv_ref, o_ref, arrived_ref, codes_ref, vec_ref, t_o_ref, t_qkv_ref, sel_t_ref, t_in_ref,
    g5_ref, g6_ref, g7_ref, g8_ref, g9_ref, feed_vec_ref, second_vec_ref,
    packed_ref,
    wide, g0, g1, g2, g3, g4, sums,
):
    step = pl.program_id(0)

    @pl.when(step == 0)
    def _():
        unpack_positions(arrived_ref, wide)

    du, rows = attention_backward_step(
        step, count_ref[0], grad_ref[...], u_ref[...], qkv_ref[...], o_ref[...], codes_ref[...],
        vec_ref[3:4, :], vec_ref[4:5, :], t_o_ref[...], t_qkv_ref[...], sel_t_ref[...], (g1, g2, g3, g4),
    )
    du = to_low(du)
    normed = chunk_tokens(wide, step)
    inputs = to_low(normed * vec_ref[0:1, :] + vec_ref[1:2, :])
    add_to(g0, step, dot_tn(inputs, du))
    d_inputs = dot(du, t_in_ref[...])
    top = [column_sum(d_inputs * normed), column_sum(d_inputs), column_sum(du.astype(F32))]
    add_to(sums, step, jnp.concatenate(top + rows + [jnp.zeros((2, WIDTH), F32)], axis=0))

    @pl.when(step == CHUNKS - 1)
    def _():
        squares = (g0, g1, g2, g3, g4, g5_ref, g6_ref, g7_ref, g8_ref, g9_ref)
        vector_rows = jnp.concatenate(
            [sums[0:6, :], second_vec_ref[0:3, :], feed_vec_ref[0:4, :], jnp.full((3, WIDTH), loss_ref[0])], axis=0
        )
        pieces = [vector_rows[:, 64 * j : 64 * (j + 1)] for j in range(5)]
        side = jnp.concatenate(pieces + [jnp.zeros((WIDTH - 80, 64), F32)], axis=0)
        for half in range(2):
            own = squares[5 * half : 5 * half + 5]
            for index in range(5):
                packed_ref[half, tile_rows(2 * index)] = own[index][:, 0:128]
                packed_ref[half, tile_rows(2 * index + 1)] = own[index][:, 128:256]
            for pair in range(2):
                packed_ref[half, tile_rows(10 + pair)] = jnp.concatenate(
                    [own[2 * pair][:, 256:320], own[2 * pair + 1][:, 256:320]], axis=1
                )
            packed_ref[half, 13 * WIDTH :] = jnp.zeros((LATE_ROWS - 13 * WIDTH, 128), F32)
            packed_ref[half, tile_rows(12)] = jnp.concatenate([own[4][:, 256:320], side], axis=1)


def first_backward(grad, count, loss_part, arrived, weights, vectors, u, qkv, mixture, later):
    operands = (
        grad, u, qkv, mixture, arrived, frame_codes(), vectors, weights["o_t"][0], weights["qkv_t"][0], slot_selector().T, weights["in_t"],
    ) + tuple(later)
    specs = [rows_of(WIDTH), rows_of(WIDTH), rows_of(3 * SLOTS), rows_of(SLOTS)] + [whole(x.shape) for x in operands[4:]]
    return pl.pallas_call(
        first_backward_kernel,
        grid=(CHUNKS,),
        in_specs=[in_smem(), in_smem()] + specs,
        out_specs=whole((2, LATE_ROWS, 128)),
        out_shape=jax.ShapeDtypeStruct((2, LATE_ROWS, 128), F32),
        scratch_shapes=[pltpu.VMEM((CLIP, OWN, WIDTH), F32)] + [pltpu.VMEM((WIDTH, WIDTH), F32)] * 5 + [pltpu.VMEM((8, WIDTH), F32)],
        compiler_params=pltpu.CompilerParams(vmem_limit_bytes=VMEM_LIMIT),
        name="first_backward",
    )(count, loss_part, *operands)


MUON_RATE = 0.2
ADAM_RATE = 0.4
DECAY = 0.01
AVERAGE = 0.75
STEP = 10
SHRINK = 1.0 - MUON_RATE * DECAY
SQUARE_RATE = MUON_RATE * 0.2 * math.sqrt(WIDTH)
UP_RATE = MUON_RATE * 0.2 * math.sqrt(2 * FF_INNER)
DOWN_RATE = MUON_RATE * 0.2 * math.sqrt(FF_INNER)
UP_TILES = 10
DOWN_TILES = 5
WIDE_TILES = 2 * UP_TILES
EARLY_ROWS = 4864
LATE_ROWS = 4224


def tile_rows(index):
    return slice(index * WIDTH, (index + 1) * WIDTH)


def halves(values):
    high = values.astype(BF16)
    return (high, (values - high.astype(F32)).astype(BF16))


def triple(left, right, transposed=False):
    stacked = jnp.concatenate([left[0], left[0], left[1]], axis=1)
    if transposed:
        return dot_nt(stacked, jnp.concatenate([right[0], right[1], right[0]], axis=1))
    return dot(stacked, jnp.concatenate([right[0], right[1], right[0]], axis=0))


def scaled_to_unit(matrix):
    return matrix * (1.0 / (jnp.sqrt(jnp.sum(matrix * matrix, keepdims=True)) + 1e-07))


def wide_moments_kernel(sum_ref, up_ref, down_ref, up_new_ref, down_new_ref, ahead_ref):
    for tile in range(UP_TILES):
        lanes = slice(128 * tile, 128 * (tile + 1))
        gradient = sum_ref[tile_rows(tile)]
        moment = 0.95 * up_ref[:, lanes] + gradient
        up_new_ref[:, lanes] = moment
        ahead_ref[tile] = gradient + 0.95 * moment
    for tile in range(DOWN_TILES):
        rows = slice(128 * tile, 128 * (tile + 1))
        gradient = sum_ref[tile_rows(UP_TILES + tile)]
        moment = 0.95 * down_ref[rows, :] + gradient.T
        down_new_ref[rows, :] = moment
        ahead_ref[UP_TILES + tile] = gradient + 0.95 * moment.T


def wide_moments(summed, up_moment, down_moment):
    return pl.pallas_call(
        wide_moments_kernel,
        in_specs=[in_vmem()] * 3,
        out_specs=[in_vmem()] * 3,
        out_shape=[
            jax.ShapeDtypeStruct(up_moment.shape, F32),
            jax.ShapeDtypeStruct(down_moment.shape, F32),
            jax.ShapeDtypeStruct((UP_TILES + DOWN_TILES, WIDTH, 128), F32),
        ],
        compiler_params=pltpu.CompilerParams(vmem_limit_bytes=VMEM_LIMIT),
        name="wide_moments",
    )(summed, up_moment, down_moment)


def wide_direction_kernel(core_ref, own_ref, got_ref, o_ref, matrix):
    def put(tile, value):
        matrix[:, 128 * tile : 128 * (tile + 1)] = value

    @pl.when(core_ref[0] == 0)
    def _():
        for tile in range(UP_TILES):
            put(tile, own_ref[tile])
            put(UP_TILES + tile, got_ref[tile])

    @pl.when(core_ref[0] != 0)
    def _():
        for tile in range(DOWN_TILES):
            put(tile, got_ref[UP_TILES - DOWN_TILES + tile])
            put(DOWN_TILES + tile, own_ref[UP_TILES + tile])
        matrix[:, 128 * UP_TILES :] = jnp.zeros((WIDTH, 128 * UP_TILES), F32)

    parts = halves(scaled_to_unit(matrix[...]))
    gram = triple(parts, parts, True)
    row = lax.broadcasted_iota(jnp.int32, (WIDTH, WIDTH), 0)
    column = lax.broadcasted_iota(jnp.int32, (WIDTH, WIDTH), 1)
    total = None
    for step in range(5):
        gram_parts = halves(gram)
        polynomial = -4.775 * gram + 2.0315 * triple(gram_parts, gram_parts)
        poly_parts = halves(polynomial)
        if total is None:
            total = polynomial + jnp.where(row == column, 3.4445, 0.0)
        else:
            total = 3.4445 * total + triple(poly_parts, halves(total))
        if step < 4:
            once = 3.4445 * gram + triple(poly_parts, gram_parts)
            gram = 3.4445 * once + triple(halves(once), poly_parts)
    direction = to_low(triple(halves(total), parts))
    for tile in range(WIDE_TILES):
        o_ref[tile] = direction[:, 128 * tile : 128 * (tile + 1)]


def wide_direction(core, own, got):
    return pl.pallas_call(
        wide_direction_kernel,
        in_specs=[in_smem(), in_vmem(), in_vmem()],
        out_specs=in_vmem(),
        out_shape=jax.ShapeDtypeStruct((WIDE_TILES, WIDTH, 128), BF16),
        scratch_shapes=[pltpu.VMEM((WIDTH, 128 * WIDE_TILES), F32)],
        compiler_params=pltpu.CompilerParams(vmem_limit_bytes=VMEM_LIMIT),
        name="wide_direction",
    )(core, own, got)


def wide_update_kernel(
    core_ref, own_ref, got_ref, up_ref, down_ref, up_ema_ref, down_ema_ref,
    up_new_ref, up_ema_new_ref, down_new_ref, down_ema_new_ref,
):
    def update(up_dir, down_dir):
        for tile in range(WIDE_TILES):
            lanes = slice(128 * tile, 128 * (tile + 1))
            up_new_ref[:, lanes] = up_ref[:, lanes] * SHRINK - UP_RATE * up_dir[tile].astype(F32)
        for tile in range(2 * DOWN_TILES):
            rows = slice(128 * tile, 128 * (tile + 1))
            down_new_ref[rows, :] = down_ref[rows, :] * SHRINK - DOWN_RATE * down_dir[tile].astype(F32).T

    def average(half):
        lanes = slice(128 * UP_TILES * half, 128 * UP_TILES * (half + 1))
        up_ema_new_ref[...] = AVERAGE * up_ema_ref[...] + (1.0 - AVERAGE) * up_new_ref[:, lanes]
        rows = slice(128 * DOWN_TILES * half, 128 * DOWN_TILES * (half + 1))
        down_ema_new_ref[...] = AVERAGE * down_ema_ref[...] + (1.0 - AVERAGE) * down_new_ref[rows, :]

    @pl.when(core_ref[0] == 0)
    def _():
        update(own_ref, got_ref)
        average(0)

    @pl.when(core_ref[0] != 0)
    def _():
        update(got_ref, own_ref)
        average(1)


def wide_update(core, own, got, up, down, up_ema, down_ema):
    return pl.pallas_call(
        wide_update_kernel,
        in_specs=[in_smem()] + [in_vmem()] * 6,
        out_specs=[in_vmem()] * 4,
        out_shape=[jax.ShapeDtypeStruct(x.shape, F32) for x in (up, up_ema, down, down_ema)],
        compiler_params=pltpu.CompilerParams(vmem_limit_bytes=VMEM_LIMIT),
        name="wide_update",
    )(core, own, got, up, down, up_ema, down_ema)


def square_directions_kernel(
    sum_ref, moment_ref, m1_ref, m2_ref, vec_ref, vec_ema_ref,
    direction_ref, moment_new_ref, m1_new_ref, m2_new_ref, vec_new_ref, vec_ema_new_ref, loss_ref,
    matrix,
):
    side = sum_ref[tile_rows(12)][:, 64:128]
    rows = jnp.concatenate([side[16 * j : 16 * (j + 1)] for j in range(5)], axis=1)
    loss_ref[...] = rows[13:14, 0:128]
    gradient = rows[0:13]
    first = 0.9 * m1_ref[...] + 0.1 * gradient
    second = 0.999 * m2_ref[...] + 0.001 * (gradient * gradient)
    m1_new_ref[...] = first
    m2_new_ref[...] = second
    adjusted = first * (1.0 / (1.0 - 0.9**STEP)) / (jnp.sqrt(second * (1.0 / (1.0 - 0.999**STEP))) + 1e-08)
    fresh = vec_ref[...] - ADAM_RATE * (adjusted + DECAY * vec_ref[...])
    vec_new_ref[...] = fresh
    vec_ema_new_ref[...] = AVERAGE * vec_ema_ref[...] + (1.0 - AVERAGE) * fresh
    for index in range(5):
        lanes = slice(64 * (index % 2), 64 * (index % 2) + 64)
        gradient = jnp.concatenate(
            [sum_ref[tile_rows(2 * index)], sum_ref[tile_rows(2 * index + 1)], sum_ref[tile_rows(10 + index // 2)][:, lanes]],
            axis=1,
        )
        moment = 0.95 * moment_ref[index] + gradient
        moment_new_ref[index] = moment
        matrix[index] = scaled_to_unit(gradient + 0.95 * moment)

    def step(_, carry):
        for index in range(5):
            current = matrix[index]
            parts = halves(current)
            gram = triple(parts, parts, True)
            gram_parts = halves(gram)
            polynomial = -4.775 * gram + 2.0315 * triple(gram_parts, gram_parts)
            matrix[index] = 3.4445 * current + triple(halves(polynomial), parts)
        return carry

    lax.fori_loop(0, 5, step, 0)
    direction_ref[...] = to_low(matrix[...])


def square_directions(summed, moment, m1, m2, vectors, vec_ema):
    shapes = [(moment.shape, BF16), (moment.shape, F32)] + [(vectors.shape, F32)] * 4 + [((1, 128), F32)]
    return pl.pallas_call(
        square_directions_kernel,
        in_specs=[in_vmem()] * 6,
        out_specs=[in_vmem()] * 7,
        out_shape=[jax.ShapeDtypeStruct(s, d) for s, d in shapes],
        scratch_shapes=[pltpu.VMEM(moment.shape, F32)],
        compiler_params=pltpu.CompilerParams(vmem_limit_bytes=VMEM_LIMIT),
        name="square_directions",
    )(summed, moment, m1, m2, vectors, vec_ema)


def square_update_kernel(core_ref, own_ref, got_ref, weight_ref, ema_ref, new_ref, ema_new_ref):
    def update(half, direction):
        for index in range(5):
            new_ref[5 * half + index] = weight_ref[5 * half + index] * SHRINK - SQUARE_RATE * direction[index].astype(F32)

    def average(half):
        for index in range(5):
            ema_new_ref[index] = AVERAGE * ema_ref[index] + (1.0 - AVERAGE) * new_ref[5 * half + index]

    for core in range(2):

        @pl.when(core_ref[0] == core)
        def _(core=core):
            update(core, own_ref)
            update(1 - core, got_ref)
            average(core)


def square_update(core, own, got, weights, ema):
    return pl.pallas_call(
        square_update_kernel,
        in_specs=[in_smem()] + [in_vmem()] * 4,
        out_specs=[in_vmem()] * 2,
        out_shape=[jax.ShapeDtypeStruct(x.shape, F32) for x in (weights, ema)],
        compiler_params=pltpu.CompilerParams(vmem_limit_bytes=VMEM_LIMIT),
        name="square_update",
    )(core, own, got, weights, ema)


TAPS = 9
CHAN = 4


def group_ones():
    group = np.arange(WIDTH) // (WIDTH // GN_GROUPS)
    return jnp.asarray((group[:, None] == group[None, :]).astype(np.float32), BF16)


def group_mean(column_sums, ones):
    rest = jnp.broadcast_to(column_sums, (8, WIDTH))
    total = jnp.zeros((8, WIDTH), F32)
    for _ in range(3):
        part = to_low(rest)
        total = total + dot(part, ones)
        rest = rest - part.astype(F32)
    return total[0:1] * (1.0 / (PIX * (WIDTH // GN_GROUPS)))


def chunk_rows(index):
    return pl.ds(pl.multiple_of(index * CHUNK, CHUNK), CHUNK)


def over_chunks(body, *start):
    return lax.fori_loop(0, CHUNKS, lambda i, carry: body(i, *carry), start)


def zero_row():
    return jnp.zeros((1, WIDTH), F32)


def group_stats(ref, ones, column_sums):
    centre = group_mean(column_sums, ones)

    def squares(i, total):
        shifted = ref[chunk_rows(i), :] - centre
        return (total + column_sum(shifted * shifted),)

    (total,) = over_chunks(squares, zero_row())
    return centre, lax.rsqrt(group_mean(total, ones) + 1e-05)


def sigmoid(values):
    return 1.0 / (1.0 + jnp.exp(-values))


def shifted_lanes(values, down, right):
    lane = lax.broadcasted_iota(jnp.int32, values.shape, 1)
    line = lane // LATENT + down
    place = lane % LATENT + right
    inside = (line >= 0) & (line < LATENT) & (place >= 0) & (place < LATENT)
    offset = (down * LATENT + right) % PIX
    moved = pltpu.roll(values, (PIX - offset) % PIX, 1) if offset else values
    return jnp.where(inside, moved, 0.0)


def put_columns(cols_ref, act_ref):
    zeros = jnp.zeros((LATENT, 3 * WIDTH), BF16)
    cols_ref[0:LATENT, :] = zeros
    cols_ref[LATENT + PIX :, :] = zeros
    act_ref[0:8, :] = jnp.zeros((8, WIDTH), F32)
    act_ref[8 + PIX :, :] = jnp.zeros((8, WIDTH), F32)

    for i in range(CHUNKS):
        place = (lax.broadcasted_iota(jnp.int32, (CHUNK, WIDTH), 0)) % LATENT
        middle = act_ref[8 + i * CHUNK : 8 + (i + 1) * CHUNK, :]
        left = act_ref[7 + i * CHUNK : 7 + (i + 1) * CHUNK, :]
        right = act_ref[9 + i * CHUNK : 9 + (i + 1) * CHUNK, :]
        left = jnp.where(place == 0, 0.0, left)
        right = jnp.where(place == LATENT - 1, 0.0, right)
        cols_ref[LATENT + i * CHUNK : LATENT + (i + 1) * CHUNK, :] = jnp.concatenate(
            [to_low(left), to_low(middle), to_low(right)], axis=1
        )


def resnet_kernel(
    noisy_ref, vec_ref, temb_ref, ones_ref, w_in_ref, w_res_ref, w_s0_ref,
    resnet_ref, tokens_ref,
    first, inner, act, cols,
):
    ones = ones_ref[...]

    def vec(i):
        return vec_ref[i : i + 1, :]

    noisy = noisy_ref[...]
    taps = [shifted_lanes(noisy, tap // 3 - 1, tap % 3 - 1) for tap in range(TAPS)]
    columns = to_low(jnp.concatenate(taps, axis=0))
    w_in = w_in_ref[...]
    total = zero_row()
    for i in range(CHUNKS):
        part = dot_tn(columns[:, i * CHUNK : (i + 1) * CHUNK], w_in) + vec(0)
        first[i * CHUNK : (i + 1) * CHUNK, :] = part
        total = total + column_sum(part)

    def activate(source, total, gain, offset):
        centre, scale = group_stats(source, ones, total)

        def one(i):
            normal = (source[chunk_rows(i), :] - centre) * scale * gain + offset
            act[pl.ds(pl.multiple_of(8 + i * CHUNK, 8), CHUNK), :] = normal * sigmoid(normal)
            return ()

        over_chunks(lambda i: one(i))
        put_columns(cols, act)

    def convolve_chunk(i, which):
        out = None
        for line in range(3):
            part = cols[pl.ds(pl.multiple_of(i * CHUNK + LATENT * line, LATENT), CHUNK), :]
            term = dot(part, w_res_ref[which, line])
            out = term if out is None else out + term
        return out

    activate(first, total, vec(1), vec(2))
    shift = vec(3) + temb_ref[...]

    def first_step(i, total):
        part = convolve_chunk(i, 0) + shift
        inner[chunk_rows(i), :] = part
        return (total + column_sum(part),)

    (total,) = over_chunks(first_step, zero_row())
    activate(inner, total, vec(4), vec(5))

    def second_step(i, total):
        part = first[chunk_rows(i), :] + (convolve_chunk(i, 1) + vec(6))
        resnet_ref[chunk_rows(i), :] = part
        return (total + column_sum(part),)

    (total,) = over_chunks(second_step, zero_row())
    centre, scale = group_stats(resnet_ref, ones, total)

    def token_step(i):
        normal = to_low((resnet_ref[chunk_rows(i), :] - centre) * scale * vec(7) + vec(8))
        tokens_ref[chunk_rows(i), :] = dot(normal, w_s0_ref[...]) + vec(9)
        return ()

    over_chunks(lambda i: token_step(i))


def resnet_block(noisy, vectors, temb, w_in, w_res, w_s0):
    return pl.pallas_call(
        resnet_kernel,
        in_specs=[in_vmem()] * 7,
        out_specs=[in_vmem()] * 2,
        out_shape=[jax.ShapeDtypeStruct((PIX, WIDTH), F32)] * 2,
        scratch_shapes=[
            pltpu.VMEM((PIX, WIDTH), F32),
            pltpu.VMEM((PIX, WIDTH), F32),
            pltpu.VMEM((PIX + 16, WIDTH), F32),
            pltpu.VMEM((PIX + 2 * LATENT, 3 * WIDTH), BF16),
        ],
        compiler_params=pltpu.CompilerParams(vmem_limit_bytes=VMEM_LIMIT),
        name="resnet_block",
    )(noisy, vectors, temb, group_ones(), w_in, w_res, w_s0)


def prepare_spatial_kernel(sq_ref, sel_ref, w_qkv, w_o, w_q2, w_o2):
    sel = sel_ref[...]
    for j in range(3):
        w_qkv[:, j * SLOTS : (j + 1) * SLOTS] = to_low(dot(sq_ref[1 + j], sel))
    w_q2[...] = to_low(dot(sq_ref[5], sel))
    w_o[...] = to_low(dot_tn(sel, sq_ref[4]))
    w_o2[...] = to_low(dot_tn(sel, sq_ref[6]))


def prepare_spatial(squares):
    shapes = [(WIDTH, 3 * SLOTS), (SLOTS, WIDTH), (WIDTH, SLOTS), (SLOTS, WIDTH)]
    return pl.pallas_call(
        prepare_spatial_kernel,
        in_specs=[in_vmem()] * 2,
        out_specs=[in_vmem()] * 4,
        out_shape=[jax.ShapeDtypeStruct(s, BF16) for s in shapes],
        compiler_params=pltpu.CompilerParams(vmem_limit_bytes=VMEM_LIMIT),
        name="spatial_weights",
    )(squares, slot_selector())


LOG2E = 1.4426950408889634
TEXT_ROWS = 128


def transformer_kernel(
    tokens_ref, resnet_ref, text_ref, vec_ref, ones_ref, sel_ref, w_qkv_ref, w_o_ref, w_q2_ref, w_kv2_ref, w_o2_ref,
    w_up_ref, w_down_ref, w_s7_ref,
    hidden_ref, packed_ref,
    queries, keys, values, text_kv,
):
    def vec(i):
        return vec_ref[i : i + 1, :]

    lane = lax.broadcasted_iota(jnp.int32, (CHUNK, SLOTS), 1)
    counter = jnp.where(lane % SLOT == HEAD_DIM, 1.0, 0.0)

    def project(i):
        a = to_low(normal_parts(tokens_ref[chunk_rows(i), :])[0] * vec(10) + vec(11))
        qkv = dot(a, w_qkv_ref[...])
        queries[chunk_rows(i), :] = to_low(qkv[:, :SLOTS])
        keys[chunk_rows(i), :] = to_low(qkv[:, SLOTS : 2 * SLOTS])
        values[chunk_rows(i), :] = to_low(qkv[:, 2 * SLOTS :] + counter)
        return ()

    over_chunks(lambda i: project(i))
    kv = to_low(dot(text_ref[...], w_kv2_ref[...]))
    text_kv[...] = jnp.zeros_like(text_kv)
    wide_kv = jnp.concatenate(
        [dot(kv[:, :WIDTH], sel_ref[...]), dot(kv[:, WIDTH:], sel_ref[...])], axis=1
    )
    text_kv[0 : wide_kv.shape[0], :] = wide_kv
    text_lane = lax.broadcasted_iota(jnp.int32, (CHUNK, TEXT_ROWS), 1)
    text_bias = jnp.where(text_lane < TEXT_LEN, 0.0, -1e30)

    def chunk_step(i, total):
        tokens = tokens_ref[chunk_rows(i), :]
        pairs = []
        for pair in range(HEADS // 2):
            lanes = slice(pair * GROUP, (pair + 1) * GROUP)
            query = queries[chunk_rows(i), lanes]
            key = keys[:, lanes]
            value = values[:, lanes]
            side = lax.broadcasted_iota(jnp.int32, (CHUNK, GROUP), 1) < SLOT
            both = None
            for head in range(2):
                zero = jnp.zeros_like(query)
                own_query = jnp.where(side, query, zero) if head == 0 else jnp.where(side, zero, query)
                scores = dot_nt(own_query, key) * (SCALE * LOG2E)
                raised = jnp.exp2(scores - jnp.max(scores, axis=1, keepdims=True))
                mixed = dot(to_low(raised), value)
                mixed = mixed * (1.0 / mixed[:, head * SLOT + HEAD_DIM : head * SLOT + HEAD_DIM + 1])
                both = mixed if head == 0 else jnp.where(side, both, mixed)
            pairs.append(to_low(both))
        tokens = tokens + (dot(jnp.concatenate(pairs, axis=1), w_o_ref[...]) + vec(12))
        c = to_low(normal_parts(tokens)[0] * vec(13) + vec(14))
        query2 = to_low(dot(c, w_q2_ref[...]))
        pairs = []
        for pair in range(HEADS // 2):
            lanes = slice(pair * GROUP, (pair + 1) * GROUP)
            text_keys = lane_halves(to_low(text_kv[:, lanes]))
            text_values = lane_halves(to_low(text_kv[:, SLOTS + pair * GROUP : SLOTS + (pair + 1) * GROUP]))
            scores = dot_nt(query2[:, lanes], text_keys) * SCALE
            probs = []
            for part in (scores[:, :TEXT_ROWS], scores[:, TEXT_ROWS:]):
                part = part + text_bias
                raised = jnp.exp(part - jnp.max(part, axis=1, keepdims=True))
                probs.append(to_low(raised * (1.0 / jnp.sum(raised, axis=1, keepdims=True))))
            pairs.append(to_low(dot(jnp.concatenate(probs, axis=1), text_values)))
        tokens = tokens + (dot(jnp.concatenate(pairs, axis=1), w_o2_ref[...]) + vec(15))
        f = to_low(normal_parts(tokens)[0] * vec(16) + vec(17))
        gate_up = dot(f, w_up_ref[...])
        inner = to_low(gate_up[:, :FF_INNER] * gelu_parts(gate_up[:, FF_INNER:])[0])
        tokens = tokens + (dot(inner, w_down_ref[...]) + vec(18))
        hidden = resnet_ref[chunk_rows(i), :] + (dot(to_low(tokens), w_s7_ref[...]) + vec(19))
        hidden_ref[chunk_rows(i), :] = hidden
        return (total + column_sum(hidden),)

    (total,) = over_chunks(chunk_step, zero_row())
    centre, scale = group_stats(hidden_ref, ones_ref[...], total)
    pack_rows(packed_ref, lambda rows: (hidden_ref[rows, :] - centre) * scale)


def pack_rows(packed_ref, rows_at):
    for member in range(CLIP):
        block = to_low(rows_at(slice(member * OWN, (member + 1) * OWN)))
        packed_ref[member, 0:64, :] = block[:, 0:128]
        packed_ref[member, 64:128, :] = block[:, 128:256]
        packed_ref[member, 128:160, :] = jnp.concatenate([block[0:32, 256:320], block[32:64, 256:320]], axis=1)


def transformer_block(tokens, resnet, text, vectors, prepared, cross_kv, up, down, w_s7):
    w_qkv, w_o, w_q2, w_o2 = prepared
    operands = (
        tokens, resnet, text, vectors, group_ones(), slot_selector(), w_qkv, w_o, w_q2, cross_kv, w_o2, up, down, w_s7,
    )
    return pl.pallas_call(
        transformer_kernel,
        in_specs=[in_vmem()] * len(operands),
        out_specs=[in_vmem()] * 2,
        out_shape=[
            jax.ShapeDtypeStruct((PIX, WIDTH), F32),
            jax.ShapeDtypeStruct((CLIP, 160, 128), BF16),
        ],
        scratch_shapes=[pltpu.VMEM((PIX, SLOTS), BF16)] * 3 + [pltpu.VMEM((TEXT_ROWS, 2 * SLOTS), F32)],
        compiler_params=pltpu.CompilerParams(vmem_limit_bytes=VMEM_LIMIT),
        name="transformer_block",
    )(*operands)


def head_kernel(
    valid_ref, total_ref, hidden_ref, branch_ref, target_ref, vec_ref, ones_ref, w_ref,
    packed_ref, loss_ref,
    mixed, act, slope,
):
    ones = ones_ref[...]
    gain = vec_ref[20:21, :]
    offset = vec_ref[21:22, :]
    column_total = zero_row()
    for member in range(CLIP):
        rows = slice(member * OWN, (member + 1) * OWN)
        last = branch_ref[member, 128:160, :]
        branch = jnp.concatenate(
            [
                branch_ref[member, 0:64, :].astype(F32),
                branch_ref[member, 64:128, :].astype(F32),
                jnp.concatenate([last[:, 0:64], last[:, 64:128]], axis=0).astype(F32),
            ],
            axis=1,
        )
        part = hidden_ref[rows, :] + branch
        mixed[rows, :] = part
        column_total = column_total + column_sum(part)
    centre, scale = group_stats(mixed, ones, column_total)

    def activate(i):
        normal = (mixed[chunk_rows(i), :] - centre) * scale
        mixed[chunk_rows(i), :] = normal
        value = normal * gain + offset
        share = sigmoid(value)
        act[chunk_rows(i), :] = to_low(value * share)
        slope[chunk_rows(i), :] = share * (1.0 + value * (1.0 - share)) * gain
        return ()

    over_chunks(lambda i: activate(i))
    weight = w_ref[...]
    by_tap = dot_nt(weight, act[...])
    predicted = jnp.zeros((8, PIX), F32)
    for tap in range(TAPS):
        predicted = predicted + shifted_lanes(by_tap[8 * tap : 8 * tap + 8], tap // 3 - 1, tap % 3 - 1)
    residual = (predicted - target_ref[...]) * valid_ref[0]
    loss_ref[...] = jnp.sum(residual * residual, keepdims=True)
    grad = to_low(2.0 * residual / total_ref[0]).astype(F32)
    columns = to_low(jnp.concatenate([shifted_lanes(grad, 1 - tap // 3, 1 - tap % 3) for tap in range(TAPS)], axis=0))
    total = zero_row()
    total_normal = zero_row()
    for i in range(CHUNKS):
        rows = slice(i * CHUNK, (i + 1) * CHUNK)
        part = dot_tn(columns[:, rows], weight) * slope[rows, :]
        slope[rows, :] = part
        total = total + column_sum(part)
        total_normal = total_normal + column_sum(part * mixed[rows, :])
    mean = group_mean(total, ones)
    mean_normal = group_mean(total_normal, ones)
    pack_rows(packed_ref, lambda rows: scale * (slope[rows, :] - mean - mixed[rows, :] * mean_normal))


def head_block(valid, total, hidden, branch, target, vectors, weight):
    return pl.pallas_call(
        head_kernel,
        in_specs=[in_smem(), in_smem()] + [in_vmem()] * 6,
        out_specs=[in_vmem()] * 2,
        out_shape=[jax.ShapeDtypeStruct((CLIP, 160, 128), BF16), jax.ShapeDtypeStruct((1, 1), F32)],
        scratch_shapes=[
            pltpu.VMEM((PIX, WIDTH), F32),
            pltpu.VMEM((PIX, WIDTH), BF16),
            pltpu.VMEM((PIX, WIDTH), F32),
        ],
        compiler_params=pltpu.CompilerParams(vmem_limit_bytes=VMEM_LIMIT),
        name="head_block",
    )(valid, total, hidden, branch, target, vectors, group_ones(), weight)


def product(left, right):
    return jnp.einsum("...i,ij->...j", left, right, preferred_element_type=jnp.float32)


def time_embed(step_values, time_w1, time_w2, temb_w, temb_bias):
    half_width = WIDTH // 2
    frequency = jnp.exp(-math.log(10000.0) * jnp.arange(half_width, dtype=jnp.float32) / half_width)
    angles = step_values[..., None] * frequency
    encoding = jnp.concatenate([jnp.cos(angles), jnp.sin(angles)], axis=-1)
    hidden = product(to_low(encoding), time_w1)
    hidden = product(to_low(jax.nn.silu(hidden)), time_w2)
    return product(to_low(jax.nn.silu(hidden)), temb_w) + temb_bias


def swap_cores(values):
    return lax.ppermute(values, "dp", [(0, 1), (1, 0)])


def frames_bit(bit):
    return (lax.axis_index("frames") // bit) % 2


def swap_frames(values, bit):
    size = lax.axis_size("frames")
    return lax.ppermute(values, "frames", [(i, i ^ bit) for i in range(size)])


def sum_over_frames(values, order):
    for bit in order:
        rows = values.shape[0] // 2
        mine = frames_bit(bit)
        own = lax.dynamic_slice_in_dim(values, mine * rows, rows, 0)
        other = lax.dynamic_slice_in_dim(values, (1 - mine) * rows, rows, 0)
        values = own + swap_frames(other, bit)
    for bit in reversed(order):
        got = swap_frames(values, bit)
        values = jnp.where(
            frames_bit(bit) == 0,
            jnp.concatenate([values, got], 0),
            jnp.concatenate([got, values], 0),
        )
    return values


def sum_rows(values):
    size = lax.axis_size("frames")
    bits = []
    bit = 1
    while bit < size:
        bits.append(bit)
        bit *= 2
    unit = 8 * size
    rows = values.shape[0]
    padded = -(-rows // unit) * unit
    values = jnp.pad(values, ((0, padded - rows), (0, 0)))
    cut = (padded // unit + 1) // 2 * unit
    first = sum_over_frames(values[:cut], bits)
    second = sum_over_frames(values[cut:], [bits[1], bits[0]] + bits[2:])
    return jnp.concatenate([first, second], 0)[:rows]


def sample_groups():
    groups = []
    for block in range(lax.axis_size("frames") // CLIP):
        for half in range(2):
            groups.append(
                [
                    2 * (block * CLIP + half * HALF + place) + core
                    for core in range(2)
                    for place in range(HALF)
                ]
            )
    return groups


def swap_samples(values):
    size = lax.axis_size("frames")
    pairs = []
    for frame in range(size):
        half = (frame % CLIP) // HALF
        pairs.append((2 * frame + 1 - half, 2 * (frame ^ HALF) + half))
    return lax.ppermute(values, ("frames", "dp"), pairs)


def shards(
    latents,
    noise,
    timesteps,
    image_flags,
    frame_counts,
    text,
    conv_in,
    res_convs,
    conv_out,
    time_w1,
    time_w2,
    temb_w,
    spatial_squares,
    cross_kv,
    spatial_up,
    spatial_down,
    frozen_vectors,
    motion_squares,
    motion_up,
    motion_down,
    motion_vectors,
    square_moment,
    up_moment,
    down_moment,
    vector_moment1,
    vector_moment2,
    square_ema,
    up_ema,
    down_ema,
    vector_ema,
):
    dp_index = lax.axis_index("dp")
    place = lax.axis_index("frames")
    block = place // CLIP
    place = place % CLIP
    half = place // HALF
    stays = half == dp_index
    frame = jnp.where(stays, place, (place + HALF) % CLIP)
    frozen_prepared = prepare_spatial(spatial_squares)
    pair = jnp.concatenate([latents.reshape(PIX, CHAN).T, noise.reshape(PIX, CHAN).T], axis=0)
    pair = jnp.where(stays, pair, swap_samples(pair)).astype(F32)

    def of_block(values):
        return lax.dynamic_index_in_dim(values[0], block, 0, keepdims=False)

    step_count = of_block(timesteps)
    facts = jnp.stack([step_count // 32, step_count % 32, of_block(image_flags)])
    facts = jnp.pad(facts.astype(BF16)[None, :], ((0, 0), (0, TEXT_DIM - 3)))
    text_facts = jnp.concatenate([of_block(text), facts], axis=0)
    text_facts = jnp.where(stays, text_facts, swap_cores(text_facts))
    facts = text_facts[TEXT_LEN].astype(F32)
    step_values = (facts[0] * 32.0 + facts[1])[None]
    flag = facts[2]
    phases = (step_values / 1000.0 + 0.008) / 1.008 * (math.pi / 2)
    keep_rate = jnp.cos(phases)[:, None]
    noise_rate = jnp.sin(phases)[:, None]
    spare = ((0, 8 - CHAN), (0, 0))
    noisy = jnp.pad(keep_rate * pair[:CHAN] + noise_rate * pair[CHAN:], spare)
    target = jnp.pad(keep_rate * pair[CHAN:] - noise_rate * pair[:CHAN], spare)
    temb_res = time_embed(step_values, time_w1, time_w2, temb_w, frozen_vectors[22])
    w_in = jnp.pad(conv_in.reshape(TAPS, CHAN, WIDTH), ((0, 0), (0, 8 - CHAN), (0, 0)))
    w_head = jnp.swapaxes(conv_out.reshape(TAPS, WIDTH, CHAN), 1, 2)
    w_head = jnp.pad(w_head, ((0, 0), (0, 8 - CHAN), (0, 0))).reshape(8 * TAPS, WIDTH)
    resnet, tokens = resnet_block(
        noisy,
        frozen_vectors,
        temb_res,
        w_in.reshape(8 * TAPS, WIDTH),
        res_convs.reshape(2, 3, 3 * WIDTH, WIDTH),
        spatial_squares[0],
    )
    hidden, packed = transformer_block(
        tokens, resnet, text_facts, frozen_vectors, frozen_prepared, cross_kv, spatial_up, spatial_down,
        spatial_squares[7],
    )
    groups = sample_groups()

    def exchange(values):
        return lax.all_to_all(
            values, ("frames", "dp"), split_axis=0, concat_axis=0, tiled=True, axis_index_groups=groups
        )

    arrived = exchange(packed)
    count = lax.dynamic_slice(frame_counts, (half, block), (1, 1)).reshape(1)
    keep = jnp.reshape(1.0 - flag, (1,))
    weights = prepare(motion_squares, motion_up, motion_down)
    branch, u, u2, u3, qkv1, qkv2, o1, o2, last = motion_forward(
        arrived, count, keep, weights, motion_vectors
    )
    frame_valid = (frame < count[0]).astype(F32)
    total_count = 4.0 * PIX * jnp.sum(frame_counts).astype(F32)
    grad, loss_part = head_block(
        frame_valid.reshape(1), total_count.reshape(1), hidden, exchange(branch), target, frozen_vectors, w_head
    )
    grad_in = exchange(grad)
    du3, early, g9, feed_sums = feed_backward(grad_in, keep, weights, motion_vectors, u3, last)
    du2, g5, g6, g7, g8, second_sums = second_backward(
        du3, count, weights, motion_vectors, u2, qkv2, o2
    )
    late = first_backward(
        du2, count, loss_part[0], arrived, weights, motion_vectors, u, qkv1, o1,
        (g5, g6, g7, g8, g9, feed_sums, second_sums),
    )
    core = dp_index.reshape(1)

    def sum_over_devices(both):
        own = lax.dynamic_index_in_dim(both, dp_index, 0, keepdims=False)
        other = lax.dynamic_index_in_dim(both, 1 - dp_index, 0, keepdims=False)
        return sum_rows(own + swap_cores(other))

    early = sum_over_devices(early)
    up_moment_new, down_moment_new, ahead = wide_moments(early, up_moment, down_moment)
    sent = lax.dynamic_slice_in_dim(ahead, (1 - dp_index) * DOWN_TILES, UP_TILES, 0)
    wide = wide_direction(core, ahead, swap_cores(sent))
    up_new, up_ema_new, down_new, down_ema_new = wide_update(
        core, wide, swap_cores(wide), motion_up, motion_down, up_ema, down_ema
    )
    late = sum_over_devices(late)
    square, square_moment_new, moment_first, moment_second, vector_new, vector_ema_new, loss_row = square_directions(
        late, square_moment, vector_moment1, vector_moment2, motion_vectors, vector_ema
    )
    square_new, square_ema_new = square_update(
        core, square, swap_cores(square), motion_squares, square_ema
    )
    return (
        loss_row[0, 0],
        total_count,
        square_new,
        square_moment_new,
        square_ema_new,
        up_new,
        up_moment_new,
        up_ema_new,
        down_new,
        down_moment_new,
        down_ema_new,
        moment_first,
        moment_second,
        vector_new,
        vector_ema_new,
    )


def solution(mesh):
    return jax.shard_map(
        shards,
        mesh=mesh,
        in_specs=(
            P("dp", "frames", None, None),
            P("dp", "frames", None, None),
            P("dp", None),
            P("dp", None),
            P(),
            P("dp", None, None, None),
            P(),
            P(),
            P(),
            P(),
            P(),
            P(),
            P(),
            P(),
            P(),
            P(),
            P(),
            P(),
            P(),
            P(),
            P(),
            P("dp", None, None),
            P(None, "dp"),
            P("dp", None),
            P(),
            P(),
            P("dp", None, None),
            P(None, "dp"),
            P("dp", None),
            P(),
        ),
        out_specs=(
            P(),
            P(),
            P(),
            P("dp", None, None),
            P("dp", None, None),
            P(),
            P(None, "dp"),
            P(None, "dp"),
            P(),
            P("dp", None),
            P("dp", None),
            P(),
            P(),
            P(),
            P(),
        ),
        check_vma=False,
    )
```

```python
import math

import jax
import jax.numpy as jnp
import numpy as np
from jax import lax
from jax.experimental import pallas as pl
from jax.experimental.pallas import tpu as pltpu
from jax.sharding import PartitionSpec as P

WIDTH = 320
HEADS = 8
HEAD_DIM = 40
FF_INNER = 1280
CLIP = 16
HALF = 8
PIX = 1024
LATENT = 32
TEXT_LEN = 77
TEXT_DIM = 768
GN_GROUPS = 32
F32 = jnp.float32
BF16 = jnp.bfloat16
OWN = PIX // CLIP
SLOT = 64
SLOTS = HEADS * SLOT
CHUNK = 512
CHUNKS = PIX // CHUNK
GROUP = 128
GROUPS = PIX // GROUP
SCALE = 1.0 / math.sqrt(HEAD_DIM)


def to_low(values):
    return values.astype(BF16)


def dot(left, right):
    return lax.dot_general(left, right, (((1,), (0,)), ((), ())), preferred_element_type=F32)


def dot_nt(left, right):
    return lax.dot_general(left, right, (((1,), (1,)), ((), ())), preferred_element_type=F32)


def dot_tn(left, right):
    return lax.dot_general(left, right, (((0,), (0,)), ((), ())), preferred_element_type=F32)


def in_vmem():
    return pl.BlockSpec(memory_space=pltpu.VMEM)


def in_smem():
    return pl.BlockSpec(memory_space=pltpu.SMEM)


def call(kernel, operands, outs, name, micros, scalars=0, scratch=(), limit=60):
    specs = [in_smem()] * scalars + [in_vmem()] * (len(operands) - scalars)
    return pl.pallas_call(
        kernel,
        in_specs=specs,
        out_specs=[in_vmem()] * len(outs),
        out_shape=[jax.ShapeDtypeStruct(shape, kind) for shape, kind in outs],
        scratch_shapes=list(scratch),
        cost_estimate=pl.CostEstimate(flops=int(micros * 1.1e9), bytes_accessed=0, transcendentals=0),
        compiler_params=pltpu.CompilerParams(vmem_limit_bytes=limit * 2**20),
        name=name,
    )(*operands)


def slot_selector():
    out = np.zeros((WIDTH, SLOTS), np.float32)
    for head in range(HEADS):
        for j in range(HEAD_DIM):
            out[head * HEAD_DIM + j, head * SLOT + j] = 1.0
    return jnp.asarray(out, BF16)


def frame_codes():
    positions = np.arange(CLIP, dtype=np.float32)[:, None]
    column = np.arange(WIDTH)
    frequency = np.exp(np.float32(-math.log(10000.0)) * (2 * (column // 2)).astype(np.float32) / WIDTH)
    angles = positions * frequency.astype(np.float32)
    codes = np.where(column % 2 == 0, np.sin(angles), np.cos(angles)).astype(np.float32)
    return jnp.asarray(np.repeat(codes, 8, axis=0))


def unpack_positions(packed_ref, wide_ref):
    wide_ref[:, :, 0:128] = packed_ref[:, 0:64, :].astype(F32)
    wide_ref[:, :, 128:256] = packed_ref[:, 64:128, :].astype(F32)
    last = packed_ref[:, 128:160, :].astype(F32)
    wide_ref[:, 0:32, 256:320] = last[:, :, 0:64]
    wide_ref[:, 32:64, 256:320] = last[:, :, 64:128]


def pack_positions(wide_ref, packed_ref):
    packed_ref[:, 0:64, :] = to_low(wide_ref[:, :, 0:128])
    packed_ref[:, 64:128, :] = to_low(wide_ref[:, :, 128:256])
    last = jnp.concatenate([wide_ref[:, 0:32, 256:320], wide_ref[:, 32:64, 256:320]], axis=2)
    packed_ref[:, 128:160, :] = to_low(last)


def tokens_of(wide_ref):
    parts = [wide_ref[:, 8 * group : 8 * group + 8, :].reshape(GROUP, WIDTH) for group in range(GROUPS)]
    return jnp.concatenate(parts, axis=0)


def put_tokens(wide_ref, tokens):
    for group in range(GROUPS):
        part = tokens[group * GROUP : (group + 1) * GROUP].reshape(CLIP, 8, WIDTH)
        wide_ref[:, 8 * group : 8 * group + 8, :] = part


def every_group(rows):
    return jnp.concatenate([rows] * GROUPS, axis=0)


def normal_parts(values):
    centre = jnp.mean(values, axis=-1, keepdims=True)
    shifted = values - centre
    scale = lax.rsqrt(jnp.mean(shifted * shifted, axis=-1, keepdims=True) + 1e-05)
    return shifted * scale, scale


def normal_back(grad, normal, scale, gain):
    inner = grad * gain
    return scale * (
        inner
        - jnp.mean(inner, axis=-1, keepdims=True)
        - normal * jnp.mean(inner * normal, axis=-1, keepdims=True)
    )


def erf_parts(gate):
    bell = jnp.exp(-0.5 * gate * gate)
    size = jnp.abs(gate) * (1.0 / math.sqrt(2.0))
    t = 1.0 / (1.0 + 0.3275911 * size)
    poly = t * (
        0.254829592
        + t * (-0.284496736 + t * (1.421413741 + t * (-1.453152027 + t * 1.061405429)))
    )
    tail = poly * bell
    return jnp.where(gate < 0.0, tail - 1.0, 1.0 - tail), bell


def gelu_parts(gate):
    erf, bell = erf_parts(gate)
    share = 0.5 + 0.5 * erf
    return gate * share, share + gate * bell * (1.0 / math.sqrt(2.0 * math.pi))


def lane_halves(values):
    lane = lax.broadcasted_iota(jnp.int32, values.shape, 1)
    zero = jnp.zeros_like(values)
    return jnp.concatenate(
        [jnp.where(lane < SLOT, values, zero), jnp.where(lane < SLOT, zero, values)], axis=0
    )


def key_bias(count, queries_first):
    shape = (GROUP, 2 * GROUP) if queries_first else (2 * GROUP, GROUP)
    row = lax.broadcasted_iota(jnp.int32, shape, 0)
    column = lax.broadcasted_iota(jnp.int32, shape, 1)
    key = (column if queries_first else row) % GROUP
    valid = (row % 8 == column % 8) & (key // 8 < count)
    return jnp.where(valid, 0.0, -1e30).astype(F32)


def attend_chunk(qkv, bias):
    out = []
    for group in range(GROUPS):
        rows = slice(group * GROUP, (group + 1) * GROUP)
        pairs = []
        for pair in range(HEADS // 2):
            lanes = pair * 2 * SLOT
            queries = qkv[rows, lanes : lanes + GROUP]
            keys = lane_halves(qkv[rows, SLOTS + lanes : SLOTS + lanes + GROUP])
            values = lane_halves(qkv[rows, 2 * SLOTS + lanes : 2 * SLOTS + lanes + GROUP])
            scores = dot_nt(queries, keys) * SCALE + bias
            probs = []
            for part in (scores[:, :GROUP], scores[:, GROUP:]):
                raised = jnp.exp(part - jnp.max(part, axis=1, keepdims=True))
                probs.append(raised * (1.0 / jnp.sum(raised, axis=1, keepdims=True)))
            pairs.append(to_low(dot(to_low(jnp.concatenate(probs, axis=1)), values)))
        out.append(jnp.concatenate(pairs, axis=1))
    return jnp.concatenate(out, axis=0)


def motion_forward_kernel(
    count_ref, keep_ref, arrived_ref, codes_ref, vec_ref, w_in_ref, w_qkv_ref, w_o_ref, w_up_ref, w_down_ref, w_out_ref,
    branch_ref, u_ref, u2_ref, u3_ref, qkv1_ref, qkv2_ref, o1_ref, o2_ref, last_ref,
    wide,
):
    def vec(i):
        return vec_ref[i : i + 1, :]

    unpack_positions(arrived_ref, wide)
    bias = key_bias(count_ref[0], True)
    codes = every_group(codes_ref[...])
    inputs = to_low(tokens_of(wide) * vec(0) + vec(1))
    stream = dot(inputs, w_in_ref[...]) + vec(2)
    for index, (first, x_ref, qkv_ref, o_ref) in enumerate(
        ((3, u_ref, qkv1_ref, o1_ref), (6, u2_ref, qkv2_ref, o2_ref))
    ):
        x_ref[...] = stream
        a = to_low(normal_parts(stream)[0] * vec(first) + vec(first + 1) + codes)
        qkv = to_low(dot(a, w_qkv_ref[index]))
        qkv_ref[...] = qkv
        mixture = attend_chunk(qkv, bias)
        o_ref[...] = mixture
        stream = stream + (dot(mixture, w_o_ref[index]) + vec(first + 2))
    u3_ref[...] = stream
    c = to_low(normal_parts(stream)[0] * vec(9) + vec(10))
    gate_up = dot(c, w_up_ref[...])
    inner = to_low(gate_up[:, :FF_INNER] * gelu_parts(gate_up[:, FF_INNER:])[0])
    last = to_low(stream + (dot(inner, w_down_ref[...]) + vec(11)))
    last_ref[...] = last
    put_tokens(wide, (dot(last, w_out_ref[...]) + vec(12)) * keep_ref[0])
    pack_positions(wide, branch_ref)


def motion_forward(arrived, count, keep, weights, vectors):
    outs = [((CLIP, 160, 128), BF16)] + [((PIX, WIDTH), F32)] * 3 + [((PIX, 3 * SLOTS), BF16)] * 2
    outs = outs + [((PIX, SLOTS), BF16)] * 2 + [((PIX, WIDTH), BF16)]
    operands = (count, keep, arrived, frame_codes(), vectors) + tuple(
        weights[name] for name in ("in", "qkv", "o", "up", "down", "out")
    )
    return call(
        motion_forward_kernel, operands, outs, "motion_forward", 23, 2, [pltpu.VMEM((CLIP, OWN, WIDTH), F32)]
    )


def prepare_kernel(sq_ref, up_ref, down_ref, sel_ref, w_in, w_qkv, w_o, w_up, w_down, w_out, t_in, t_qkv, t_o, t_up, t_down, t_out):
    sel = sel_ref[...]
    low = [to_low(sq_ref[i]) for i in range(10)]
    w_in[...] = low[0]
    t_in[...] = low[0].T
    w_out[...] = low[9]
    t_out[...] = low[9].T
    for index, first in enumerate((1, 5)):
        for j in range(3):
            padded = to_low(dot(low[first + j], sel))
            w_qkv[index, :, j * SLOTS : (j + 1) * SLOTS] = padded
            t_qkv[index, j * SLOTS : (j + 1) * SLOTS, :] = padded.T
        padded = to_low(dot_nt(low[first + 3].T, sel.T))
        t_o[index] = padded
        w_o[index] = padded.T
    up = to_low(up_ref[...])
    w_up[...] = up
    t_up[...] = up.T
    down = to_low(down_ref[...])
    t_down[...] = down
    w_down[...] = down.T


def prepare(squares, up, down):
    shapes = {
        "in": (WIDTH, WIDTH), "qkv": (2, WIDTH, 3 * SLOTS), "o": (2, SLOTS, WIDTH), "up": (WIDTH, 2 * FF_INNER),
        "down": (FF_INNER, WIDTH), "out": (WIDTH, WIDTH),
        "in_t": (WIDTH, WIDTH), "qkv_t": (2, 3 * SLOTS, WIDTH), "o_t": (2, WIDTH, SLOTS), "up_t": (2 * FF_INNER, WIDTH),
        "down_t": (WIDTH, FF_INNER), "out_t": (WIDTH, WIDTH),
    }
    made = call(
        prepare_kernel, (squares, up, down, slot_selector()), [(x, BF16) for x in shapes.values()], "motion_weights", 9
    )
    return dict(zip(shapes, made))


def column_sum(values):
    return jnp.sum(values, axis=0, keepdims=True)


def feed_backward_kernel(
    core_ref, keep_ref, grad_ref, u3_ref, last_ref, vec_ref, w_up_ref, t_up_ref, t_down_ref, t_out_ref,
    du3_ref, own_ref, other_ref, g_out_ref, g_vec_ref,
    wide,
):
    gain = vec_ref[9:10, :]
    unpack_positions(grad_ref, wide)
    dbranch = to_low(tokens_of(wide) * keep_ref[0])
    g_out_ref[...] = dot_tn(last_ref[...], dbranch)
    du4 = dot(dbranch, t_out_ref[...])
    d4 = to_low(du4)
    normal, scale = normal_parts(u3_ref[...])
    c = to_low(normal * gain + vec_ref[10:11, :])
    z = dot(c, w_up_ref[...])
    value = z[:, :FF_INNER]
    gelu, slope = gelu_parts(z[:, FF_INNER:])
    inner = to_low(value * gelu)
    dinner = dot(d4, t_down_ref[...])
    dz = to_low(jnp.concatenate([dinner * gelu, dinner * value * slope], axis=1))
    g_down = dot_tn(d4, inner)
    g_up = dot_tn(c, dz)
    bound = jnp.maximum(jnp.max(jnp.abs(g_up)), jnp.max(jnp.abs(g_down)))

    def put(ref, half):
        for tile in range(UP_TILES):
            start = half * FF_INNER + tile * 128
            ref[tile_rows(tile)] = g_up[:, start : start + 128]
        for tile in range(DOWN_TILES):
            start = half * (FF_INNER // 2) + tile * 128
            ref[tile_rows(UP_TILES + tile)] = g_down[:, start : start + 128]
        used = (UP_TILES + DOWN_TILES) * WIDTH
        ref[used:] = jnp.full((EARLY_ROWS - used, 128), bound)

    for core in range(2):

        @pl.when(core_ref[0] == core)
        def _(core=core):
            put(own_ref, core)
            put(other_ref, 1 - core)

    dc = dot(dz, t_up_ref[...])
    du3_ref[...] = du4 + normal_back(dc, normal, scale, gain)
    rows = [column_sum(dc * normal), column_sum(dc), column_sum(d4.astype(F32)), column_sum(dbranch.astype(F32))]
    g_vec_ref[...] = jnp.concatenate(rows + [jnp.zeros((4, WIDTH), F32)], axis=0)


def feed_backward(core, grad, keep, weights, vectors, u3, last):
    operands = (core, keep, grad, u3, last, vectors) + tuple(weights[n] for n in ("up", "up_t", "down_t", "out_t"))
    outs = [(PIX, WIDTH), (EARLY_ROWS, 128), (EARLY_ROWS, 128), (WIDTH, WIDTH), (8, WIDTH)]
    return call(
        feed_backward_kernel, operands, [(x, F32) for x in outs], "feed_backward", 18, 2,
        [pltpu.VMEM((CLIP, OWN, WIDTH), F32)],
    )


def attend_back_chunk(qkv, d_mixture, bias):
    out = []
    for group in range(GROUPS):
        rows = slice(group * GROUP, (group + 1) * GROUP)
        grads = [[], [], []]
        for pair in range(HEADS // 2):
            lanes = pair * 2 * SLOT
            queries = qkv[rows, lanes : lanes + GROUP]
            keys = lane_halves(qkv[rows, SLOTS + lanes : SLOTS + lanes + GROUP])
            values = lane_halves(qkv[rows, 2 * SLOTS + lanes : 2 * SLOTS + lanes + GROUP])
            d_out = d_mixture[rows, lanes : lanes + GROUP]
            scores = dot_nt(keys, queries) * SCALE + bias
            d_probs = dot_nt(values, d_out)
            low_probs = []
            d_scores = []
            for head in range(2):
                part = scores[head * GROUP : (head + 1) * GROUP]
                d_part = d_probs[head * GROUP : (head + 1) * GROUP]
                raised = jnp.exp(part - jnp.max(part, axis=0, keepdims=True))
                probs = raised * (1.0 / jnp.sum(raised, axis=0, keepdims=True))
                low_probs.append(to_low(probs))
                d_scores.append(to_low(probs * (d_part - jnp.sum(probs * d_part, axis=0, keepdims=True))))
            low_probs = jnp.concatenate(low_probs, axis=0)
            d_scores = jnp.concatenate(d_scores, axis=0)
            d_values = dot(low_probs, d_out)
            d_keys = dot(d_scores, queries) * SCALE
            d_queries = dot_tn(d_scores, keys) * SCALE
            lane = lax.broadcasted_iota(jnp.int32, (GROUP, GROUP), 1)
            grads[0].append(to_low(d_queries))
            grads[1].append(to_low(jnp.where(lane < SLOT, d_keys[:GROUP], d_keys[GROUP:])))
            grads[2].append(to_low(jnp.where(lane < SLOT, d_values[:GROUP], d_values[GROUP:])))
        out.append(jnp.concatenate(grads[0] + grads[1] + grads[2], axis=1))
    return jnp.concatenate(out, axis=0)


def attention_backward(count, grad, stream, qkv, gain, t_o, t_qkv):
    d_out = to_low(grad)
    d_mixture = to_low(dot(d_out, t_o))
    d_qkv = attend_back_chunk(qkv, d_mixture, key_bias(count, False))
    normal, scale = normal_parts(stream)
    d_a = dot(d_qkv, t_qkv)
    rows = [column_sum(d_a * normal), column_sum(d_a), column_sum(d_out.astype(F32))]
    return grad + normal_back(d_a, normal, scale, gain), d_qkv, rows


def second_backward_kernel(
    count_ref, grad_ref, u2_ref, qkv_ref, vec_ref, t_o_ref, t_qkv_ref,
    du2_ref, d_qkv_ref, g_vec_ref,
):
    du2, d_qkv, rows = attention_backward(
        count_ref[0], grad_ref[...], u2_ref[...], qkv_ref[...], vec_ref[6:7, :], t_o_ref[1], t_qkv_ref[1]
    )
    du2_ref[...] = du2
    d_qkv_ref[...] = d_qkv
    g_vec_ref[...] = jnp.concatenate(rows + [jnp.zeros((5, WIDTH), F32)], axis=0)


def second_backward(grad, count, weights, vectors, u2, qkv):
    operands = (count, grad, u2, qkv, vectors, weights["o_t"], weights["qkv_t"])
    outs = [((PIX, WIDTH), F32), ((PIX, 3 * SLOTS), BF16), ((8, WIDTH), F32)]
    return call(second_backward_kernel, operands, outs, "second_backward", 15, 1, limit=36)


def first_backward_kernel(
    count_ref, grad_ref, u_ref, qkv_ref, arrived_ref, vec_ref, t_o_ref, t_qkv_ref, t_in_ref,
    du_ref, d_qkv_ref, g_vec_ref,
    wide,
):
    unpack_positions(arrived_ref, wide)
    du, d_qkv, rows = attention_backward(
        count_ref[0], grad_ref[...], u_ref[...], qkv_ref[...], vec_ref[3:4, :], t_o_ref[0], t_qkv_ref[0]
    )
    du = to_low(du)
    du_ref[...] = du
    d_qkv_ref[...] = d_qkv
    d_inputs = dot(du, t_in_ref[...])
    top = [column_sum(d_inputs * tokens_of(wide)), column_sum(d_inputs), column_sum(du.astype(F32))]
    g_vec_ref[...] = jnp.concatenate(top + rows + [jnp.zeros((2, WIDTH), F32)], axis=0)


def first_backward(grad, count, arrived, weights, vectors, u, qkv):
    operands = (count, grad, u, qkv, arrived, vectors, weights["o_t"], weights["qkv_t"], weights["in_t"])
    outs = [((PIX, WIDTH), BF16), ((PIX, 3 * SLOTS), BF16), ((8, WIDTH), F32)]
    return call(
        first_backward_kernel, operands, outs, "first_backward", 17, 1, [pltpu.VMEM((CLIP, OWN, WIDTH), F32)], limit=36
    )


def attention_grads(grad, stream, d_qkv, mixture, codes, gain, offset, sel_t):
    padded = dot_tn(mixture, to_low(grad))
    w_o_grad = jnp.concatenate([padded[head * SLOT : head * SLOT + HEAD_DIM] for head in range(HEADS)], axis=0)
    a = to_low(normal_parts(stream)[0] * gain + offset + every_group(codes))
    grads = []
    for j in range(3):
        tight = to_low(dot(d_qkv[:, j * SLOTS : (j + 1) * SLOTS], sel_t))
        grads.append(dot_tn(a, tight))
    return grads + [w_o_grad]


def second_grads_kernel(grad_ref, u2_ref, d_qkv_ref, o_ref, codes_ref, vec_ref, sel_t_ref, gq_ref, gk_ref, gv_ref, go_ref):
    grads = attention_grads(
        grad_ref[...], u2_ref[...], d_qkv_ref[...], o_ref[...], codes_ref[...], vec_ref[6:7, :], vec_ref[7:8, :], sel_t_ref[...]
    )
    for ref, value in zip((gq_ref, gk_ref, gv_ref, go_ref), grads):
        ref[...] = value


def second_grads(grad, vectors, u2, d_qkv, mixture):
    operands = (grad, u2, d_qkv, mixture, frame_codes(), vectors, slot_selector().T)
    return call(second_grads_kernel, operands, [((WIDTH, WIDTH), F32)] * 4, "second_grads", 7, limit=36)


def first_grads_kernel(
    core_ref, loss_ref, grad_ref, u_ref, d_qkv_ref, o_ref, du_ref, arrived_ref, codes_ref, vec_ref, sel_t_ref,
    g5_ref, g6_ref, g7_ref, g8_ref, g9_ref, feed_vec_ref, second_vec_ref, first_vec_ref,
    own_ref, other_ref,
    wide,
):
    unpack_positions(arrived_ref, wide)
    grads = attention_grads(
        grad_ref[...], u_ref[...], d_qkv_ref[...], o_ref[...], codes_ref[...], vec_ref[3:4, :], vec_ref[4:5, :], sel_t_ref[...]
    )
    inputs = to_low(tokens_of(wide) * vec_ref[0:1, :] + vec_ref[1:2, :])
    later = [ref[...] for ref in (g5_ref, g6_ref, g7_ref, g8_ref, g9_ref)]
    squares = [dot_tn(inputs, du_ref[...])] + grads + later
    vector_rows = jnp.concatenate(
        [first_vec_ref[0:6, :], second_vec_ref[0:3, :], feed_vec_ref[0:4, :], jnp.full((3, WIDTH), loss_ref[0])], axis=0
    )
    bound = jnp.max(jnp.abs(vector_rows))
    for square in squares:
        bound = jnp.maximum(bound, jnp.max(jnp.abs(square)))
    pieces = [vector_rows[:, 64 * j : 64 * (j + 1)] for j in range(5)]
    side = jnp.concatenate(pieces + [jnp.zeros((WIDTH - 80, 64), F32)], axis=0)

    def put(ref, half):
        own = squares[5 * half : 5 * half + 5]
        for index in range(5):
            ref[tile_rows(2 * index)] = own[index][:, 0:128]
            ref[tile_rows(2 * index + 1)] = own[index][:, 128:256]
        for pair in range(2):
            ref[tile_rows(10 + pair)] = jnp.concatenate([own[2 * pair][:, 256:320], own[2 * pair + 1][:, 256:320]], axis=1)
        ref[tile_rows(12)] = jnp.concatenate([own[4][:, 256:320], side], axis=1)
        ref[13 * WIDTH :] = jnp.full((LATE_ROWS - 13 * WIDTH, 128), bound)

    for core in range(2):

        @pl.when(core_ref[0] == core)
        def _(core=core):
            put(own_ref, core)
            put(other_ref, 1 - core)


def first_grads(core, loss_part, grad, arrived, vectors, u, d_qkv, mixture, du, later):
    operands = (
        core, loss_part, grad, u, d_qkv, mixture, du, arrived, frame_codes(), vectors, slot_selector().T,
    ) + tuple(later)
    outs = [((LATE_ROWS, 128), F32)] * 2
    return call(first_grads_kernel, operands, outs, "first_grads", 10, 2, [pltpu.VMEM((CLIP, OWN, WIDTH), F32)], limit=44)


MUON_RATE = 0.2
ADAM_RATE = 0.4
DECAY = 0.01
AVERAGE = 0.75
STEP = 10
SHRINK = 1.0 - MUON_RATE * DECAY
SQUARE_RATE = MUON_RATE * 0.2 * math.sqrt(WIDTH)
UP_RATE = MUON_RATE * 0.2 * math.sqrt(2 * FF_INNER)
DOWN_RATE = MUON_RATE * 0.2 * math.sqrt(FF_INNER)
UP_TILES = 10
DOWN_TILES = 5
WIDE_TILES = 2 * UP_TILES
EARLY_ROWS = 4864 + 16
LATE_ROWS = 4224 + 16


def tile_rows(index):
    return slice(index * WIDTH, (index + 1) * WIDTH)


def halves(values):
    high = values.astype(BF16)
    return (high, (values - high.astype(F32)).astype(BF16))


def triple(left, right, transposed=False):
    stacked = jnp.concatenate([left[0], left[0], left[1]], axis=1)
    if transposed:
        return dot_nt(stacked, jnp.concatenate([right[0], right[1], right[0]], axis=1))
    return dot(stacked, jnp.concatenate([right[0], right[1], right[0]], axis=0))


def scaled_to_unit(matrix):
    return matrix * (1.0 / (jnp.sqrt(jnp.sum(matrix * matrix, keepdims=True)) + 1e-07))


def wide_moments_kernel(sum_ref, up_ref, down_ref, up_new_ref, down_new_ref, ahead_ref):
    for tile in range(UP_TILES):
        lanes = slice(128 * tile, 128 * (tile + 1))
        gradient = sum_ref[tile_rows(tile)]
        moment = 0.95 * up_ref[:, lanes] + gradient
        up_new_ref[:, lanes] = moment
        ahead_ref[tile] = gradient + 0.95 * moment
    for tile in range(DOWN_TILES):
        lanes = slice(128 * tile, 128 * (tile + 1))
        gradient = sum_ref[tile_rows(UP_TILES + tile)]
        moment = 0.95 * down_ref[:, lanes] + gradient
        down_new_ref[:, lanes] = moment
        ahead_ref[UP_TILES + tile] = gradient + 0.95 * moment


def wide_moments(summed, up_moment, down_moment):
    outs = [up_moment.shape, down_moment.shape, (UP_TILES + DOWN_TILES, WIDTH, 128)]
    return call(
        wide_moments_kernel, (summed, up_moment, down_moment), [(x, F32) for x in outs], "wide_moments", 4, limit=32
    )


def wide_direction_kernel(core_ref, own_ref, got_ref, o_ref, matrix):
    def put(tile, value):
        matrix[:, 128 * tile : 128 * (tile + 1)] = value

    @pl.when(core_ref[0] == 0)
    def _():
        for tile in range(UP_TILES):
            put(tile, own_ref[tile])
            put(UP_TILES + tile, got_ref[tile])

    @pl.when(core_ref[0] != 0)
    def _():
        for tile in range(DOWN_TILES):
            put(tile, got_ref[UP_TILES - DOWN_TILES + tile])
            put(DOWN_TILES + tile, own_ref[UP_TILES + tile])
        matrix[:, 128 * UP_TILES :] = jnp.zeros((WIDTH, 128 * UP_TILES), F32)

    parts = halves(scaled_to_unit(matrix[...]))
    gram = triple(parts, parts, True)
    row = lax.broadcasted_iota(jnp.int32, (WIDTH, WIDTH), 0)
    column = lax.broadcasted_iota(jnp.int32, (WIDTH, WIDTH), 1)
    total = None
    for step in range(5):
        gram_parts = halves(gram)
        polynomial = -4.775 * gram + 2.0315 * triple(gram_parts, gram_parts)
        poly_parts = halves(polynomial)
        if total is None:
            total = polynomial + jnp.where(row == column, 3.4445, 0.0)
        else:
            total = 3.4445 * total + triple(poly_parts, halves(total))
        if step < 4:
            once = 3.4445 * gram + triple(poly_parts, gram_parts)
            gram = 3.4445 * once + triple(halves(once), poly_parts)
    direction = to_low(triple(halves(total), parts))
    for tile in range(WIDE_TILES):
        o_ref[tile] = direction[:, 128 * tile : 128 * (tile + 1)]


def wide_direction(core, own, got):
    outs = [((WIDE_TILES, WIDTH, 128), BF16)]
    return call(
        wide_direction_kernel, (core, own, got), outs, "wide_direction", 16, 1, [pltpu.VMEM((WIDTH, 128 * WIDE_TILES), F32)], limit=40
    )[0]


def wide_update_kernel(
    core_ref, own_ref, got_ref, up_ref, down_ref, up_ema_ref, down_ema_ref,
    up_new_ref, up_ema_new_ref, down_new_ref, down_ema_new_ref,
):
    def update(up_dir, down_dir):
        for tile in range(WIDE_TILES):
            lanes = slice(128 * tile, 128 * (tile + 1))
            up_new_ref[:, lanes] = up_ref[:, lanes] * SHRINK - UP_RATE * up_dir[tile].astype(F32)
        for tile in range(2 * DOWN_TILES):
            lanes = slice(128 * tile, 128 * (tile + 1))
            down_new_ref[:, lanes] = down_ref[:, lanes] * SHRINK - DOWN_RATE * down_dir[tile].astype(F32)

    def average(half):
        lanes = slice(128 * UP_TILES * half, 128 * UP_TILES * (half + 1))
        up_ema_new_ref[...] = AVERAGE * up_ema_ref[...] + (1.0 - AVERAGE) * up_new_ref[:, lanes]
        lanes = slice(128 * DOWN_TILES * half, 128 * DOWN_TILES * (half + 1))
        down_ema_new_ref[...] = AVERAGE * down_ema_ref[...] + (1.0 - AVERAGE) * down_new_ref[:, lanes]

    @pl.when(core_ref[0] == 0)
    def _():
        update(own_ref, got_ref)
        average(0)

    @pl.when(core_ref[0] != 0)
    def _():
        update(got_ref, own_ref)
        average(1)


def wide_update(core, own, got, up, down, up_ema, down_ema):
    outs = [(x.shape, F32) for x in (up, up_ema, down, down_ema)]
    return call(wide_update_kernel, (core, own, got, up, down, up_ema, down_ema), outs, "wide_update", 7, 1, limit=32)


def square_directions_kernel(
    sum_ref, moment_ref, m1_ref, m2_ref, vec_ref, vec_ema_ref,
    direction_ref, moment_new_ref, m1_new_ref, m2_new_ref, vec_new_ref, vec_ema_new_ref, loss_ref,
    matrix,
):
    side = sum_ref[tile_rows(12)][:, 64:128]
    rows = jnp.concatenate([side[16 * j : 16 * (j + 1)] for j in range(5)], axis=1)
    loss_ref[...] = rows[13:14, 0:128]
    gradient = rows[0:13]
    first = 0.9 * m1_ref[...] + 0.1 * gradient
    second = 0.999 * m2_ref[...] + 0.001 * (gradient * gradient)
    m1_new_ref[...] = first
    m2_new_ref[...] = second
    adjusted = first * (1.0 / (1.0 - 0.9**STEP)) / (jnp.sqrt(second * (1.0 / (1.0 - 0.999**STEP))) + 1e-08)
    fresh = vec_ref[...] - ADAM_RATE * (adjusted + DECAY * vec_ref[...])
    vec_new_ref[...] = fresh
    vec_ema_new_ref[...] = AVERAGE * vec_ema_ref[...] + (1.0 - AVERAGE) * fresh
    for index in range(5):
        lanes = slice(64 * (index % 2), 64 * (index % 2) + 64)
        gradient = jnp.concatenate(
            [sum_ref[tile_rows(2 * index)], sum_ref[tile_rows(2 * index + 1)], sum_ref[tile_rows(10 + index // 2)][:, lanes]],
            axis=1,
        )
        moment = 0.95 * moment_ref[index] + gradient
        moment_new_ref[index] = moment
        matrix[index] = scaled_to_unit(gradient + 0.95 * moment)

    def step(_, carry):
        current = [matrix[index] for index in range(5)]
        parts = [halves(x) for x in current]
        grams = [triple(x, x, True) for x in parts]
        gram_parts = [halves(x) for x in grams]
        polynomials = [-4.775 * gram + 2.0315 * triple(x, x) for gram, x in zip(grams, gram_parts)]
        poly_parts = [halves(x) for x in polynomials]
        for index in range(5):
            matrix[index] = 3.4445 * current[index] + triple(poly_parts[index], parts[index])
        return carry

    lax.fori_loop(0, 5, step, 0)
    direction_ref[...] = to_low(matrix[...])


def square_directions(summed, moment, m1, m2, vectors, vec_ema):
    outs = [(moment.shape, BF16), (moment.shape, F32)] + [(vectors.shape, F32)] * 4 + [((1, 128), F32)]
    operands = (summed, moment, m1, m2, vectors, vec_ema)
    return call(square_directions_kernel, operands, outs, "square_directions", 30, 0, [pltpu.VMEM(moment.shape, F32)], limit=40)


def square_update_kernel(core_ref, own_ref, got_ref, weight_ref, ema_ref, new_ref, ema_new_ref):
    def update(half, direction):
        for index in range(5):
            new_ref[5 * half + index] = weight_ref[5 * half + index] * SHRINK - SQUARE_RATE * direction[index].astype(F32)

    def average(half):
        for index in range(5):
            ema_new_ref[index] = AVERAGE * ema_ref[index] + (1.0 - AVERAGE) * new_ref[5 * half + index]

    for core in range(2):

        @pl.when(core_ref[0] == core)
        def _(core=core):
            update(core, own_ref)
            update(1 - core, got_ref)
            average(core)


def square_update(core, own, got, weights, ema):
    outs = [(x.shape, F32) for x in (weights, ema)]
    return call(square_update_kernel, (core, own, got, weights, ema), outs, "square_update", 6, 1, limit=32)


TAPS = 9
CHAN = 4


def group_ones():
    group = np.arange(WIDTH) // (WIDTH // GN_GROUPS)
    return jnp.asarray((group[:, None] == group[None, :]).astype(np.float32), BF16)


def group_mean(column_sums, ones):
    rest = jnp.broadcast_to(column_sums, (8, WIDTH))
    total = jnp.zeros((8, WIDTH), F32)
    for _ in range(3):
        part = to_low(rest)
        total = total + dot(part, ones)
        rest = rest - part.astype(F32)
    return total[0:1] * (1.0 / (PIX * (WIDTH // GN_GROUPS)))


def chunk_rows(index):
    return pl.ds(pl.multiple_of(index * CHUNK, CHUNK), CHUNK)


def over_chunks(body, *start):
    return lax.fori_loop(0, CHUNKS, lambda i, carry: body(i, *carry), start)


def zero_row():
    return jnp.zeros((1, WIDTH), F32)


def group_stats(ref, ones, column_sums):
    centre = group_mean(column_sums, ones)

    def squares(i, total):
        shifted = ref[chunk_rows(i), :] - centre
        return (total + column_sum(shifted * shifted),)

    (total,) = over_chunks(squares, zero_row())
    return centre, lax.rsqrt(group_mean(total, ones) + 1e-05)


def sigmoid(values):
    return 1.0 / (1.0 + jnp.exp(-values))


def shifted_lanes(values, down, right):
    lane = lax.broadcasted_iota(jnp.int32, values.shape, 1)
    line = lane // LATENT + down
    place = lane % LATENT + right
    inside = (line >= 0) & (line < LATENT) & (place >= 0) & (place < LATENT)
    offset = (down * LATENT + right) % PIX
    moved = pltpu.roll(values, (PIX - offset) % PIX, 1) if offset else values
    return jnp.where(inside, moved, 0.0)


def put_columns(cols_ref, act_ref):
    zeros = jnp.zeros((LATENT, 3 * WIDTH), BF16)
    cols_ref[0:LATENT, :] = zeros
    cols_ref[LATENT + PIX :, :] = zeros
    act_ref[0:8, :] = jnp.zeros((8, WIDTH), F32)
    act_ref[8 + PIX :, :] = jnp.zeros((8, WIDTH), F32)

    for i in range(CHUNKS):
        place = (lax.broadcasted_iota(jnp.int32, (CHUNK, WIDTH), 0)) % LATENT
        middle = act_ref[8 + i * CHUNK : 8 + (i + 1) * CHUNK, :]
        left = act_ref[7 + i * CHUNK : 7 + (i + 1) * CHUNK, :]
        right = act_ref[9 + i * CHUNK : 9 + (i + 1) * CHUNK, :]
        left = jnp.where(place == 0, 0.0, left)
        right = jnp.where(place == LATENT - 1, 0.0, right)
        cols_ref[LATENT + i * CHUNK : LATENT + (i + 1) * CHUNK, :] = jnp.concatenate(
            [to_low(left), to_low(middle), to_low(right)], axis=1
        )


def resnet_kernel(
    rates_ref, pair_ref, vec_ref, temb_ref, ones_ref, w_in_ref, w_res_ref, squares_ref,
    resnet_ref, tokens_ref,
    first, inner, act, cols,
):
    ones = ones_ref[...]

    def vec(i):
        return vec_ref[i : i + 1, :]

    pair = pair_ref[...].astype(F32)
    noisy = rates_ref[0] * pair + rates_ref[1] * jnp.concatenate([pair[CHAN:], pair[:CHAN]], axis=0)
    columns = tap_rows([shifted_lanes(noisy, tap // 3 - 1, tap % 3 - 1)[:CHAN] for tap in range(TAPS)])
    w_in = tap_rows([w_in_ref[tap // 3, tap % 3] for tap in range(TAPS)])
    total = zero_row()
    for i in range(CHUNKS):
        part = dot_tn(columns[:, i * CHUNK : (i + 1) * CHUNK], w_in) + vec(0)
        first[i * CHUNK : (i + 1) * CHUNK, :] = part
        total = total + column_sum(part)

    def activate(source, total, gain, offset):
        centre, scale = group_stats(source, ones, total)

        def one(i):
            normal = (source[chunk_rows(i), :] - centre) * scale * gain + offset
            act[pl.ds(pl.multiple_of(8 + i * CHUNK, 8), CHUNK), :] = normal * sigmoid(normal)
            return ()

        over_chunks(lambda i: one(i))
        put_columns(cols, act)

    def convolve_chunk(i, which):
        out = None
        for line in range(3):
            part = cols[pl.ds(pl.multiple_of(i * CHUNK + LATENT * line, LATENT), CHUNK), :]
            term = dot(part, w_res_ref[which, line])
            out = term if out is None else out + term
        return out

    activate(first, total, vec(1), vec(2))
    shift = vec(3) + temb_ref[...]

    def first_step(i, total):
        part = convolve_chunk(i, 0) + shift
        inner[chunk_rows(i), :] = part
        return (total + column_sum(part),)

    (total,) = over_chunks(first_step, zero_row())
    activate(inner, total, vec(4), vec(5))

    def second_step(i, total):
        part = first[chunk_rows(i), :] + (convolve_chunk(i, 1) + vec(6))
        resnet_ref[chunk_rows(i), :] = part
        return (total + column_sum(part),)

    (total,) = over_chunks(second_step, zero_row())
    centre, scale = group_stats(resnet_ref, ones, total)

    def token_step(i):
        normal = to_low((resnet_ref[chunk_rows(i), :] - centre) * scale * vec(7) + vec(8))
        tokens_ref[chunk_rows(i), :] = dot(normal, squares_ref[0]) + vec(9)
        return ()

    over_chunks(lambda i: token_step(i))


def resnet_block(rates, pair, vectors, temb, w_in, w_res, squares):
    operands = (rates, pair, vectors, temb, group_ones(), w_in, w_res, squares)
    scratch = [
        pltpu.VMEM((PIX, WIDTH), F32),
        pltpu.VMEM((PIX, WIDTH), F32),
        pltpu.VMEM((PIX + 16, WIDTH), F32),
        pltpu.VMEM((PIX + 2 * LATENT, 3 * WIDTH), BF16),
    ]
    return call(resnet_kernel, operands, [((PIX, WIDTH), F32)] * 2, "resnet_block", 15, 1, scratch)


def tap_rows(pieces):
    zeros = jnp.zeros((8 - CHAN, pieces[0].shape[1]), F32)
    return to_low(jnp.concatenate([x for piece in pieces for x in (piece.astype(F32), zeros)], axis=0))


def prepare_spatial_kernel(sq_ref, sel_ref, w_qkv, w_o, w_q2, w_o2):
    sel = sel_ref[...]
    for j in range(3):
        w_qkv[:, j * SLOTS : (j + 1) * SLOTS] = to_low(dot(sq_ref[1 + j], sel))
    w_q2[...] = to_low(dot(sq_ref[5], sel))
    w_o[...] = to_low(dot_tn(sel, sq_ref[4]))
    w_o2[...] = to_low(dot_tn(sel, sq_ref[6]))


def prepare_spatial(squares):
    shapes = [(WIDTH, 3 * SLOTS), (SLOTS, WIDTH), (WIDTH, SLOTS), (SLOTS, WIDTH)]
    return call(prepare_spatial_kernel, (squares, slot_selector()), [(x, BF16) for x in shapes], "spatial_weights", 3, limit=16)


LOG2E = 1.4426950408889634
TEXT_ROWS = 128


def transformer_kernel(
    tokens_ref, resnet_ref, text_ref, vec_ref, ones_ref, sel_ref, w_qkv_ref, w_o_ref, w_q2_ref, w_kv2_ref, w_o2_ref,
    w_up_ref, t_down_ref, squares_ref,
    hidden_ref, packed_ref,
    queries, keys, values, text_kv,
):
    def vec(i):
        return vec_ref[i : i + 1, :]

    lane = lax.broadcasted_iota(jnp.int32, (CHUNK, SLOTS), 1)
    counter = jnp.where(lane % SLOT == HEAD_DIM, 1.0, 0.0)

    def project(i):
        a = to_low(normal_parts(tokens_ref[chunk_rows(i), :])[0] * vec(10) + vec(11))
        qkv = dot(a, w_qkv_ref[...])
        queries[chunk_rows(i), :] = to_low(qkv[:, :SLOTS])
        keys[chunk_rows(i), :] = to_low(qkv[:, SLOTS : 2 * SLOTS])
        values[chunk_rows(i), :] = to_low(qkv[:, 2 * SLOTS :] + counter)
        return ()

    over_chunks(lambda i: project(i))
    kv = to_low(dot(text_ref[...], w_kv2_ref[...]))
    text_kv[...] = jnp.zeros_like(text_kv)
    wide_kv = jnp.concatenate(
        [dot(kv[:, :WIDTH], sel_ref[...]), dot(kv[:, WIDTH:], sel_ref[...])], axis=1
    )
    text_kv[0 : wide_kv.shape[0], :] = wide_kv
    text_lane = lax.broadcasted_iota(jnp.int32, (CHUNK, TEXT_ROWS), 1)
    text_bias = jnp.where(text_lane < TEXT_LEN, 0.0, -1e30)

    def chunk_step(i, total):
        tokens = tokens_ref[chunk_rows(i), :]
        pairs = []
        for pair in range(HEADS // 2):
            lanes = slice(pair * GROUP, (pair + 1) * GROUP)
            query = queries[chunk_rows(i), lanes]
            key = keys[:, lanes]
            value = values[:, lanes]
            side = lax.broadcasted_iota(jnp.int32, (CHUNK, GROUP), 1) < SLOT
            both = None
            for head in range(2):
                zero = jnp.zeros_like(query)
                own_query = jnp.where(side, query, zero) if head == 0 else jnp.where(side, zero, query)
                scores = dot_nt(own_query, key) * (SCALE * LOG2E)
                raised = jnp.exp2(scores - jnp.max(scores, axis=1, keepdims=True))
                mixed = dot(to_low(raised), value)
                mixed = mixed * (1.0 / mixed[:, head * SLOT + HEAD_DIM : head * SLOT + HEAD_DIM + 1])
                both = mixed if head == 0 else jnp.where(side, both, mixed)
            pairs.append(to_low(both))
        tokens = tokens + (dot(jnp.concatenate(pairs, axis=1), w_o_ref[...]) + vec(12))
        c = to_low(normal_parts(tokens)[0] * vec(13) + vec(14))
        query2 = to_low(dot(c, w_q2_ref[...]))
        pairs = []
        for pair in range(HEADS // 2):
            lanes = slice(pair * GROUP, (pair + 1) * GROUP)
            text_keys = lane_halves(to_low(text_kv[:, lanes]))
            text_values = lane_halves(to_low(text_kv[:, SLOTS + pair * GROUP : SLOTS + (pair + 1) * GROUP]))
            scores = dot_nt(query2[:, lanes], text_keys) * SCALE
            probs = []
            for part in (scores[:, :TEXT_ROWS], scores[:, TEXT_ROWS:]):
                part = part + text_bias
                raised = jnp.exp(part - jnp.max(part, axis=1, keepdims=True))
                probs.append(to_low(raised * (1.0 / jnp.sum(raised, axis=1, keepdims=True))))
            pairs.append(to_low(dot(jnp.concatenate(probs, axis=1), text_values)))
        tokens = tokens + (dot(jnp.concatenate(pairs, axis=1), w_o2_ref[...]) + vec(15))
        f = to_low(normal_parts(tokens)[0] * vec(16) + vec(17))
        gate_up = dot(f, w_up_ref[...])
        inner = to_low(gate_up[:, :FF_INNER] * gelu_parts(gate_up[:, FF_INNER:])[0])
        tokens = tokens + (dot_nt(inner, t_down_ref[...]) + vec(18))
        hidden = resnet_ref[chunk_rows(i), :] + (dot(to_low(tokens), squares_ref[7]) + vec(19))
        hidden_ref[chunk_rows(i), :] = hidden
        return (total + column_sum(hidden),)

    (total,) = over_chunks(chunk_step, zero_row())
    centre, scale = group_stats(hidden_ref, ones_ref[...], total)
    pack_rows(packed_ref, lambda rows: (hidden_ref[rows, :] - centre) * scale)


def pack_rows(packed_ref, rows_at):
    for member in range(CLIP):
        block = to_low(rows_at(slice(member * OWN, (member + 1) * OWN)))
        packed_ref[member, 0:64, :] = block[:, 0:128]
        packed_ref[member, 64:128, :] = block[:, 128:256]
        packed_ref[member, 128:160, :] = jnp.concatenate([block[0:32, 256:320], block[32:64, 256:320]], axis=1)


def transformer_block(tokens, resnet, text, vectors, prepared, cross_kv, up, down, squares):
    w_qkv, w_o, w_q2, w_o2 = prepared
    operands = (
        tokens, resnet, text, vectors, group_ones(), slot_selector(), w_qkv, w_o, w_q2, cross_kv, w_o2, up, down, squares,
    )
    scratch = [pltpu.VMEM((PIX, SLOTS), BF16)] * 3 + [pltpu.VMEM((TEXT_ROWS, 2 * SLOTS), F32)]
    outs = [((PIX, WIDTH), F32), ((CLIP, 160, 128), BF16)]
    return call(transformer_kernel, operands, outs, "transformer_block", 32, 0, scratch)


def head_kernel(
    facts_ref, hidden_ref, branch_ref, pair_ref, vec_ref, ones_ref, w_ref,
    packed_ref, loss_ref,
    mixed, act, slope,
):
    ones = ones_ref[...]
    gain = vec_ref[20:21, :]
    offset = vec_ref[21:22, :]
    column_total = zero_row()
    for member in range(CLIP):
        rows = slice(member * OWN, (member + 1) * OWN)
        last = branch_ref[member, 128:160, :]
        branch = jnp.concatenate(
            [
                branch_ref[member, 0:64, :].astype(F32),
                branch_ref[member, 64:128, :].astype(F32),
                jnp.concatenate([last[:, 0:64], last[:, 64:128]], axis=0).astype(F32),
            ],
            axis=1,
        )
        part = hidden_ref[rows, :] + branch
        mixed[rows, :] = part
        column_total = column_total + column_sum(part)
    centre, scale = group_stats(mixed, ones, column_total)

    def activate(i):
        normal = (mixed[chunk_rows(i), :] - centre) * scale
        mixed[chunk_rows(i), :] = normal
        value = normal * gain + offset
        share = sigmoid(value)
        act[chunk_rows(i), :] = to_low(value * share)
        slope[chunk_rows(i), :] = share * (1.0 + value * (1.0 - share)) * gain
        return ()

    over_chunks(lambda i: activate(i))
    weight = tap_rows([w_ref[tap // 3, tap % 3] for tap in range(TAPS)])
    by_tap = dot_nt(weight, act[...])
    predicted = jnp.zeros((8, PIX), F32)
    for tap in range(TAPS):
        predicted = predicted + shifted_lanes(by_tap[8 * tap : 8 * tap + 8], tap // 3 - 1, tap % 3 - 1)
    pair = pair_ref[...].astype(F32)
    target = facts_ref[0] * jnp.concatenate([pair[CHAN:], pair[:CHAN]], axis=0) - facts_ref[1] * pair
    target = jnp.where(lax.broadcasted_iota(jnp.int32, pair.shape, 0) < CHAN, target, 0.0)
    residual = (predicted - target) * facts_ref[2]
    loss_ref[...] = jnp.sum(residual * residual, keepdims=True)
    grad = to_low(2.0 * residual / facts_ref[3]).astype(F32)
    columns = tap_rows([shifted_lanes(grad, 1 - tap // 3, 1 - tap % 3)[:CHAN] for tap in range(TAPS)])
    total = zero_row()
    total_normal = zero_row()
    for i in range(CHUNKS):
        rows = slice(i * CHUNK, (i + 1) * CHUNK)
        part = dot_tn(columns[:, rows], weight) * slope[rows, :]
        slope[rows, :] = part
        total = total + column_sum(part)
        total_normal = total_normal + column_sum(part * mixed[rows, :])
    mean = group_mean(total, ones)
    mean_normal = group_mean(total_normal, ones)
    pack_rows(packed_ref, lambda rows: scale * (slope[rows, :] - mean - mixed[rows, :] * mean_normal))


def head_block(facts, hidden, branch, pair, vectors, weight):
    operands = (facts, hidden, branch, pair, vectors, group_ones(), weight)
    outs = [((CLIP, 160, 128), BF16), ((1, 1), F32)]
    scratch = [pltpu.VMEM((PIX, WIDTH), F32), pltpu.VMEM((PIX, WIDTH), BF16), pltpu.VMEM((PIX, WIDTH), F32)]
    return call(head_kernel, operands, outs, "head_block", 6, 1, scratch, limit=36)


def product(left, right):
    return jnp.einsum("...i,ij->...j", left, right, preferred_element_type=jnp.float32)


def time_embed(step_values, time_w1, time_w2, temb_w, temb_bias):
    half_width = WIDTH // 2
    frequency = jnp.exp(-math.log(10000.0) * jnp.arange(half_width, dtype=jnp.float32) / half_width)
    angles = step_values[..., None] * frequency
    encoding = jnp.concatenate([jnp.cos(angles), jnp.sin(angles)], axis=-1)
    hidden = product(to_low(encoding), time_w1)
    hidden = product(to_low(jax.nn.silu(hidden)), time_w2)
    return product(to_low(jax.nn.silu(hidden)), temb_w) + temb_bias


def swap_cores(values):
    return lax.ppermute(values, "dp", [(0, 1), (1, 0)])


WIRE = jnp.float16
TAIL = 16


def frame_phases():
    size = lax.axis_size("frames")
    phases = []
    shift = 0
    while (1 << shift) < size:
        group = min(4, size >> shift)
        phases.append((shift, group))
        shift += group.bit_length() - 1
    return phases


def frame_digit(shift, group):
    return (lax.axis_index("frames") >> shift) % group


def swap_frames(values, shift, distance):
    size = lax.axis_size("frames")
    return lax.ppermute(values, "frames", [(i, i ^ (distance << shift)) for i in range(size)])


def coded(values, start, rows, bound):
    part = lax.dynamic_slice_in_dim(values, start, rows + TAIL, 0)
    exponent = jnp.floor(14.0 - jnp.log2(jnp.maximum(bound, 1e-30)))
    place = lax.broadcasted_iota(jnp.int32, (rows + TAIL, 1), 0)
    return jnp.where(place < rows, part * jnp.exp2(exponent), exponent).astype(WIRE)


def exponent_of(message, rows):
    return message[rows : rows + 1].astype(F32)


def reduce_start(values, bound, shift, group):
    rows = (values.shape[0] - TAIL) // group
    mine = frame_digit(shift, group)
    return [coded(values, (mine ^ d) * rows, rows, bound) for d in range(1, group)]


def reduce_send(messages, shift):
    return [swap_frames(message, shift, d + 1) for d, message in enumerate(messages)]


def reduce_end(values, bound, got, shift, group):
    rows = (values.shape[0] - TAIL) // group
    total = lax.dynamic_slice_in_dim(values, frame_digit(shift, group) * rows, rows + TAIL, 0)
    for message in got:
        exponent = exponent_of(message, rows)
        total = total + message.astype(F32) * jnp.exp2(-exponent)
        bound = bound + jnp.exp2(15.0 - exponent)
    return total, bound


def gather_send(block, shift, group):
    return [swap_frames(block, shift, d) for d in range(1, group)]


def gather_end(block, got, shift, group):
    rows = block.shape[0]
    mine = frame_digit(shift, group)
    total = jnp.zeros((group * rows, 128), block.dtype)
    for d, part in enumerate([block] + got):
        total = lax.dynamic_update_slice_in_dim(total, part, (mine ^ d) * rows, 0)
    return total


def decoded(block, piece):
    parts = block.reshape(-1, piece, 128)
    exponent = parts[:, piece - TAIL : piece - TAIL + 1].astype(F32)
    return (parts[:, : piece - TAIL].astype(F32) * jnp.exp2(-exponent)).reshape(-1, 128)


def first_bound(values, used):
    return values[used : used + 1]


def fit_rows(values):
    unit = 8 * lax.axis_size("frames")
    rows = values.shape[0] - TAIL
    padded = -(-rows // unit) * unit
    return jnp.pad(values, ((0, padded - rows), (0, 0))) if padded > rows else values


def sample_groups():
    groups = []
    for block in range(lax.axis_size("frames") // CLIP):
        for half in range(2):
            groups.append(
                [
                    2 * (block * CLIP + half * HALF + place) + core
                    for core in range(2)
                    for place in range(HALF)
                ]
            )
    return groups


def swap_samples(values):
    size = lax.axis_size("frames")
    pairs = []
    for frame in range(size):
        half = (frame % CLIP) // HALF
        pairs.append((2 * frame + 1 - half, 2 * (frame ^ HALF) + half))
    return lax.ppermute(values, ("frames", "dp"), pairs)


def shards(
    latents,
    noise,
    timesteps,
    image_flags,
    frame_counts,
    text,
    conv_in,
    res_convs,
    conv_out,
    time_w1,
    time_w2,
    temb_w,
    spatial_squares,
    cross_kv,
    spatial_up,
    spatial_down,
    frozen_vectors,
    motion_squares,
    motion_up,
    motion_down,
    motion_vectors,
    square_moment,
    up_moment,
    down_moment,
    vector_moment1,
    vector_moment2,
    square_ema,
    up_ema,
    down_ema,
    vector_ema,
):
    dp_index = lax.axis_index("dp")
    place = lax.axis_index("frames")
    block = place // CLIP
    place = place % CLIP
    half = place // HALF
    stays = half == dp_index
    frame = jnp.where(stays, place, (place + HALF) % CLIP)
    pair = jnp.concatenate([latents.reshape(PIX, CHAN).T, noise.reshape(PIX, CHAN).T], axis=0)
    pair = jnp.where(stays, pair, swap_samples(pair))

    def of_block(values):
        return lax.dynamic_index_in_dim(values[0], block, 0, keepdims=False)

    text_rows = of_block(text)
    text_rows = jnp.where(stays, text_rows, swap_cores(text_rows))
    step_values = of_block(timesteps).astype(F32)[None]
    phases = (step_values / 1000.0 + 0.008) / 1.008 * (math.pi / 2)
    temb_res = time_embed(step_values, time_w1, time_w2, temb_w, frozen_vectors[22])
    flag = of_block(image_flags).astype(F32)[None]
    facts = jnp.concatenate([temb_res[0], jnp.cos(phases), jnp.sin(phases), 1.0 - flag, jnp.zeros((61,), F32)])
    facts = facts.reshape(1, 384)
    facts = jnp.where(stays, facts, swap_cores(facts))
    temb_res = facts[:, :WIDTH]
    rates = facts[0, WIDTH : WIDTH + 2]
    keep = facts[0, WIDTH + 2 : WIDTH + 3]
    frozen_prepared = prepare_spatial(spatial_squares)
    resnet, tokens = resnet_block(
        rates, pair, frozen_vectors, temb_res, conv_in, res_convs.reshape(2, 3, 3 * WIDTH, WIDTH), spatial_squares
    )
    hidden, packed = transformer_block(
        tokens, resnet, text_rows, frozen_vectors, frozen_prepared, cross_kv, spatial_up, spatial_down.T, spatial_squares
    )
    groups = sample_groups()

    def exchange(values):
        return lax.all_to_all(
            values, ("frames", "dp"), split_axis=0, concat_axis=0, tiled=True, axis_index_groups=groups
        )

    arrived = exchange(packed)
    count = lax.dynamic_slice(frame_counts, (half, block), (1, 1)).reshape(1)
    weights = prepare(motion_squares, motion_up, motion_down.T)
    branch, u, u2, u3, qkv1, qkv2, o1, o2, last = motion_forward(
        arrived, count, keep, weights, motion_vectors
    )
    frame_valid = (frame < count).astype(F32)
    total_count = 4.0 * PIX * jnp.sum(frame_counts).astype(F32)
    grad, loss_part = head_block(
        jnp.concatenate([rates, frame_valid, total_count[None]]),
        hidden, exchange(branch), pair, frozen_vectors, jnp.swapaxes(conv_out, 2, 3),
    )
    grad_in = exchange(grad)
    core = dp_index.reshape(1)
    du3, early, early_other, g9, feed_sums = feed_backward(
        core, grad_in, keep, weights, motion_vectors, u3, last
    )
    phases = frame_phases()
    ordered = lax.optimization_barrier

    def gather_last(block, got, piece, rows):
        parts = [decoded(part, piece) for part in [block] + got]
        return gather_end(parts[0], parts[1:], *phases[0])[:rows]

    early_got = swap_cores(early_other)
    second = second_backward(du3, count, weights, motion_vectors, u2, qkv2)
    early_got, *second = ordered((early_got, *second))
    du2, d_qkv2, second_sums = second

    early = early + early_got
    early_bound = first_bound(early, (UP_TILES + DOWN_TILES) * WIDTH)
    early = fit_rows(early)
    messages = reduce_start(early, early_bound, *phases[0])
    du2, *messages = ordered((du2, *messages))
    got = reduce_send(messages, phases[0][0])
    first = first_backward(du2, count, arrived, weights, motion_vectors, u, qkv1)
    *first, du3 = ordered((*first, du3, *got))[: len(first) + 1]
    du, d_qkv1, first_sums = first
    early, early_bound = reduce_end(early, early_bound, got, *phases[0])

    shift, group = phases[1]
    messages = reduce_start(early, early_bound, shift, group)
    du3, *messages = ordered((du3, *messages))
    got = reduce_send(messages, shift)
    later = second_grads(du3, motion_vectors, u2, d_qkv2, o2)
    *later, du2 = ordered((*later, du2, *got))[: len(later) + 1]
    early, early_bound = reduce_end(early, early_bound, got, shift, group)
    for shift, group in phases[2:]:
        got = reduce_send(reduce_start(early, early_bound, shift, group), shift)
        early, early_bound = reduce_end(early, early_bound, got, shift, group)

    early_block = coded(early, 0, early.shape[0] - TAIL, early_bound)
    early_piece = early_block.shape[0]
    for shift, group in reversed(phases[2:]):
        early_block = gather_end(early_block, gather_send(early_block, shift, group), shift, group)
    du2, early_block = ordered((du2, early_block))
    got = gather_send(early_block, *phases[1])
    late, late_other = first_grads(
        core, loss_part[0] / (1024.0 * total_count), du2, arrived, motion_vectors, u, d_qkv1, o1, du,
        (*later, g9, feed_sums, second_sums, first_sums),
    )
    late, late_other, early_block, *got = ordered((late, late_other, early_block, *got))
    early_block = gather_end(early_block, got, *phases[1])

    early_block, late_other = ordered((early_block, late_other))
    late_got = swap_cores(late_other)
    early_got = gather_send(early_block, *phases[0])
    late, late_got = ordered((late, late_got))
    late = late + late_got
    late_bound = first_bound(late, 13 * WIDTH)
    late = fit_rows(late)
    messages = reduce_start(late, late_bound, *phases[0])
    early_block, *more = ordered((early_block, *early_got, *messages))
    early_got, messages = more[: len(early_got)], more[len(early_got) :]

    got = reduce_send(messages, phases[0][0])
    early = gather_last(early_block, early_got, early_piece, EARLY_ROWS - TAIL)
    up_moment_new, down_moment_new, ahead = wide_moments(early, up_moment, down_moment.T)
    sent = lax.dynamic_slice_in_dim(ahead, (1 - dp_index) * DOWN_TILES, UP_TILES, 0)
    ahead, sent, *got = ordered((ahead, sent, *got))
    late, late_bound = reduce_end(late, late_bound, got, *phases[0])

    ahead_got = swap_cores(sent)
    for shift, group in phases[1:]:
        got = reduce_send(reduce_start(late, late_bound, shift, group), shift)
        late, late_bound = reduce_end(late, late_bound, got, shift, group)
    late_block = coded(late, 0, late.shape[0] - TAIL, late_bound)
    late_piece = late_block.shape[0]
    late_block, ahead, ahead_got = ordered((late_block, ahead, ahead_got))

    def gather_middle(block):
        for shift, group in reversed(phases[1:]):
            block = gather_end(block, gather_send(block, shift, group), shift, group)
        return block

    late_block = gather_middle(late_block)
    late_got = gather_send(late_block, *phases[0])
    wide = wide_direction(core, ahead, ahead_got)
    wide, late_block, *late_got = ordered((wide, late_block, *late_got))

    wide_got = swap_cores(wide)
    late = gather_last(late_block, late_got, late_piece, LATE_ROWS - TAIL)
    square, square_moment_new, moment_first, moment_second, vector_new, vector_ema_new, loss_row = square_directions(
        late, square_moment, vector_moment1, vector_moment2, motion_vectors, vector_ema
    )
    square, wide_got = ordered((square, wide_got))
    square_got = swap_cores(square)
    up_new, up_ema_new, down_new, down_ema_new = wide_update(
        core, wide, wide_got, motion_up, motion_down.T, up_ema, down_ema.T
    )
    square_got, up_new, up_ema_new, down_new, down_ema_new = ordered(
        (square_got, up_new, up_ema_new, down_new, down_ema_new)
    )
    square_new, square_ema_new = square_update(
        core, square, square_got, motion_squares, square_ema
    )
    return (
        loss_row[0, 0] * (1024.0 * total_count),
        total_count,
        square_new,
        square_moment_new,
        square_ema_new,
        up_new,
        up_moment_new,
        up_ema_new,
        down_new.T,
        down_moment_new.T,
        down_ema_new.T,
        moment_first,
        moment_second,
        vector_new,
        vector_ema_new,
    )


def solution(mesh):
    return jax.shard_map(
        shards,
        mesh=mesh,
        in_specs=(
            P("dp", "frames", None, None),
            P("dp", "frames", None, None),
            P("dp", None),
            P("dp", None),
            P(),
            P("dp", None, None, None),
            P(),
            P(),
            P(),
            P(),
            P(),
            P(),
            P(),
            P(),
            P(),
            P(),
            P(),
            P(),
            P(),
            P(),
            P(),
            P("dp", None, None),
            P(None, "dp"),
            P("dp", None),
            P(),
            P(),
            P("dp", None, None),
            P(None, "dp"),
            P("dp", None),
            P(),
        ),
        out_specs=(
            P(),
            P(),
            P(),
            P("dp", None, None),
            P("dp", None, None),
            P(),
            P(None, "dp"),
            P(None, "dp"),
            P(),
            P("dp", None),
            P("dp", None),
            P(),
            P(),
            P(),
            P(),
        ),
        check_vma=False,
    )
```

```python
import math

import jax
import jax.numpy as jnp
import numpy as np
from jax import lax
from jax.experimental import pallas as pl
from jax.experimental.pallas import tpu as pltpu
from jax.sharding import PartitionSpec as P

WIDTH = 320
HEADS = 8
HEAD_DIM = 40
FF_INNER = 1280
CLIP = 16
HALF = 8
PIX = 1024
LATENT = 32
TEXT_LEN = 77
TEXT_DIM = 768
GN_GROUPS = 32
F32 = jnp.float32
BF16 = jnp.bfloat16
OWN = PIX // CLIP
SLOT = 64
SLOTS = HEADS * SLOT
CHUNK = 1024
CHUNKS = PIX // CHUNK
GROUP = 128
GROUPS = PIX // GROUP
SCALE = 1.0 / math.sqrt(HEAD_DIM)


def to_low(values):
    return values.astype(BF16)


def dot(left, right):
    return lax.dot_general(left, right, (((1,), (0,)), ((), ())), preferred_element_type=F32)


def dot_nt(left, right):
    return lax.dot_general(left, right, (((1,), (1,)), ((), ())), preferred_element_type=F32)


def dot_tn(left, right):
    return lax.dot_general(left, right, (((0,), (0,)), ((), ())), preferred_element_type=F32)


def in_vmem():
    return pl.BlockSpec(memory_space=pltpu.VMEM)


COS, SIN, KEEP, COUNT, VALID, TOTAL = range(WIDTH, WIDTH + 6)


def in_smem():
    return pl.BlockSpec(memory_space=pltpu.SMEM)


def call(kernel, operands, outs, name, micros, scalars=0, scratch=(), limit=60):
    specs = [in_smem()] * scalars + [in_vmem()] * (len(operands) - scalars)
    return pl.pallas_call(
        kernel,
        in_specs=specs,
        out_specs=[in_vmem()] * len(outs),
        out_shape=[jax.ShapeDtypeStruct(shape, kind) for shape, kind in outs],
        scratch_shapes=list(scratch),
        cost_estimate=pl.CostEstimate(flops=int(micros * 1.1e9), bytes_accessed=0, transcendentals=0),
        compiler_params=pltpu.CompilerParams(vmem_limit_bytes=limit * 2**20),
        name=name,
    )(*operands)


def slot_selector():
    out = np.zeros((WIDTH, SLOTS), np.float32)
    for head in range(HEADS):
        for j in range(HEAD_DIM):
            out[head * HEAD_DIM + j, head * SLOT + j] = 1.0
    return jnp.asarray(out, BF16)


def frame_codes():
    positions = np.arange(CLIP, dtype=np.float32)[:, None]
    column = np.arange(WIDTH)
    frequency = np.exp(np.float32(-math.log(10000.0)) * (2 * (column // 2)).astype(np.float32) / WIDTH)
    angles = positions * frequency.astype(np.float32)
    codes = np.where(column % 2 == 0, np.sin(angles), np.cos(angles)).astype(np.float32)
    return jnp.asarray(np.repeat(codes, 8, axis=0))


def unpack_positions(packed_ref, wide_ref):
    wide_ref[:, :, 0:128] = packed_ref[:, 0:64, :].astype(F32)
    wide_ref[:, :, 128:256] = packed_ref[:, 64:128, :].astype(F32)
    last = packed_ref[:, 128:160, :].astype(F32)
    wide_ref[:, 0:32, 256:320] = last[:, :, 0:64]
    wide_ref[:, 32:64, 256:320] = last[:, :, 64:128]


def pack_positions(wide_ref, packed_ref):
    packed_ref[:, 0:64, :] = to_low(wide_ref[:, :, 0:128])
    packed_ref[:, 64:128, :] = to_low(wide_ref[:, :, 128:256])
    last = jnp.concatenate([wide_ref[:, 0:32, 256:320], wide_ref[:, 32:64, 256:320]], axis=2)
    packed_ref[:, 128:160, :] = to_low(last)


def tokens_of(wide_ref):
    parts = [wide_ref[:, 8 * group : 8 * group + 8, :].reshape(GROUP, WIDTH) for group in range(GROUPS)]
    return jnp.concatenate(parts, axis=0)


def put_tokens(wide_ref, tokens):
    for group in range(GROUPS):
        part = tokens[group * GROUP : (group + 1) * GROUP].reshape(CLIP, 8, WIDTH)
        wide_ref[:, 8 * group : 8 * group + 8, :] = part


def every_group(rows):
    return jnp.concatenate([rows] * GROUPS, axis=0)


def normal_parts(values):
    centre = jnp.mean(values, axis=-1, keepdims=True)
    shifted = values - centre
    scale = lax.rsqrt(jnp.mean(shifted * shifted, axis=-1, keepdims=True) + 1e-05)
    return shifted * scale, scale


def normal_back(grad, normal, scale, gain):
    inner = grad * gain
    return scale * (
        inner
        - jnp.mean(inner, axis=-1, keepdims=True)
        - normal * jnp.mean(inner * normal, axis=-1, keepdims=True)
    )


def erf_parts(gate):
    bell = jnp.exp(-0.5 * gate * gate)
    size = jnp.abs(gate) * (1.0 / math.sqrt(2.0))
    t = 1.0 / (1.0 + 0.3275911 * size)
    poly = t * (
        0.254829592
        + t * (-0.284496736 + t * (1.421413741 + t * (-1.453152027 + t * 1.061405429)))
    )
    tail = poly * bell
    return jnp.where(gate < 0.0, tail - 1.0, 1.0 - tail), bell


def gelu_parts(gate):
    erf, bell = erf_parts(gate)
    share = 0.5 + 0.5 * erf
    return gate * share, share + gate * bell * (1.0 / math.sqrt(2.0 * math.pi))


PIECE = 256
PIECES = FF_INNER // PIECE


def feed_forward(inputs, w_up_ref, down_of):
    total = None
    for piece in range(PIECES):
        units = slice(piece * PIECE, (piece + 1) * PIECE)
        gates = slice(FF_INNER + piece * PIECE, FF_INNER + (piece + 1) * PIECE)
        value = dot(inputs, w_up_ref[:, units])
        inner = to_low(value * gelu_parts(dot(inputs, w_up_ref[:, gates]))[0])
        part = down_of(inner, units)
        total = part if total is None else total + part
    return total


def lane_halves(values):
    lane = lax.broadcasted_iota(jnp.int32, values.shape, 1)
    zero = jnp.zeros_like(values)
    return jnp.concatenate(
        [jnp.where(lane < SLOT, values, zero), jnp.where(lane < SLOT, zero, values)], axis=0
    )


def key_bias(count, queries_first):
    shape = (GROUP, 2 * GROUP) if queries_first else (2 * GROUP, GROUP)
    row = lax.broadcasted_iota(jnp.int32, shape, 0)
    column = lax.broadcasted_iota(jnp.int32, shape, 1)
    key = (column if queries_first else row) % GROUP
    valid = (row % 8 == column % 8) & ((key // 8).astype(F32) < count)
    return jnp.where(valid, 0.0, -1e30).astype(F32)


def attend_chunk(qkv, bias):
    out = []
    for group in range(GROUPS):
        rows = slice(group * GROUP, (group + 1) * GROUP)
        pairs = []
        for pair in range(HEADS // 2):
            lanes = pair * 2 * SLOT
            queries = qkv[rows, lanes : lanes + GROUP]
            keys = lane_halves(qkv[rows, SLOTS + lanes : SLOTS + lanes + GROUP])
            values = lane_halves(qkv[rows, 2 * SLOTS + lanes : 2 * SLOTS + lanes + GROUP])
            scores = dot_nt(queries, keys) * SCALE + bias
            probs = []
            for part in (scores[:, :GROUP], scores[:, GROUP:]):
                raised = jnp.exp(part - jnp.max(part, axis=1, keepdims=True))
                probs.append(raised * (1.0 / jnp.sum(raised, axis=1, keepdims=True)))
            pairs.append(to_low(dot(to_low(jnp.concatenate(probs, axis=1)), values)))
        out.append(jnp.concatenate(pairs, axis=1))
    return jnp.concatenate(out, axis=0)


def motion_forward_kernel(
    facts_ref, arrived_ref, codes_ref, vec_ref, w_in_ref, w_qkv_ref, w_o_ref, w_up_ref, w_down_ref, w_out_ref,
    branch_ref, u_ref, u2_ref, u3_ref, qkv1_ref, qkv2_ref, o1_ref, o2_ref, last_ref,
    wide,
):
    def vec(i):
        return vec_ref[i : i + 1, :]

    unpack_positions(arrived_ref, wide)
    bias = key_bias(facts_ref[0, COUNT], True)
    codes = every_group(codes_ref[...])
    inputs = to_low(tokens_of(wide) * vec(0) + vec(1))
    stream = dot(inputs, w_in_ref[...]) + vec(2)
    for index, (first, x_ref, qkv_ref, o_ref) in enumerate(
        ((3, u_ref, qkv1_ref, o1_ref), (6, u2_ref, qkv2_ref, o2_ref))
    ):
        x_ref[...] = stream
        a = to_low(normal_parts(stream)[0] * vec(first) + vec(first + 1) + codes)
        qkv = to_low(dot(a, w_qkv_ref[index]))
        qkv_ref[...] = qkv
        mixture = attend_chunk(qkv, bias)
        o_ref[...] = mixture
        stream = stream + (dot(mixture, w_o_ref[index]) + vec(first + 2))
    u3_ref[...] = stream
    c = to_low(normal_parts(stream)[0] * vec(9) + vec(10))
    fed = feed_forward(c, w_up_ref, lambda inner, units: dot(inner, w_down_ref[units, :]))
    last = to_low(stream + (fed + vec(11)))
    last_ref[...] = last
    put_tokens(wide, (dot(last, w_out_ref[...]) + vec(12)) * facts_ref[0, KEEP])
    pack_positions(wide, branch_ref)


def motion_forward(facts, arrived, weights, vectors):
    outs = [((CLIP, 160, 128), BF16)] + [((PIX, WIDTH), F32)] * 3 + [((PIX, 3 * SLOTS), BF16)] * 2
    outs = outs + [((PIX, SLOTS), BF16)] * 2 + [((PIX, WIDTH), BF16)]
    operands = (facts, arrived, frame_codes(), vectors) + tuple(
        weights[name] for name in ("in", "qkv", "o", "up", "down", "out")
    )
    return call(
        motion_forward_kernel, operands, outs, "motion_forward", 23, 1, [pltpu.VMEM((CLIP, OWN, WIDTH), F32)]
    )


def prepare_kernel(sq_ref, up_ref, down_ref, sel_ref, w_in, w_qkv, w_o, w_up, w_down, w_out, t_in, t_qkv, t_o, t_up, t_down, t_out):
    sel = sel_ref[...]
    low = [to_low(sq_ref[i]) for i in range(10)]
    w_in[...] = low[0]
    t_in[...] = low[0].T
    w_out[...] = low[9]
    t_out[...] = low[9].T
    for index, first in enumerate((1, 5)):
        for j in range(3):
            padded = to_low(dot(low[first + j], sel))
            w_qkv[index, :, j * SLOTS : (j + 1) * SLOTS] = padded
            t_qkv[index, j * SLOTS : (j + 1) * SLOTS, :] = padded.T
        padded = to_low(dot_nt(low[first + 3].T, sel.T))
        t_o[index] = padded
        w_o[index] = padded.T
    up = to_low(up_ref[...])
    w_up[...] = up
    t_up[...] = up.T
    down = to_low(down_ref[...])
    t_down[...] = down
    w_down[...] = down.T


def prepare(squares, up, down):
    shapes = {
        "in": (WIDTH, WIDTH), "qkv": (2, WIDTH, 3 * SLOTS), "o": (2, SLOTS, WIDTH), "up": (WIDTH, 2 * FF_INNER),
        "down": (FF_INNER, WIDTH), "out": (WIDTH, WIDTH),
        "in_t": (WIDTH, WIDTH), "qkv_t": (2, 3 * SLOTS, WIDTH), "o_t": (2, WIDTH, SLOTS), "up_t": (2 * FF_INNER, WIDTH),
        "down_t": (WIDTH, FF_INNER), "out_t": (WIDTH, WIDTH),
    }
    made = call(
        prepare_kernel, (squares, up, down, slot_selector()), [(x, BF16) for x in shapes.values()], "motion_weights", 9
    )
    return dict(zip(shapes, made))


def column_sum(values):
    return jnp.sum(values, axis=0, keepdims=True)


def feed_backward_kernel(
    core_ref, facts_ref, grad_ref, u3_ref, last_ref, vec_ref, w_up_ref, t_up_ref, t_down_ref, t_out_ref,
    du3_ref, own_ref, other_ref, g_out_ref, g_vec_ref,
    wide,
):
    gain = vec_ref[9:10, :]
    unpack_positions(grad_ref, wide)
    dbranch = to_low(tokens_of(wide) * facts_ref[0, KEEP])
    g_out_ref[...] = dot_tn(last_ref[...], dbranch)
    du4 = dot(dbranch, t_out_ref[...])
    d4 = to_low(du4)
    normal, scale = normal_parts(u3_ref[...])
    c = to_low(normal * gain + vec_ref[10:11, :])
    z = dot(c, w_up_ref[...])
    value = z[:, :FF_INNER]
    gelu, slope = gelu_parts(z[:, FF_INNER:])
    inner = to_low(value * gelu)
    dinner = dot(d4, t_down_ref[...])
    dz = to_low(jnp.concatenate([dinner * gelu, dinner * value * slope], axis=1))
    g_down = dot_tn(d4, inner)
    g_up = dot_tn(c, dz)
    bound = jnp.maximum(jnp.max(jnp.abs(g_up)), jnp.max(jnp.abs(g_down)))

    def put(ref, half):
        for tile in range(UP_TILES):
            start = half * FF_INNER + tile * 128
            ref[tile_rows(tile)] = g_up[:, start : start + 128]
        for tile in range(DOWN_TILES):
            start = half * (FF_INNER // 2) + tile * 128
            ref[tile_rows(UP_TILES + tile)] = g_down[:, start : start + 128]
        used = (UP_TILES + DOWN_TILES) * WIDTH
        ref[used:] = jnp.full((EARLY_ROWS - used, 128), bound)

    for core in range(2):

        @pl.when(core_ref[0] == core)
        def _(core=core):
            put(own_ref, core)
            put(other_ref, 1 - core)

    dc = dot(dz, t_up_ref[...])
    du3_ref[...] = du4 + normal_back(dc, normal, scale, gain)
    rows = [column_sum(dc * normal), column_sum(dc), column_sum(d4.astype(F32)), column_sum(dbranch.astype(F32))]
    g_vec_ref[...] = jnp.concatenate(rows + [jnp.zeros((4, WIDTH), F32)], axis=0)


def feed_backward(core, facts, grad, weights, vectors, u3, last):
    operands = (core, facts, grad, u3, last, vectors) + tuple(weights[n] for n in ("up", "up_t", "down_t", "out_t"))
    outs = [(PIX, WIDTH), (EARLY_ROWS, 128), (EARLY_ROWS, 128), (WIDTH, WIDTH), (8, WIDTH)]
    return call(
        feed_backward_kernel, operands, [(x, F32) for x in outs], "feed_backward", 18, 2,
        [pltpu.VMEM((CLIP, OWN, WIDTH), F32)],
    )


def attend_back_chunk(qkv, d_mixture, bias):
    out = []
    for group in range(GROUPS):
        rows = slice(group * GROUP, (group + 1) * GROUP)
        grads = [[], [], []]
        for pair in range(HEADS // 2):
            lanes = pair * 2 * SLOT
            queries = qkv[rows, lanes : lanes + GROUP]
            keys = lane_halves(qkv[rows, SLOTS + lanes : SLOTS + lanes + GROUP])
            values = lane_halves(qkv[rows, 2 * SLOTS + lanes : 2 * SLOTS + lanes + GROUP])
            d_out = d_mixture[rows, lanes : lanes + GROUP]
            scores = dot_nt(keys, queries) * SCALE + bias
            d_probs = dot_nt(values, d_out)
            low_probs = []
            d_scores = []
            for head in range(2):
                part = scores[head * GROUP : (head + 1) * GROUP]
                d_part = d_probs[head * GROUP : (head + 1) * GROUP]
                raised = jnp.exp(part - jnp.max(part, axis=0, keepdims=True))
                probs = raised * (1.0 / jnp.sum(raised, axis=0, keepdims=True))
                low_probs.append(to_low(probs))
                d_scores.append(to_low(probs * (d_part - jnp.sum(probs * d_part, axis=0, keepdims=True))))
            low_probs = jnp.concatenate(low_probs, axis=0)
            d_scores = jnp.concatenate(d_scores, axis=0)
            d_values = dot(low_probs, d_out)
            d_keys = dot(d_scores, queries) * SCALE
            d_queries = dot_tn(d_scores, keys) * SCALE
            lane = lax.broadcasted_iota(jnp.int32, (GROUP, GROUP), 1)
            grads[0].append(to_low(d_queries))
            grads[1].append(to_low(jnp.where(lane < SLOT, d_keys[:GROUP], d_keys[GROUP:])))
            grads[2].append(to_low(jnp.where(lane < SLOT, d_values[:GROUP], d_values[GROUP:])))
        out.append(jnp.concatenate(grads[0] + grads[1] + grads[2], axis=1))
    return jnp.concatenate(out, axis=0)


def attention_backward(count, grad, stream, qkv, gain, t_o, t_qkv):
    d_out = to_low(grad)
    d_mixture = to_low(dot(d_out, t_o))
    d_qkv = attend_back_chunk(qkv, d_mixture, key_bias(count, False))
    normal, scale = normal_parts(stream)
    d_a = dot(d_qkv, t_qkv)
    rows = [column_sum(d_a * normal), column_sum(d_a), column_sum(d_out.astype(F32))]
    return grad + normal_back(d_a, normal, scale, gain), d_qkv, rows


def second_backward_kernel(
    facts_ref, grad_ref, u2_ref, qkv_ref, vec_ref, t_o_ref, t_qkv_ref,
    du2_ref, d_qkv_ref, g_vec_ref,
):
    du2, d_qkv, rows = attention_backward(
        facts_ref[0, COUNT], grad_ref[...], u2_ref[...], qkv_ref[...], vec_ref[6:7, :], t_o_ref[1], t_qkv_ref[1]
    )
    du2_ref[...] = du2
    d_qkv_ref[...] = d_qkv
    g_vec_ref[...] = jnp.concatenate(rows + [jnp.zeros((5, WIDTH), F32)], axis=0)


def second_backward(grad, facts, weights, vectors, u2, qkv):
    operands = (facts, grad, u2, qkv, vectors, weights["o_t"], weights["qkv_t"])
    outs = [((PIX, WIDTH), F32), ((PIX, 3 * SLOTS), BF16), ((8, WIDTH), F32)]
    return call(second_backward_kernel, operands, outs, "second_backward", 15, 1, limit=36)


def first_backward_kernel(
    facts_ref, grad_ref, u_ref, qkv_ref, arrived_ref, vec_ref, t_o_ref, t_qkv_ref, t_in_ref,
    du_ref, d_qkv_ref, g_vec_ref,
    wide,
):
    unpack_positions(arrived_ref, wide)
    du, d_qkv, rows = attention_backward(
        facts_ref[0, COUNT], grad_ref[...], u_ref[...], qkv_ref[...], vec_ref[3:4, :], t_o_ref[0], t_qkv_ref[0]
    )
    du = to_low(du)
    du_ref[...] = du
    d_qkv_ref[...] = d_qkv
    d_inputs = dot(du, t_in_ref[...])
    top = [column_sum(d_inputs * tokens_of(wide)), column_sum(d_inputs), column_sum(du.astype(F32))]
    g_vec_ref[...] = jnp.concatenate(top + rows + [jnp.zeros((2, WIDTH), F32)], axis=0)


def first_backward(grad, facts, arrived, weights, vectors, u, qkv):
    operands = (facts, grad, u, qkv, arrived, vectors, weights["o_t"], weights["qkv_t"], weights["in_t"])
    outs = [((PIX, WIDTH), BF16), ((PIX, 3 * SLOTS), BF16), ((8, WIDTH), F32)]
    return call(
        first_backward_kernel, operands, outs, "first_backward", 17, 1, [pltpu.VMEM((CLIP, OWN, WIDTH), F32)], limit=36
    )


def attention_grads(grad, stream, d_qkv, mixture, codes, gain, offset, sel_t):
    padded = dot_tn(mixture, to_low(grad))
    w_o_grad = jnp.concatenate([padded[head * SLOT : head * SLOT + HEAD_DIM] for head in range(HEADS)], axis=0)
    a = to_low(normal_parts(stream)[0] * gain + offset + every_group(codes))
    grads = []
    for j in range(3):
        tight = to_low(dot(d_qkv[:, j * SLOTS : (j + 1) * SLOTS], sel_t))
        grads.append(dot_tn(a, tight))
    return grads + [w_o_grad]


def second_grads_kernel(grad_ref, u2_ref, d_qkv_ref, o_ref, codes_ref, vec_ref, sel_t_ref, gq_ref, gk_ref, gv_ref, go_ref):
    grads = attention_grads(
        grad_ref[...], u2_ref[...], d_qkv_ref[...], o_ref[...], codes_ref[...], vec_ref[6:7, :], vec_ref[7:8, :], sel_t_ref[...]
    )
    for ref, value in zip((gq_ref, gk_ref, gv_ref, go_ref), grads):
        ref[...] = value


def second_grads(grad, vectors, u2, d_qkv, mixture):
    operands = (grad, u2, d_qkv, mixture, frame_codes(), vectors, slot_selector().T)
    return call(second_grads_kernel, operands, [((WIDTH, WIDTH), F32)] * 4, "second_grads", 7, limit=36)


def first_grads_kernel(
    core_ref, facts_ref, loss_ref, grad_ref, u_ref, d_qkv_ref, o_ref, du_ref, arrived_ref, codes_ref, vec_ref, sel_t_ref,
    g5_ref, g6_ref, g7_ref, g8_ref, g9_ref, feed_vec_ref, second_vec_ref, first_vec_ref,
    own_ref, other_ref,
    wide,
):
    unpack_positions(arrived_ref, wide)
    grads = attention_grads(
        grad_ref[...], u_ref[...], d_qkv_ref[...], o_ref[...], codes_ref[...], vec_ref[3:4, :], vec_ref[4:5, :], sel_t_ref[...]
    )
    inputs = to_low(tokens_of(wide) * vec_ref[0:1, :] + vec_ref[1:2, :])
    later = [ref[...] for ref in (g5_ref, g6_ref, g7_ref, g8_ref, g9_ref)]
    squares = [dot_tn(inputs, du_ref[...])] + grads + later
    vector_rows = jnp.concatenate(
        [first_vec_ref[0:6, :], second_vec_ref[0:3, :], feed_vec_ref[0:4, :], jnp.full((3, WIDTH), loss_ref[0, 0] / (1024.0 * facts_ref[0, TOTAL]))], axis=0
    )
    bound = jnp.max(jnp.abs(vector_rows))
    for square in squares:
        bound = jnp.maximum(bound, jnp.max(jnp.abs(square)))
    pieces = [vector_rows[:, 64 * j : 64 * (j + 1)] for j in range(5)]
    side = jnp.concatenate(pieces + [jnp.zeros((WIDTH - 80, 64), F32)], axis=0)

    def put(ref, half):
        own = squares[5 * half : 5 * half + 5]
        for index in range(5):
            ref[tile_rows(2 * index)] = own[index][:, 0:128]
            ref[tile_rows(2 * index + 1)] = own[index][:, 128:256]
        for pair in range(2):
            ref[tile_rows(10 + pair)] = jnp.concatenate([own[2 * pair][:, 256:320], own[2 * pair + 1][:, 256:320]], axis=1)
        ref[tile_rows(12)] = jnp.concatenate([own[4][:, 256:320], side], axis=1)
        ref[13 * WIDTH :] = jnp.full((LATE_ROWS - 13 * WIDTH, 128), bound)

    for core in range(2):

        @pl.when(core_ref[0] == core)
        def _(core=core):
            put(own_ref, core)
            put(other_ref, 1 - core)


def first_grads(core, facts, loss_part, grad, arrived, vectors, u, d_qkv, mixture, du, later):
    operands = (
        core, facts, loss_part, grad, u, d_qkv, mixture, du, arrived, frame_codes(), vectors, slot_selector().T,
    ) + tuple(later)
    outs = [((LATE_ROWS, 128), F32)] * 2
    return call(first_grads_kernel, operands, outs, "first_grads", 10, 3, [pltpu.VMEM((CLIP, OWN, WIDTH), F32)], limit=44)


MUON_RATE = 0.2
ADAM_RATE = 0.4
DECAY = 0.01
AVERAGE = 0.75
STEP = 10
SHRINK = 1.0 - MUON_RATE * DECAY
SQUARE_RATE = MUON_RATE * 0.2 * math.sqrt(WIDTH)
UP_RATE = MUON_RATE * 0.2 * math.sqrt(2 * FF_INNER)
DOWN_RATE = MUON_RATE * 0.2 * math.sqrt(FF_INNER)
UP_TILES = 10
DOWN_TILES = 5
WIDE_TILES = 2 * UP_TILES
EARLY_ROWS = 4864 + 16
LATE_ROWS = 4224 + 16


def tile_rows(index):
    return slice(index * WIDTH, (index + 1) * WIDTH)


def halves(values):
    high = values.astype(BF16)
    return (high, (values - high.astype(F32)).astype(BF16))


def triple(left, right):
    stacked = jnp.concatenate([left[0], left[0], left[1]], axis=1)
    return dot(stacked, jnp.concatenate([right[0], right[1], right[0]], axis=0))


def gram_of(parts):
    high, low = parts
    half = dot_nt(jnp.concatenate([high, high], axis=1), jnp.concatenate([high * 0.5, low], axis=1))
    return half + half.T


def scaled_to_unit(matrix):
    return matrix * (1.0 / (jnp.sqrt(jnp.sum(matrix * matrix, keepdims=True)) + 1e-07))


def wide_moments_kernel(sum_ref, up_ref, down_ref, up_new_ref, down_new_ref, ahead_ref):
    for tile in range(UP_TILES):
        lanes = slice(128 * tile, 128 * (tile + 1))
        gradient = sum_ref[tile_rows(tile)]
        moment = 0.95 * up_ref[:, lanes] + gradient
        up_new_ref[:, lanes] = moment
        ahead_ref[tile] = gradient + 0.95 * moment
    for tile in range(DOWN_TILES):
        lanes = slice(128 * tile, 128 * (tile + 1))
        gradient = sum_ref[tile_rows(UP_TILES + tile)]
        moment = 0.95 * down_ref[:, lanes] + gradient
        down_new_ref[:, lanes] = moment
        ahead_ref[UP_TILES + tile] = gradient + 0.95 * moment


def wide_moments(summed, up_moment, down_moment):
    outs = [up_moment.shape, down_moment.shape, (UP_TILES + DOWN_TILES, WIDTH, 128)]
    return call(
        wide_moments_kernel, (summed, up_moment, down_moment), [(x, F32) for x in outs], "wide_moments", 4, limit=32
    )


def wide_direction_kernel(core_ref, own_ref, got_ref, o_ref, matrix):
    def put(tile, value):
        matrix[:, 128 * tile : 128 * (tile + 1)] = value

    @pl.when(core_ref[0] == 0)
    def _():
        for tile in range(UP_TILES):
            put(tile, own_ref[tile])
            put(UP_TILES + tile, got_ref[tile])

    @pl.when(core_ref[0] != 0)
    def _():
        for tile in range(DOWN_TILES):
            put(tile, got_ref[UP_TILES - DOWN_TILES + tile])
            put(DOWN_TILES + tile, own_ref[UP_TILES + tile])
        matrix[:, 128 * UP_TILES :] = jnp.zeros((WIDTH, 128 * UP_TILES), F32)

    parts = halves(scaled_to_unit(matrix[...]))
    gram = gram_of(parts)
    row = lax.broadcasted_iota(jnp.int32, (WIDTH, WIDTH), 0)
    column = lax.broadcasted_iota(jnp.int32, (WIDTH, WIDTH), 1)
    total = None
    for step in range(5):
        gram_parts = halves(gram)
        polynomial = -4.775 * gram + 2.0315 * gram_of(gram_parts)
        poly_parts = halves(polynomial)
        if total is None:
            total = polynomial + jnp.where(row == column, 3.4445, 0.0)
        else:
            total = 3.4445 * total + triple(poly_parts, halves(total))
        if step < 4:
            once = 3.4445 * gram + triple(poly_parts, gram_parts)
            gram = 3.4445 * once + triple(halves(once), poly_parts)
    direction = to_low(triple(halves(total), parts))
    for tile in range(WIDE_TILES):
        o_ref[tile] = direction[:, 128 * tile : 128 * (tile + 1)]


def wide_direction(core, own, got):
    outs = [((WIDE_TILES, WIDTH, 128), BF16)]
    return call(
        wide_direction_kernel, (core, own, got), outs, "wide_direction", 16, 1, [pltpu.VMEM((WIDTH, 128 * WIDE_TILES), F32)], limit=40
    )[0]


class Inward:
    def __init__(self, source, target, semaphore):
        self.copy = pltpu.make_async_copy(source, target, semaphore)
        self.target = target
        self.state = 0

    def begin(self):
        self.copy.start()
        self.state = 1

    def ready(self):
        if self.state == 1:
            self.copy.wait()
            self.state = 2
        return self.target

    def __getitem__(self, index):
        return self.ready()[index]


def anywhere():
    return pl.BlockSpec(memory_space=pl.ANY)


def squares_step(current, passes):
    def symmetric(values, count):
        if count == 1:
            low = [to_low(x) for x in values]
            return [dot_nt(x, x) for x in low]
        return [gram_of(halves(x)) for x in values]

    grams = symmetric(current, passes[0])
    squared = symmetric(grams, passes[1])
    polynomials = [-4.775 * gram + 2.0315 * square for gram, square in zip(grams, squared)]
    if passes[2] == 1:
        moved = [dot(to_low(p), to_low(x)) for p, x in zip(polynomials, current)]
    else:
        moved = [triple(halves(p), halves(x)) for p, x in zip(polynomials, current)]
    return [3.4445 * x + y for x, y in zip(current, moved)]


DIRECTION_OUTS = 11


def directions_kernel(core_ref, sums, *refs):
    count = 11
    sources, refs = refs[:count], refs[count:]
    targets, refs = refs[:DIRECTION_OUTS], refs[DIRECTION_OUTS:]
    inner, refs = refs[:count], refs[count:]
    outer, refs = refs[:DIRECTION_OUTS], refs[DIRECTION_OUTS:]
    coming, going, matrix = refs
    inputs = [Inward(x, y, coming.at[i]) for i, (x, y) in enumerate(zip(sources, inner))]
    moment_ref, m1_ref, m2_ref, vec_ref, vec_ema_ref = inputs[:5]
    own_ref, got_ref, up_ref, down_ref, up_ema_ref, down_ema_ref = inputs[5:]
    leaving = [pltpu.make_async_copy(x, y, going.at[i]) for i, (x, y) in enumerate(zip(outer, targets))]
    (
        direction_ref, moment_new_ref, m1_new_ref, m2_new_ref, vec_new_ref, vec_ema_new_ref, loss_ref,
        up_new_ref, up_ema_new_ref, down_new_ref, down_ema_new_ref,
    ) = outer
    for value in inputs[:5]:
        value.begin()
    for value in inputs[:5]:
        value.ready()
    for value in inputs[5:]:
        value.begin()

    side = sums[tile_rows(12)][:, 64:128]
    rows = jnp.concatenate([side[16 * j : 16 * (j + 1)] for j in range(5)], axis=1)
    loss_ref[...] = rows[13:14, 0:128]
    gradient = rows[0:13]
    first = 0.9 * m1_ref[...] + 0.1 * gradient
    second = 0.999 * m2_ref[...] + 0.001 * (gradient * gradient)
    m1_new_ref[...] = first
    m2_new_ref[...] = second
    adjusted = first * (1.0 / (1.0 - 0.9**STEP)) / (jnp.sqrt(second * (1.0 / (1.0 - 0.999**STEP))) + 1e-08)
    fresh = vec_ref[...] - ADAM_RATE * (adjusted + DECAY * vec_ref[...])
    vec_new_ref[...] = fresh
    vec_ema_new_ref[...] = AVERAGE * vec_ema_ref[...] + (1.0 - AVERAGE) * fresh
    for index in range(5):
        lanes = slice(64 * (index % 2), 64 * (index % 2) + 64)
        gradient = jnp.concatenate(
            [sums[tile_rows(2 * index)], sums[tile_rows(2 * index + 1)], sums[tile_rows(10 + index // 2)][:, lanes]], axis=1
        )
        moment = 0.95 * moment_ref[index] + gradient
        moment_new_ref[index] = moment
        matrix[index] = scaled_to_unit(gradient + 0.95 * moment)
    for copy in leaving[1:7]:
        copy.start()

    def advance(passes):
        moved = squares_step([matrix[index] for index in range(5)], passes)
        for index in range(5):
            matrix[index] = moved[index]

    advance((1, 1, 1))
    advance((1, 1, 1))
    for value in inputs[5:]:
        value.ready()

    def update(up_dir, down_dir):
        for tile in range(WIDE_TILES):
            lanes = slice(128 * tile, 128 * (tile + 1))
            up_new_ref[:, lanes] = up_ref[:, lanes] * SHRINK - UP_RATE * up_dir[tile].astype(F32)
        for tile in range(2 * DOWN_TILES):
            lanes = slice(128 * tile, 128 * (tile + 1))
            down_new_ref[:, lanes] = down_ref[:, lanes] * SHRINK - DOWN_RATE * down_dir[tile].astype(F32)

    def average(half):
        lanes = slice(128 * UP_TILES * half, 128 * UP_TILES * (half + 1))
        up_ema_new_ref[...] = AVERAGE * up_ema_ref[...] + (1.0 - AVERAGE) * up_new_ref[:, lanes]
        lanes = slice(128 * DOWN_TILES * half, 128 * DOWN_TILES * (half + 1))
        down_ema_new_ref[...] = AVERAGE * down_ema_ref[...] + (1.0 - AVERAGE) * down_new_ref[:, lanes]

    @pl.when(core_ref[0] == 0)
    def _():
        update(own_ref, got_ref)
        average(0)

    @pl.when(core_ref[0] != 0)
    def _():
        update(got_ref, own_ref)
        average(1)

    for copy in leaving[7:]:
        copy.start()
    advance((3, 1, 3))
    advance((3, 3, 3))
    advance((3, 3, 3))
    direction_ref[...] = to_low(matrix[...])
    leaving[0].start()
    for copy in leaving:
        copy.wait()


def directions(core, summed, moment, m1, m2, vectors, vec_ema, own, got, up, down, up_ema, down_ema):
    operands = (moment, m1, m2, vectors, vec_ema, own, got, up, down, up_ema, down_ema)
    outs = [(moment.shape, BF16), (moment.shape, F32)] + [(vectors.shape, F32)] * 4 + [((1, 128), F32)]
    outs = outs + [(x.shape, F32) for x in (up, up_ema, down, down_ema)]
    return pl.pallas_call(
        directions_kernel,
        in_specs=[in_smem(), in_vmem()] + [anywhere()] * len(operands),
        out_specs=[anywhere()] * len(outs),
        out_shape=[jax.ShapeDtypeStruct(*out) for out in outs],
        scratch_shapes=[pltpu.VMEM(x.shape, x.dtype) for x in operands]
        + [pltpu.VMEM(*out) for out in outs]
        + [pltpu.SemaphoreType.DMA((len(operands),)), pltpu.SemaphoreType.DMA((len(outs),))]
        + [pltpu.VMEM(moment.shape, F32)],
        cost_estimate=pl.CostEstimate(flops=int(22 * 1.1e9), bytes_accessed=0, transcendentals=0),
        compiler_params=pltpu.CompilerParams(vmem_limit_bytes=46 * 2**20),
        name="directions",
    )(core, summed, *operands)


def own_squares_kernel(core_ref, own_ref, weight_ref, ema_ref, new_ref, ema_new_ref, own, weight, ema, new, ema_new, coming, going):
    core = core_ref[0]
    arrivals = []
    for j in range(5):
        pairs = ((weight_ref.at[core, j], weight.at[j]), (own_ref.at[j], own.at[j]), (ema_ref.at[j], ema.at[j]))
        arrivals.append([pltpu.make_async_copy(x, y, coming.at[i, j]) for i, (x, y) in enumerate(pairs)])
    for copies in arrivals:
        for copy in copies:
            copy.start()
    leaving = []
    for j in range(5):
        for copy in arrivals[j]:
            copy.wait()
        fresh = weight[j] * SHRINK - SQUARE_RATE * own[j].astype(F32)
        new[j] = fresh
        ema_new[j] = AVERAGE * ema[j] + (1.0 - AVERAGE) * fresh
        for i, (x, y) in enumerate(((new.at[j], new_ref.at[core, j]), (ema_new.at[j], ema_new_ref.at[j]))):
            leaving.append(pltpu.make_async_copy(x, y, going.at[i, j]))
            leaving[-1].start()
    for copy in leaving:
        copy.wait()


def own_squares(core, own, weights, ema):
    square = (5, WIDTH, WIDTH)
    return pl.pallas_call(
        own_squares_kernel,
        in_specs=[in_smem()] + [anywhere()] * 3,
        out_specs=[anywhere()] * 2,
        out_shape=[jax.ShapeDtypeStruct((2,) + square, F32), jax.ShapeDtypeStruct(square, F32)],
        scratch_shapes=[pltpu.VMEM(square, BF16)]
        + [pltpu.VMEM(square, F32)] * 4
        + [pltpu.SemaphoreType.DMA((3, 5)), pltpu.SemaphoreType.DMA((2, 5))],
        cost_estimate=pl.CostEstimate(flops=int(4 * 1.1e9), bytes_accessed=0, transcendentals=0),
        compiler_params=pltpu.CompilerParams(vmem_limit_bytes=60 * 2**20),
        name="own_squares",
    )(core, own, weights, ema)


def other_squares_kernel(core_ref, got_ref, weight_ref, begun_ref, new_ref, got, weight, new, coming, going):
    other = 1 - core_ref[0]
    arrivals = []
    for j in range(5):
        pairs = ((weight_ref.at[other, j], weight.at[j]), (got_ref.at[j], got.at[j]))
        arrivals.append([pltpu.make_async_copy(x, y, coming.at[i, j]) for i, (x, y) in enumerate(pairs)])
    for copies in arrivals:
        for copy in copies:
            copy.start()
    leaving = []
    for j in range(5):
        for copy in arrivals[j]:
            copy.wait()
        new[j] = weight[j] * SHRINK - SQUARE_RATE * got[j].astype(F32)
        leaving.append(pltpu.make_async_copy(new.at[j], new_ref.at[other, j], going.at[j]))
        leaving[-1].start()
    for copy in leaving:
        copy.wait()


def other_squares(core, got, weights, begun):
    square = (5, WIDTH, WIDTH)
    return pl.pallas_call(
        other_squares_kernel,
        in_specs=[in_smem()] + [anywhere()] * 3,
        out_specs=anywhere(),
        out_shape=jax.ShapeDtypeStruct(begun.shape, F32),
        input_output_aliases={3: 0},
        scratch_shapes=[pltpu.VMEM(square, BF16)]
        + [pltpu.VMEM(square, F32)] * 2
        + [pltpu.SemaphoreType.DMA((2, 5)), pltpu.SemaphoreType.DMA((5,))],
        cost_estimate=pl.CostEstimate(flops=int(3 * 1.1e9), bytes_accessed=0, transcendentals=0),
        compiler_params=pltpu.CompilerParams(vmem_limit_bytes=60 * 2**20),
        name="other_squares",
    )(core, got, weights, begun)


TAPS = 9
CHAN = 4


def group_ones():
    group = np.arange(WIDTH) // (WIDTH // GN_GROUPS)
    return jnp.asarray((group[:, None] == group[None, :]).astype(np.float32), BF16)


def group_mean(column_sums, ones):
    rest = jnp.broadcast_to(column_sums, (8, WIDTH))
    total = jnp.zeros((8, WIDTH), F32)
    for _ in range(3):
        part = to_low(rest)
        total = total + dot(part, ones)
        rest = rest - part.astype(F32)
    return total[0:1] * (1.0 / (PIX * (WIDTH // GN_GROUPS)))


def chunk_rows(index):
    return pl.ds(pl.multiple_of(index * CHUNK, CHUNK), CHUNK)


def over_chunks(body, *start):
    return lax.fori_loop(0, CHUNKS, lambda i, carry: body(i, *carry), start)


def zero_row():
    return jnp.zeros((1, WIDTH), F32)


def group_stats(ref, ones, column_sums):
    centre = group_mean(column_sums, ones)

    def squares(i, total):
        shifted = ref[chunk_rows(i), :] - centre
        return (total + column_sum(shifted * shifted),)

    (total,) = over_chunks(squares, zero_row())
    return centre, lax.rsqrt(group_mean(total, ones) + 1e-05)


def sigmoid(values):
    return 1.0 / (1.0 + jnp.exp(-values))


def shifted_lanes(values, down, right):
    lane = lax.broadcasted_iota(jnp.int32, values.shape, 1)
    line = lane // LATENT + down
    place = lane % LATENT + right
    inside = (line >= 0) & (line < LATENT) & (place >= 0) & (place < LATENT)
    offset = (down * LATENT + right) % PIX
    moved = pltpu.roll(values, (PIX - offset) % PIX, 1) if offset else values
    return jnp.where(inside, moved, 0.0)


def put_columns(cols_ref, act_ref):
    zeros = jnp.zeros((LATENT, 3 * WIDTH), BF16)
    cols_ref[0:LATENT, :] = zeros
    cols_ref[LATENT + PIX :, :] = zeros
    act_ref[0:8, :] = jnp.zeros((8, WIDTH), F32)
    act_ref[8 + PIX :, :] = jnp.zeros((8, WIDTH), F32)

    for i in range(CHUNKS):
        place = (lax.broadcasted_iota(jnp.int32, (CHUNK, WIDTH), 0)) % LATENT
        middle = act_ref[8 + i * CHUNK : 8 + (i + 1) * CHUNK, :]
        left = act_ref[7 + i * CHUNK : 7 + (i + 1) * CHUNK, :]
        right = act_ref[9 + i * CHUNK : 9 + (i + 1) * CHUNK, :]
        left = jnp.where(place == 0, 0.0, left)
        right = jnp.where(place == LATENT - 1, 0.0, right)
        cols_ref[LATENT + i * CHUNK : LATENT + (i + 1) * CHUNK, :] = jnp.concatenate(
            [to_low(left), to_low(middle), to_low(right)], axis=1
        )


def resnet_kernel(
    facts_ref, pair_ref, vec_ref, temb_ref, ones_ref, w_in_ref, w_res_ref, squares_ref,
    resnet_ref, tokens_ref,
    first, inner, act, cols,
):
    ones = ones_ref[...]

    def vec(i):
        return vec_ref[i : i + 1, :]

    pair = pair_ref[...].astype(F32)
    noisy = facts_ref[0, COS] * pair + facts_ref[0, SIN] * jnp.concatenate([pair[CHAN:], pair[:CHAN]], axis=0)
    columns = tap_rows([shifted_lanes(noisy, tap // 3 - 1, tap % 3 - 1)[:CHAN] for tap in range(TAPS)])
    w_in = tap_rows([w_in_ref[tap // 3, tap % 3] for tap in range(TAPS)])
    total = zero_row()
    for i in range(CHUNKS):
        part = dot_tn(columns[:, i * CHUNK : (i + 1) * CHUNK], w_in) + vec(0)
        first[i * CHUNK : (i + 1) * CHUNK, :] = part
        total = total + column_sum(part)

    def activate(source, total, gain, offset):
        centre, scale = group_stats(source, ones, total)

        def one(i):
            normal = (source[chunk_rows(i), :] - centre) * scale * gain + offset
            act[pl.ds(pl.multiple_of(8 + i * CHUNK, 8), CHUNK), :] = normal * sigmoid(normal)
            return ()

        over_chunks(lambda i: one(i))
        put_columns(cols, act)

    def convolve_chunk(i, which):
        out = None
        for line in range(3):
            part = cols[pl.ds(pl.multiple_of(i * CHUNK + LATENT * line, LATENT), CHUNK), :]
            term = dot(part, w_res_ref[which, line])
            out = term if out is None else out + term
        return out

    activate(first, total, vec(1), vec(2))
    shift = vec(3) + temb_ref[:, :WIDTH]

    def first_step(i, total):
        part = convolve_chunk(i, 0) + shift
        inner[chunk_rows(i), :] = part
        return (total + column_sum(part),)

    (total,) = over_chunks(first_step, zero_row())
    activate(inner, total, vec(4), vec(5))

    def second_step(i, total):
        part = first[chunk_rows(i), :] + (convolve_chunk(i, 1) + vec(6))
        resnet_ref[chunk_rows(i), :] = part
        return (total + column_sum(part),)

    (total,) = over_chunks(second_step, zero_row())
    centre, scale = group_stats(resnet_ref, ones, total)

    def token_step(i):
        normal = to_low((resnet_ref[chunk_rows(i), :] - centre) * scale * vec(7) + vec(8))
        tokens_ref[chunk_rows(i), :] = dot(normal, squares_ref[0]) + vec(9)
        return ()

    over_chunks(lambda i: token_step(i))


def resnet_block(facts, pair, vectors, w_in, w_res, squares):
    operands = (facts, pair, vectors, facts, group_ones(), w_in, w_res, squares)
    scratch = [
        pltpu.VMEM((PIX, WIDTH), F32),
        pltpu.VMEM((PIX, WIDTH), F32),
        pltpu.VMEM((PIX + 16, WIDTH), F32),
        pltpu.VMEM((PIX + 2 * LATENT, 3 * WIDTH), BF16),
    ]
    return call(resnet_kernel, operands, [((PIX, WIDTH), F32)] * 2, "resnet_block", 15, 1, scratch)


def tap_rows(pieces):
    zeros = jnp.zeros((8 - CHAN, pieces[0].shape[1]), F32)
    return to_low(jnp.concatenate([x for piece in pieces for x in (piece.astype(F32), zeros)], axis=0))


LOG2E = 1.4426950408889634
TEXT_ROWS = 128


def transformer_kernel(
    tokens_ref, resnet_ref, text_ref, vec_ref, ones_ref, sel_ref, w_kv2_ref,
    w_up_ref, t_down_ref, squares_ref,
    hidden_ref, packed_ref,
    queries, keys, values, text_kv, w_qkv_ref, w_q2_ref, w_o_ref, w_o2_ref,
):
    def vec(i):
        return vec_ref[i : i + 1, :]

    sel = sel_ref[...]
    for j in range(3):
        w_qkv_ref[:, j * SLOTS : (j + 1) * SLOTS] = to_low(dot(squares_ref[1 + j], sel))
    w_q2 = to_low(dot(squares_ref[5], sel))
    w_o = to_low(dot_tn(sel, squares_ref[4]))
    w_o2 = to_low(dot_tn(sel, squares_ref[6]))
    w_q2_ref[...] = w_q2
    w_o_ref[...] = w_o
    w_o2_ref[...] = w_o2
    lane = lax.broadcasted_iota(jnp.int32, (CHUNK, SLOTS), 1)
    counter = jnp.where(lane % SLOT == HEAD_DIM, 1.0, 0.0)

    def project(i):
        a = to_low(normal_parts(tokens_ref[chunk_rows(i), :])[0] * vec(10) + vec(11))
        qkv = dot(a, w_qkv_ref[...])
        queries[chunk_rows(i), :] = to_low(qkv[:, :SLOTS])
        keys[chunk_rows(i), :] = to_low(qkv[:, SLOTS : 2 * SLOTS])
        values[chunk_rows(i), :] = to_low(qkv[:, 2 * SLOTS :] + counter)
        return ()

    over_chunks(lambda i: project(i))
    kv = to_low(dot(text_ref[...], w_kv2_ref[...]))
    text_kv[...] = jnp.zeros_like(text_kv)
    wide_kv = jnp.concatenate(
        [dot(kv[:, :WIDTH], sel_ref[...]), dot(kv[:, WIDTH:], sel_ref[...])], axis=1
    )
    text_kv[0 : wide_kv.shape[0], :] = wide_kv
    text_lane = lax.broadcasted_iota(jnp.int32, (CHUNK, TEXT_ROWS), 1)
    text_bias = jnp.where(text_lane < TEXT_LEN, 0.0, -1e30)

    def chunk_step(i, total):
        tokens = tokens_ref[chunk_rows(i), :]
        pairs = []
        for pair in range(HEADS // 2):
            lanes = slice(pair * GROUP, (pair + 1) * GROUP)
            query = queries[chunk_rows(i), lanes]
            key = keys[:, lanes]
            value = values[:, lanes]
            side = lax.broadcasted_iota(jnp.int32, (CHUNK, GROUP), 1) < SLOT
            both = None
            for head in range(2):
                zero = jnp.zeros_like(query)
                own_query = jnp.where(side, query, zero) if head == 0 else jnp.where(side, zero, query)
                scores = dot_nt(own_query, key) * (SCALE * LOG2E)
                raised = jnp.exp2(scores - jnp.max(scores, axis=1, keepdims=True))
                mixed = dot(to_low(raised), value)
                mixed = mixed * (1.0 / mixed[:, head * SLOT + HEAD_DIM : head * SLOT + HEAD_DIM + 1])
                both = mixed if head == 0 else jnp.where(side, both, mixed)
            pairs.append(to_low(both))
        tokens = tokens + (dot(jnp.concatenate(pairs, axis=1), w_o_ref[...]) + vec(12))
        c = to_low(normal_parts(tokens)[0] * vec(13) + vec(14))
        query2 = to_low(dot(c, w_q2_ref[...]))
        pairs = []
        for pair in range(HEADS // 2):
            lanes = slice(pair * GROUP, (pair + 1) * GROUP)
            text_keys = lane_halves(to_low(text_kv[:, lanes]))
            text_values = lane_halves(to_low(text_kv[:, SLOTS + pair * GROUP : SLOTS + (pair + 1) * GROUP]))
            scores = dot_nt(query2[:, lanes], text_keys) * SCALE
            probs = []
            for part in (scores[:, :TEXT_ROWS], scores[:, TEXT_ROWS:]):
                part = part + text_bias
                raised = jnp.exp(part - jnp.max(part, axis=1, keepdims=True))
                probs.append(to_low(raised * (1.0 / jnp.sum(raised, axis=1, keepdims=True))))
            pairs.append(to_low(dot(jnp.concatenate(probs, axis=1), text_values)))
        tokens = tokens + (dot(jnp.concatenate(pairs, axis=1), w_o2_ref[...]) + vec(15))
        f = to_low(normal_parts(tokens)[0] * vec(16) + vec(17))
        fed = feed_forward(f, w_up_ref, lambda inner, units: dot_nt(inner, t_down_ref[:, units]))
        tokens = tokens + (fed + vec(18))
        hidden = resnet_ref[chunk_rows(i), :] + (dot(to_low(tokens), squares_ref[7]) + vec(19))
        hidden_ref[chunk_rows(i), :] = hidden
        return (total + column_sum(hidden),)

    (total,) = over_chunks(chunk_step, zero_row())
    centre, scale = group_stats(hidden_ref, ones_ref[...], total)
    pack_rows(packed_ref, lambda rows: (hidden_ref[rows, :] - centre) * scale)


def pack_rows(packed_ref, rows_at):
    for member in range(CLIP):
        block = to_low(rows_at(slice(member * OWN, (member + 1) * OWN)))
        packed_ref[member, 0:64, :] = block[:, 0:128]
        packed_ref[member, 64:128, :] = block[:, 128:256]
        packed_ref[member, 128:160, :] = jnp.concatenate([block[0:32, 256:320], block[32:64, 256:320]], axis=1)


def transformer_block(tokens, resnet, text, vectors, cross_kv, up, down, squares):
    operands = (
        tokens, resnet, text, vectors, group_ones(), slot_selector(), cross_kv, up, down, squares,
    )
    scratch = [pltpu.VMEM((PIX, SLOTS), BF16)] * 3 + [pltpu.VMEM((TEXT_ROWS, 2 * SLOTS), F32)]
    scratch += [pltpu.VMEM((WIDTH, 3 * SLOTS), BF16), pltpu.VMEM((WIDTH, SLOTS), BF16)] + [pltpu.VMEM((SLOTS, WIDTH), BF16)] * 2
    outs = [((PIX, WIDTH), F32), ((CLIP, 160, 128), BF16)]
    return call(transformer_kernel, operands, outs, "transformer_block", 32, 0, scratch)


def head_kernel(
    facts_ref, hidden_ref, branch_ref, pair_ref, vec_ref, ones_ref, w_ref,
    packed_ref, loss_ref,
    mixed, act, slope,
):
    ones = ones_ref[...]
    gain = vec_ref[20:21, :]
    offset = vec_ref[21:22, :]
    column_total = zero_row()
    for member in range(CLIP):
        rows = slice(member * OWN, (member + 1) * OWN)
        last = branch_ref[member, 128:160, :]
        branch = jnp.concatenate(
            [
                branch_ref[member, 0:64, :].astype(F32),
                branch_ref[member, 64:128, :].astype(F32),
                jnp.concatenate([last[:, 0:64], last[:, 64:128]], axis=0).astype(F32),
            ],
            axis=1,
        )
        part = hidden_ref[rows, :] + branch
        mixed[rows, :] = part
        column_total = column_total + column_sum(part)
    centre, scale = group_stats(mixed, ones, column_total)

    def activate(i):
        normal = (mixed[chunk_rows(i), :] - centre) * scale
        mixed[chunk_rows(i), :] = normal
        value = normal * gain + offset
        share = sigmoid(value)
        act[chunk_rows(i), :] = to_low(value * share)
        slope[chunk_rows(i), :] = share * (1.0 + value * (1.0 - share)) * gain
        return ()

    over_chunks(lambda i: activate(i))
    weight = tap_rows([w_ref[tap // 3, tap % 3] for tap in range(TAPS)])
    by_tap = dot_nt(weight, act[...])
    predicted = jnp.zeros((8, PIX), F32)
    for tap in range(TAPS):
        predicted = predicted + shifted_lanes(by_tap[8 * tap : 8 * tap + 8], tap // 3 - 1, tap % 3 - 1)
    pair = pair_ref[...].astype(F32)
    target = facts_ref[0, COS] * jnp.concatenate([pair[CHAN:], pair[:CHAN]], axis=0) - facts_ref[0, SIN] * pair
    target = jnp.where(lax.broadcasted_iota(jnp.int32, pair.shape, 0) < CHAN, target, 0.0)
    residual = (predicted - target) * facts_ref[0, VALID]
    loss_ref[...] = jnp.sum(residual * residual, keepdims=True)
    grad = to_low(2.0 * residual / facts_ref[0, TOTAL]).astype(F32)
    columns = tap_rows([shifted_lanes(grad, 1 - tap // 3, 1 - tap % 3)[:CHAN] for tap in range(TAPS)])
    total = zero_row()
    total_normal = zero_row()
    for i in range(CHUNKS):
        rows = slice(i * CHUNK, (i + 1) * CHUNK)
        part = dot_tn(columns[:, rows], weight) * slope[rows, :]
        slope[rows, :] = part
        total = total + column_sum(part)
        total_normal = total_normal + column_sum(part * mixed[rows, :])
    mean = group_mean(total, ones)
    mean_normal = group_mean(total_normal, ones)
    pack_rows(packed_ref, lambda rows: scale * (slope[rows, :] - mean - mixed[rows, :] * mean_normal))


def head_block(facts, hidden, branch, pair, vectors, weight):
    operands = (facts, hidden, branch, pair, vectors, group_ones(), weight)
    outs = [((CLIP, 160, 128), BF16), ((1, 1), F32)]
    scratch = [pltpu.VMEM((PIX, WIDTH), F32), pltpu.VMEM((PIX, WIDTH), BF16), pltpu.VMEM((PIX, WIDTH), F32)]
    return call(head_kernel, operands, outs, "head_block", 6, 1, scratch, limit=36)


def product(left, right):
    return jnp.einsum("...i,ij->...j", left, right, preferred_element_type=jnp.float32)


def time_embed(step_values, time_w1, time_w2, temb_w, temb_bias):
    half_width = WIDTH // 2
    frequency = jnp.exp(-math.log(10000.0) * jnp.arange(half_width, dtype=jnp.float32) / half_width)
    angles = step_values[..., None] * frequency
    encoding = jnp.concatenate([jnp.cos(angles), jnp.sin(angles)], axis=-1)
    hidden = product(to_low(encoding), time_w1)
    hidden = product(to_low(jax.nn.silu(hidden)), time_w2)
    return product(to_low(jax.nn.silu(hidden)), temb_w) + temb_bias


def swap_cores(values):
    return lax.ppermute(values, "dp", [(0, 1), (1, 0)])


WIRE = jnp.float16
TAIL = 16


def frame_phases():
    size = lax.axis_size("frames")
    phases = []
    shift = 0
    while (1 << shift) < size:
        group = min(4, size >> shift)
        phases.append((shift, group))
        shift += group.bit_length() - 1
    return phases


def frame_digit(shift, group):
    return (lax.axis_index("frames") >> shift) % group


def swap_frames(values, shift, distance):
    size = lax.axis_size("frames")
    return lax.ppermute(values, "frames", [(i, i ^ (distance << shift)) for i in range(size)])


def coded(values, start, rows, bound):
    part = lax.dynamic_slice_in_dim(values, start, rows + TAIL, 0)
    exponent = jnp.floor(14.0 - jnp.log2(jnp.maximum(bound, 1e-30)))
    place = lax.broadcasted_iota(jnp.int32, (rows + TAIL, 1), 0)
    return jnp.where(place < rows, part * jnp.exp2(exponent), exponent).astype(WIRE)


def exponent_of(message, rows):
    return message[rows : rows + 1].astype(F32)


def reduce_start(values, bound, shift, group):
    rows = (values.shape[0] - TAIL) // group
    mine = frame_digit(shift, group)
    return [coded(values, (mine ^ d) * rows, rows, bound) for d in range(1, group)]


def reduce_send(messages, shift):
    return [swap_frames(message, shift, d + 1) for d, message in enumerate(messages)]


def reduce_end(values, bound, got, shift, group):
    rows = (values.shape[0] - TAIL) // group
    total = lax.dynamic_slice_in_dim(values, frame_digit(shift, group) * rows, rows + TAIL, 0)
    for message in got:
        exponent = exponent_of(message, rows)
        total = total + message.astype(F32) * jnp.exp2(-exponent)
        bound = bound + jnp.exp2(15.0 - exponent)
    return total, bound


def gather_send(block, shift, group):
    return [swap_frames(block, shift, d) for d in range(1, group)]


def gather_end(block, got, shift, group):
    rows = block.shape[0]
    mine = frame_digit(shift, group)
    total = jnp.zeros((group * rows, 128), block.dtype)
    for d, part in enumerate([block] + got):
        total = lax.dynamic_update_slice_in_dim(total, part, (mine ^ d) * rows, 0)
    return total


def decoded(block, piece):
    parts = block.reshape(-1, piece, 128)
    exponent = parts[:, piece - TAIL : piece - TAIL + 1].astype(F32)
    return (parts[:, : piece - TAIL].astype(F32) * jnp.exp2(-exponent)).reshape(-1, 128)


def first_bound(values, used):
    return values[used : used + 1]


def fit_rows(values):
    unit = 8 * lax.axis_size("frames")
    rows = values.shape[0] - TAIL
    padded = -(-rows // unit) * unit
    return jnp.pad(values, ((0, padded - rows), (0, 0))) if padded > rows else values


def sample_groups():
    groups = []
    for block in range(lax.axis_size("frames") // CLIP):
        for half in range(2):
            groups.append(
                [
                    2 * (block * CLIP + half * HALF + place) + core
                    for core in range(2)
                    for place in range(HALF)
                ]
            )
    return groups


def swap_samples(values):
    size = lax.axis_size("frames")
    pairs = []
    for frame in range(size):
        half = (frame % CLIP) // HALF
        pairs.append((2 * frame + 1 - half, 2 * (frame ^ HALF) + half))
    return lax.ppermute(values, ("frames", "dp"), pairs)


def shards(
    latents,
    noise,
    timesteps,
    image_flags,
    frame_counts,
    text,
    conv_in,
    res_convs,
    conv_out,
    time_w1,
    time_w2,
    temb_w,
    spatial_squares,
    cross_kv,
    spatial_up,
    spatial_down,
    frozen_vectors,
    motion_squares,
    motion_up,
    motion_down,
    motion_vectors,
    square_moment,
    up_moment,
    down_moment,
    vector_moment1,
    vector_moment2,
    square_ema,
    up_ema,
    down_ema,
    vector_ema,
):
    dp_index = lax.axis_index("dp")
    place = lax.axis_index("frames")
    block = place // CLIP
    place = place % CLIP
    half = place // HALF
    stays = half == dp_index
    frame = jnp.where(stays, place, (place + HALF) % CLIP)
    pair = jnp.concatenate([latents.reshape(PIX, CHAN).T, noise.reshape(PIX, CHAN).T], axis=0)
    pair = jnp.where(stays, pair, swap_samples(pair))

    def of_block(values):
        return lax.dynamic_index_in_dim(values[0], block, 0, keepdims=False)

    text_rows = of_block(text)
    text_rows = jnp.where(stays, text_rows, swap_cores(text_rows))
    step_values = of_block(timesteps).astype(F32)[None]
    phases = (step_values / 1000.0 + 0.008) / 1.008 * (math.pi / 2)
    temb_res = time_embed(step_values, time_w1, time_w2, temb_w, frozen_vectors[22])
    flag = of_block(image_flags).astype(F32)[None]
    facts = jnp.concatenate([temb_res[0], jnp.cos(phases), jnp.sin(phases), 1.0 - flag, jnp.zeros((61,), F32)])
    facts = facts.reshape(1, 384)
    facts = jnp.where(stays, facts, swap_cores(facts))
    count = lax.dynamic_slice(frame_counts, (half, block), (1, 1)).reshape(1).astype(F32)
    total_count = 4.0 * PIX * jnp.sum(frame_counts).astype(F32)
    valid = (frame.astype(F32) < count).astype(F32)
    more = jnp.concatenate([jnp.zeros((COUNT,), F32), count, valid, total_count[None], jnp.zeros((383 - TOTAL,), F32)])
    facts = facts + more.reshape(1, 384)
    resnet, tokens = resnet_block(
        facts, pair, frozen_vectors, conv_in, res_convs.reshape(2, 3, 3 * WIDTH, WIDTH), spatial_squares
    )
    hidden, packed = transformer_block(
        tokens, resnet, text_rows, frozen_vectors, cross_kv, spatial_up, spatial_down.T, spatial_squares
    )
    groups = sample_groups()

    def exchange(values):
        return lax.all_to_all(
            values, ("frames", "dp"), split_axis=0, concat_axis=0, tiled=True, axis_index_groups=groups
        )

    arrived = exchange(packed)
    weights = prepare(motion_squares, motion_up, motion_down.T)
    branch, u, u2, u3, qkv1, qkv2, o1, o2, last = motion_forward(
        facts, arrived, weights, motion_vectors
    )
    grad, loss_part = head_block(
        facts, hidden, exchange(branch), pair, frozen_vectors, jnp.swapaxes(conv_out, 2, 3),
    )
    grad_in = exchange(grad)
    core = dp_index.reshape(1)
    du3, early, early_other, g9, feed_sums = feed_backward(
        core, facts, grad_in, weights, motion_vectors, u3, last
    )
    phases = frame_phases()
    ordered = lax.optimization_barrier

    def gather_last(block, got, piece, rows):
        parts = [decoded(part, piece) for part in [block] + got]
        return gather_end(parts[0], parts[1:], *phases[0])[:rows]

    early_got = swap_cores(early_other)
    second = second_backward(du3, facts, weights, motion_vectors, u2, qkv2)
    early_got, *second = ordered((early_got, *second))
    du2, d_qkv2, second_sums = second

    early = early + early_got
    early_bound = first_bound(early, (UP_TILES + DOWN_TILES) * WIDTH)
    early = fit_rows(early)
    messages = reduce_start(early, early_bound, *phases[0])
    du2, *messages = ordered((du2, *messages))
    got = reduce_send(messages, phases[0][0])
    first = first_backward(du2, facts, arrived, weights, motion_vectors, u, qkv1)
    *first, du3 = ordered((*first, du3, *got))[: len(first) + 1]
    du, d_qkv1, first_sums = first
    early, early_bound = reduce_end(early, early_bound, got, *phases[0])

    shift, group = phases[1]
    messages = reduce_start(early, early_bound, shift, group)
    du3, *messages = ordered((du3, *messages))
    got = reduce_send(messages, shift)
    later = second_grads(du3, motion_vectors, u2, d_qkv2, o2)
    *later, du2 = ordered((*later, du2, *got))[: len(later) + 1]
    early, early_bound = reduce_end(early, early_bound, got, shift, group)
    for shift, group in phases[2:]:
        got = reduce_send(reduce_start(early, early_bound, shift, group), shift)
        early, early_bound = reduce_end(early, early_bound, got, shift, group)

    early_block = coded(early, 0, early.shape[0] - TAIL, early_bound)
    early_piece = early_block.shape[0]
    for shift, group in reversed(phases[2:]):
        early_block = gather_end(early_block, gather_send(early_block, shift, group), shift, group)
    du2, early_block = ordered((du2, early_block))
    got = gather_send(early_block, *phases[1])
    late, late_other = first_grads(
        core, facts, loss_part, du2, arrived, motion_vectors, u, d_qkv1, o1, du,
        (*later, g9, feed_sums, second_sums, first_sums),
    )
    late, late_other, early_block, *got = ordered((late, late_other, early_block, *got))
    early_block = gather_end(early_block, got, *phases[1])

    early_block, late_other = ordered((early_block, late_other))
    late_got = swap_cores(late_other)
    early_got = gather_send(early_block, *phases[0])
    late = late + late_got
    late_bound = first_bound(late, 13 * WIDTH)
    late = fit_rows(late)
    got = reduce_send(reduce_start(late, late_bound, *phases[0]), phases[0][0])
    early_block, *more = ordered((early_block, *early_got, *got))
    early_got, got = more[: len(early_got)], more[len(early_got) :]
    late, late_bound = reduce_end(late, late_bound, got, *phases[0])
    messages = reduce_start(late, late_bound, *phases[1])
    early_block, *messages = ordered((early_block, *messages))
    got = reduce_send(messages, phases[1][0])
    early = gather_last(early_block, early_got, early_piece, EARLY_ROWS - TAIL)
    up_moment_new, down_moment_new, ahead = wide_moments(early, up_moment, down_moment.T)
    sent = lax.dynamic_slice_in_dim(ahead, (1 - dp_index) * DOWN_TILES, UP_TILES, 0)
    sent, *got = ordered((sent, *got))
    late, late_bound = reduce_end(late, late_bound, got, *phases[1])
    ahead_got = swap_cores(sent)
    for shift, group in phases[2:]:
        got = reduce_send(reduce_start(late, late_bound, shift, group), shift)
        late, late_bound = reduce_end(late, late_bound, got, shift, group)
    late_block = coded(late, 0, late.shape[0] - TAIL, late_bound)
    late_piece = late_block.shape[0]
    for shift, group in reversed(phases[1:]):
        late_block = gather_end(late_block, gather_send(late_block, shift, group), shift, group)
    late_block, ahead_got = ordered((late_block, ahead_got))
    late_got = gather_send(late_block, *phases[0])
    wide = wide_direction(core, ahead, ahead_got)
    wide, late_block, *late_got = ordered((wide, late_block, *late_got))

    wide_got = swap_cores(wide)
    late = gather_last(late_block, late_got, late_piece, LATE_ROWS - TAIL)
    (
        square, square_moment_new, moment_first, moment_second, vector_new, vector_ema_new, loss_row,
        up_new, up_ema_new, down_new, down_ema_new,
    ) = directions(
        core, late, square_moment, vector_moment1, vector_moment2, motion_vectors, vector_ema,
        wide, wide_got, motion_up, motion_down.T, up_ema, down_ema.T,
    )
    square_got = swap_cores(square)
    halved = motion_squares.reshape(2, 5, WIDTH, WIDTH)
    square_new, square_ema_new = own_squares(core, square, halved, square_ema)
    square_new = other_squares(core, square_got, halved, square_new).reshape(motion_squares.shape)
    return (
        loss_row[0, 0] * (1024.0 * total_count),
        total_count,
        square_new,
        square_moment_new,
        square_ema_new,
        up_new,
        up_moment_new,
        up_ema_new,
        down_new.T,
        down_moment_new.T,
        down_ema_new.T,
        moment_first,
        moment_second,
        vector_new,
        vector_ema_new,
    )


def solution(mesh):
    return jax.shard_map(
        shards,
        mesh=mesh,
        in_specs=(
            P("dp", "frames", None, None),
            P("dp", "frames", None, None),
            P("dp", None),
            P("dp", None),
            P(),
            P("dp", None, None, None),
            P(),
            P(),
            P(),
            P(),
            P(),
            P(),
            P(),
            P(),
            P(),
            P(),
            P(),
            P(),
            P(),
            P(),
            P(),
            P("dp", None, None),
            P(None, "dp"),
            P("dp", None),
            P(),
            P(),
            P("dp", None, None),
            P(None, "dp"),
            P("dp", None),
            P(),
        ),
        out_specs=(
            P(),
            P(),
            P(),
            P("dp", None, None),
            P("dp", None, None),
            P(),
            P(None, "dp"),
            P(None, "dp"),
            P(),
            P("dp", None),
            P("dp", None),
            P(),
            P(),
            P(),
            P(),
        ),
        check_vma=False,
    )
```

```python
import functools
import math

import jax
import jax.numpy as jnp
import numpy as np
from jax import lax
from jax.experimental import pallas as pl
from jax.experimental.pallas import tpu as pltpu
from jax.sharding import PartitionSpec as P

WIDTH = 320
HEADS = 8
HEAD_DIM = 40
FF_INNER = 1280
CLIP = 16
HALF = 8
PIX = 1024
LATENT = 32
TEXT_LEN = 77
TEXT_DIM = 768
GN_GROUPS = 32
F32 = jnp.float32
BF16 = jnp.bfloat16
OWN = PIX // CLIP
SLOT = 64
SLOTS = HEADS * SLOT
CHUNK = 1024
CHUNKS = PIX // CHUNK
GROUP = 128
GROUPS = PIX // GROUP
SCALE = 1.0 / math.sqrt(HEAD_DIM)


def to_low(values):
    return values.astype(BF16)


def dot(left, right):
    return lax.dot_general(left, right, (((1,), (0,)), ((), ())), preferred_element_type=F32)


def dot_nt(left, right):
    return lax.dot_general(left, right, (((1,), (1,)), ((), ())), preferred_element_type=F32)


def dot_tn(left, right):
    return lax.dot_general(left, right, (((0,), (0,)), ((), ())), preferred_element_type=F32)


def in_vmem():
    return pl.BlockSpec(memory_space=pltpu.VMEM)


COS, SIN, KEEP, COUNT, VALID, TOTAL = range(WIDTH, WIDTH + 6)


def in_smem():
    return pl.BlockSpec(memory_space=pltpu.SMEM)


def call(kernel, operands, outs, name, micros, scalars=0, scratch=(), limit=60):
    specs = [in_smem()] * scalars + [in_vmem()] * (len(operands) - scalars)
    return pl.pallas_call(
        kernel,
        in_specs=specs,
        out_specs=[in_vmem()] * len(outs),
        out_shape=[jax.ShapeDtypeStruct(shape, kind) for shape, kind in outs],
        scratch_shapes=list(scratch),
        cost_estimate=pl.CostEstimate(flops=int(micros * 1.1e9), bytes_accessed=0, transcendentals=0),
        compiler_params=pltpu.CompilerParams(vmem_limit_bytes=limit * 2**20),
        name=name,
    )(*operands)


def slot_selector():
    out = np.zeros((WIDTH, SLOTS), np.float32)
    for head in range(HEADS):
        for j in range(HEAD_DIM):
            out[head * HEAD_DIM + j, head * SLOT + j] = 1.0
    return jnp.asarray(out, BF16)


def frame_codes():
    positions = np.arange(CLIP, dtype=np.float32)[:, None]
    column = np.arange(WIDTH)
    frequency = np.exp(np.float32(-math.log(10000.0)) * (2 * (column // 2)).astype(np.float32) / WIDTH)
    angles = positions * frequency.astype(np.float32)
    codes = np.where(column % 2 == 0, np.sin(angles), np.cos(angles)).astype(np.float32)
    return jnp.asarray(np.repeat(codes, 8, axis=0))


def unpack_positions(packed_ref, wide_ref):
    wide_ref[:, :, 0:128] = packed_ref[:, 0:64, :].astype(F32)
    wide_ref[:, :, 128:256] = packed_ref[:, 64:128, :].astype(F32)
    last = packed_ref[:, 128:160, :].astype(F32)
    wide_ref[:, 0:32, 256:320] = last[:, :, 0:64]
    wide_ref[:, 32:64, 256:320] = last[:, :, 64:128]


def pack_positions(wide_ref, packed_ref):
    packed_ref[:, 0:64, :] = to_low(wide_ref[:, :, 0:128])
    packed_ref[:, 64:128, :] = to_low(wide_ref[:, :, 128:256])
    last = jnp.concatenate([wide_ref[:, 0:32, 256:320], wide_ref[:, 32:64, 256:320]], axis=2)
    packed_ref[:, 128:160, :] = to_low(last)


def tokens_of(wide_ref):
    parts = [wide_ref[:, 8 * group : 8 * group + 8, :].reshape(GROUP, WIDTH) for group in range(GROUPS)]
    return jnp.concatenate(parts, axis=0)


def put_tokens(wide_ref, tokens):
    for group in range(GROUPS):
        part = tokens[group * GROUP : (group + 1) * GROUP].reshape(CLIP, 8, WIDTH)
        wide_ref[:, 8 * group : 8 * group + 8, :] = part


def every_group(rows):
    return jnp.concatenate([rows] * GROUPS, axis=0)


def normal_parts(values):
    centre = jnp.mean(values, axis=-1, keepdims=True)
    shifted = values - centre
    scale = lax.rsqrt(jnp.mean(shifted * shifted, axis=-1, keepdims=True) + 1e-05)
    return shifted * scale, scale


def normal_back(grad, normal, scale, gain):
    inner = grad * gain
    return scale * (
        inner
        - jnp.mean(inner, axis=-1, keepdims=True)
        - normal * jnp.mean(inner * normal, axis=-1, keepdims=True)
    )


def erf_parts(gate):
    bell = jnp.exp(-0.5 * gate * gate)
    size = jnp.abs(gate) * (1.0 / math.sqrt(2.0))
    t = 1.0 / (1.0 + 0.3275911 * size)
    poly = t * (
        0.254829592
        + t * (-0.284496736 + t * (1.421413741 + t * (-1.453152027 + t * 1.061405429)))
    )
    tail = poly * bell
    return jnp.where(gate < 0.0, tail - 1.0, 1.0 - tail), bell


def gelu_parts(gate):
    erf, bell = erf_parts(gate)
    share = 0.5 + 0.5 * erf
    return gate * share, share + gate * bell * (1.0 / math.sqrt(2.0 * math.pi))


PIECE = 256
PIECES = FF_INNER // PIECE


def feed_forward(inputs, w_up_ref, down_of):
    total = None
    for piece in range(PIECES):
        units = slice(piece * PIECE, (piece + 1) * PIECE)
        gates = slice(FF_INNER + piece * PIECE, FF_INNER + (piece + 1) * PIECE)
        value = dot(inputs, w_up_ref[:, units])
        inner = to_low(value * gelu_parts(dot(inputs, w_up_ref[:, gates]))[0])
        part = down_of(inner, units)
        total = part if total is None else total + part
    return total


def lane_halves(values):
    lane = lax.broadcasted_iota(jnp.int32, values.shape, 1)
    zero = jnp.zeros_like(values)
    return jnp.concatenate(
        [jnp.where(lane < SLOT, values, zero), jnp.where(lane < SLOT, zero, values)], axis=0
    )


def key_bias(count, queries_first):
    shape = (GROUP, 2 * GROUP) if queries_first else (2 * GROUP, GROUP)
    row = lax.broadcasted_iota(jnp.int32, shape, 0)
    column = lax.broadcasted_iota(jnp.int32, shape, 1)
    key = (column if queries_first else row) % GROUP
    valid = (row % 8 == column % 8) & ((key // 8).astype(F32) < count)
    return jnp.where(valid, 0.0, -1e30).astype(F32)


def attend_chunk(qkv, bias):
    out = []
    for group in range(GROUPS):
        rows = slice(group * GROUP, (group + 1) * GROUP)
        pairs = []
        for pair in range(HEADS // 2):
            lanes = pair * 2 * SLOT
            queries = qkv[rows, lanes : lanes + GROUP]
            keys = lane_halves(qkv[rows, SLOTS + lanes : SLOTS + lanes + GROUP])
            values = lane_halves(qkv[rows, 2 * SLOTS + lanes : 2 * SLOTS + lanes + GROUP])
            scores = dot_nt(queries, keys) * SCALE + bias
            probs = []
            for part in (scores[:, :GROUP], scores[:, GROUP:]):
                raised = jnp.exp(part - jnp.max(part, axis=1, keepdims=True))
                probs.append(raised * (1.0 / jnp.sum(raised, axis=1, keepdims=True)))
            pairs.append(to_low(dot(to_low(jnp.concatenate(probs, axis=1)), values)))
        out.append(jnp.concatenate(pairs, axis=1))
    return jnp.concatenate(out, axis=0)


def motion_forward_kernel(
    facts_ref, arrived_ref, codes_ref, vec_ref, w_in_ref, w_qkv_ref, w_o_ref, w_up_ref, w_down_ref, w_out_ref,
    branch_ref, u_ref, u2_ref, u3_ref, qkv1_ref, qkv2_ref, o1_ref, o2_ref, last_ref,
    wide,
):
    def vec(i):
        return vec_ref[i : i + 1, :]

    unpack_positions(arrived_ref, wide)
    bias = key_bias(facts_ref[0, COUNT], True)
    codes = every_group(codes_ref[...])
    inputs = to_low(tokens_of(wide) * vec(0) + vec(1))
    stream = dot(inputs, w_in_ref[...]) + vec(2)
    for index, (first, x_ref, qkv_ref, o_ref) in enumerate(
        ((3, u_ref, qkv1_ref, o1_ref), (6, u2_ref, qkv2_ref, o2_ref))
    ):
        x_ref[...] = stream
        a = to_low(normal_parts(stream)[0] * vec(first) + vec(first + 1) + codes)
        qkv = to_low(dot(a, w_qkv_ref[index]))
        qkv_ref[...] = qkv
        mixture = attend_chunk(qkv, bias)
        o_ref[...] = mixture
        stream = stream + (dot(mixture, w_o_ref[index]) + vec(first + 2))
    u3_ref[...] = stream
    c = to_low(normal_parts(stream)[0] * vec(9) + vec(10))
    fed = feed_forward(c, w_up_ref, lambda inner, units: dot(inner, w_down_ref[units, :]))
    last = to_low(stream + (fed + vec(11)))
    last_ref[...] = last
    put_tokens(wide, (dot(last, w_out_ref[...]) + vec(12)) * facts_ref[0, KEEP])
    pack_positions(wide, branch_ref)


def motion_forward(facts, arrived, weights, vectors):
    outs = [((CLIP, 160, 128), BF16)] + [((PIX, WIDTH), F32)] * 3 + [((PIX, 3 * SLOTS), BF16)] * 2
    outs = outs + [((PIX, SLOTS), BF16)] * 2 + [((PIX, WIDTH), BF16)]
    operands = (facts, arrived, frame_codes(), vectors) + tuple(
        weights[name] for name in ("in", "qkv", "o", "up", "down", "out")
    )
    return call(
        motion_forward_kernel, operands, outs, "motion_forward", 23, 1, [pltpu.VMEM((CLIP, OWN, WIDTH), F32)]
    )


def prepare_kernel(sq_ref, up_ref, down_ref, sel_ref, w_in, w_qkv, w_o, w_up, w_down, w_out, t_in, t_qkv, t_o, t_up, t_down, t_out):
    sel = sel_ref[...]
    low = [to_low(sq_ref[i]) for i in range(10)]
    w_in[...] = low[0]
    t_in[...] = low[0].T
    w_out[...] = low[9]
    t_out[...] = low[9].T
    for index, first in enumerate((1, 5)):
        for j in range(3):
            padded = to_low(dot(low[first + j], sel))
            w_qkv[index, :, j * SLOTS : (j + 1) * SLOTS] = padded
            t_qkv[index, j * SLOTS : (j + 1) * SLOTS, :] = padded.T
        padded = to_low(dot_nt(low[first + 3].T, sel.T))
        t_o[index] = padded
        w_o[index] = padded.T
    up = to_low(up_ref[...])
    w_up[...] = up
    t_up[...] = up.T
    down = to_low(down_ref[...])
    t_down[...] = down
    w_down[...] = down.T


def prepare(squares, up, down):
    shapes = {
        "in": (WIDTH, WIDTH), "qkv": (2, WIDTH, 3 * SLOTS), "o": (2, SLOTS, WIDTH), "up": (WIDTH, 2 * FF_INNER),
        "down": (FF_INNER, WIDTH), "out": (WIDTH, WIDTH),
        "in_t": (WIDTH, WIDTH), "qkv_t": (2, 3 * SLOTS, WIDTH), "o_t": (2, WIDTH, SLOTS), "up_t": (2 * FF_INNER, WIDTH),
        "down_t": (WIDTH, FF_INNER), "out_t": (WIDTH, WIDTH),
    }
    made = call(
        prepare_kernel, (squares, up, down, slot_selector()), [(x, BF16) for x in shapes.values()], "motion_weights", 9
    )
    return dict(zip(shapes, made))


def column_sum(values):
    return jnp.sum(values, axis=0, keepdims=True)


def anywhere():
    return pl.BlockSpec(memory_space=pl.ANY)


def feed_backward_kernel(
    core_ref, facts_ref, grad_ref, u3_ref, vec_ref, w_up_ref, t_down_ref, t_out_ref,
    dz_ref, du4_ref, dbranch_ref, own_ref, other_ref,
    wide, dz_here, leaving,
):
    unpack_positions(grad_ref, wide)
    dbranch = to_low(tokens_of(wide) * facts_ref[0, KEEP])
    dbranch_ref[...] = dbranch
    du4 = dot(dbranch, t_out_ref[...])
    du4_ref[...] = du4
    d4 = to_low(du4)
    c = to_low(normal_parts(u3_ref[...])[0] * vec_ref[9:10, :] + vec_ref[10:11, :])
    z = dot(c, w_up_ref[...])
    value = z[:, :FF_INNER]
    gelu, slope = gelu_parts(z[:, FF_INNER:])
    inner = to_low(value * gelu)
    dinner = dot(d4, t_down_ref[...])
    dz = to_low(jnp.concatenate([dinner * gelu, dinner * value * slope], axis=1))
    dz_here[...] = dz
    copy = pltpu.make_async_copy(dz_here, dz_ref, leaving)
    copy.start()
    g_down = dot_tn(d4, inner)
    g_up = dot_tn(c, dz)
    bound = jnp.maximum(jnp.max(jnp.abs(g_up)), jnp.max(jnp.abs(g_down)))

    def put(ref, half):
        for tile in range(UP_TILES):
            start = half * FF_INNER + tile * 128
            ref[tile_rows(tile)] = g_up[:, start : start + 128]
        for tile in range(DOWN_TILES):
            start = half * (FF_INNER // 2) + tile * 128
            ref[tile_rows(UP_TILES + tile)] = g_down[:, start : start + 128]
        used = (UP_TILES + DOWN_TILES) * WIDTH
        ref[used:] = jnp.full((EARLY_ROWS - used, 128), bound)

    for core in range(2):

        @pl.when(core_ref[0] == core)
        def _(core=core):
            put(own_ref, core)
            put(other_ref, 1 - core)

    copy.wait()


def feed_backward(core, facts, grad, weights, vectors, u3):
    operands = (core, facts, grad, u3, vectors) + tuple(weights[n] for n in ("up", "down_t", "out_t"))
    outs = [((PIX, 2 * FF_INNER), BF16), ((PIX, WIDTH), F32), ((PIX, WIDTH), BF16)] + [((EARLY_ROWS, 128), F32)] * 2
    return pl.pallas_call(
        feed_backward_kernel,
        in_specs=[in_smem()] * 2 + [in_vmem()] * (len(operands) - 2),
        out_specs=[anywhere()] + [in_vmem()] * 4,
        out_shape=[jax.ShapeDtypeStruct(*out) for out in outs],
        scratch_shapes=[
            pltpu.VMEM((CLIP, OWN, WIDTH), F32),
            pltpu.VMEM((PIX, 2 * FF_INNER), BF16),
            pltpu.SemaphoreType.DMA,
        ],
        cost_estimate=pl.CostEstimate(flops=int(15 * 1.1e9), bytes_accessed=0, transcendentals=0),
        compiler_params=pltpu.CompilerParams(vmem_limit_bytes=60 * 2**20),
        name="feed_backward",
    )(*operands)


def upper_backward_kernel(
    vec_ref, t_up_at, dz_at, du4_at, u3_at, dbranch_at, last_at,
    du3_ref, g_out_ref, g_vec_ref,
    t_up, dz, du4_here, u3_here, dbranch_here, last_here, coming,
):
    size = PIX // 4
    pairs = [(t_up_at, t_up)]
    for part in range(4):
        rows = slice(part * size, (part + 1) * size)
        pairs.append((dz_at.at[rows], dz.at[rows]))
    pairs += [(du4_at, du4_here), (u3_at, u3_here), (dbranch_at, dbranch_here), (last_at, last_here)]
    arrivals = [pltpu.make_async_copy(x, y, coming.at[k]) for k, (x, y) in enumerate(pairs)]
    for copy in arrivals:
        copy.start()
    arrivals[0].wait()
    parts = []
    for part in range(4):
        arrivals[part + 1].wait()
        parts.append(dot(dz[part * size : (part + 1) * size, :], t_up[...]))
    dc = jnp.concatenate(parts, axis=0)
    for copy in arrivals[5:]:
        copy.wait()
    du4 = du4_here[...]
    dbranch = dbranch_here[...]
    normal, scale = normal_parts(u3_here[...])
    du3_ref[...] = du4 + normal_back(dc, normal, scale, vec_ref[9:10, :])
    g_out_ref[...] = dot_tn(last_here[...], dbranch)
    sums = [column_sum(dc * normal), column_sum(dc), column_sum(to_low(du4).astype(F32)), column_sum(dbranch.astype(F32))]
    g_vec_ref[...] = jnp.concatenate(sums + [jnp.zeros((4, WIDTH), F32)], axis=0)


def upper_backward(dz, du4, dbranch, u3, last, vectors, weights):
    moved = (weights["up_t"], dz, du4, u3, dbranch, last)
    outs = [((PIX, WIDTH), F32), ((WIDTH, WIDTH), F32), ((8, WIDTH), F32)]
    return pl.pallas_call(
        upper_backward_kernel,
        in_specs=[in_vmem()] + [anywhere()] * len(moved),
        out_specs=[in_vmem()] * 3,
        out_shape=[jax.ShapeDtypeStruct(*out) for out in outs],
        scratch_shapes=[pltpu.VMEM(x.shape, x.dtype) for x in moved] + [pltpu.SemaphoreType.DMA((9,))],
        cost_estimate=pl.CostEstimate(flops=int(6 * 1.1e9), bytes_accessed=0, transcendentals=0),
        compiler_params=pltpu.CompilerParams(vmem_limit_bytes=60 * 2**20),
        name="upper_backward",
    )(vectors, *moved)


def attend_back_chunk(qkv, d_mixture, bias):
    out = []
    for group in range(GROUPS):
        rows = slice(group * GROUP, (group + 1) * GROUP)
        grads = [[], [], []]
        for pair in range(HEADS // 2):
            lanes = pair * 2 * SLOT
            queries = qkv[rows, lanes : lanes + GROUP]
            keys = lane_halves(qkv[rows, SLOTS + lanes : SLOTS + lanes + GROUP])
            values = lane_halves(qkv[rows, 2 * SLOTS + lanes : 2 * SLOTS + lanes + GROUP])
            d_out = d_mixture[rows, lanes : lanes + GROUP]
            scores = dot_nt(keys, queries) * SCALE + bias
            d_probs = dot_nt(values, d_out)
            low_probs = []
            d_scores = []
            for head in range(2):
                part = scores[head * GROUP : (head + 1) * GROUP]
                d_part = d_probs[head * GROUP : (head + 1) * GROUP]
                raised = jnp.exp(part - jnp.max(part, axis=0, keepdims=True))
                probs = raised * (1.0 / jnp.sum(raised, axis=0, keepdims=True))
                low_probs.append(to_low(probs))
                d_scores.append(to_low(probs * (d_part - jnp.sum(probs * d_part, axis=0, keepdims=True))))
            low_probs = jnp.concatenate(low_probs, axis=0)
            d_scores = jnp.concatenate(d_scores, axis=0)
            d_values = dot(low_probs, d_out)
            d_keys = dot(d_scores, queries) * SCALE
            d_queries = dot_tn(d_scores, keys) * SCALE
            lane = lax.broadcasted_iota(jnp.int32, (GROUP, GROUP), 1)
            grads[0].append(to_low(d_queries))
            grads[1].append(to_low(jnp.where(lane < SLOT, d_keys[:GROUP], d_keys[GROUP:])))
            grads[2].append(to_low(jnp.where(lane < SLOT, d_values[:GROUP], d_values[GROUP:])))
        out.append(jnp.concatenate(grads[0] + grads[1] + grads[2], axis=1))
    return jnp.concatenate(out, axis=0)


def attention_backward(count, grad, stream, qkv, gain, t_o, t_qkv):
    d_out = to_low(grad)
    d_mixture = to_low(dot(d_out, t_o))
    d_qkv = attend_back_chunk(qkv, d_mixture, key_bias(count, False))
    normal, scale = normal_parts(stream)
    d_a = dot(d_qkv, t_qkv)
    rows = [column_sum(d_a * normal), column_sum(d_a), column_sum(d_out.astype(F32))]
    return grad + normal_back(d_a, normal, scale, gain), d_qkv, rows


def second_backward_kernel(
    facts_ref, grad_ref, u2_ref, qkv_ref, vec_ref, t_o_ref, t_qkv_ref,
    du2_ref, d_qkv_ref, g_vec_ref,
):
    du2, d_qkv, rows = attention_backward(
        facts_ref[0, COUNT], grad_ref[...], u2_ref[...], qkv_ref[...], vec_ref[6:7, :], t_o_ref[1], t_qkv_ref[1]
    )
    du2_ref[...] = du2
    d_qkv_ref[...] = d_qkv
    g_vec_ref[...] = jnp.concatenate(rows + [jnp.zeros((5, WIDTH), F32)], axis=0)


def second_backward(grad, facts, weights, vectors, u2, qkv):
    operands = (facts, grad, u2, qkv, vectors, weights["o_t"], weights["qkv_t"])
    outs = [((PIX, WIDTH), F32), ((PIX, 3 * SLOTS), BF16), ((8, WIDTH), F32)]
    return call(second_backward_kernel, operands, outs, "second_backward", 15, 1, limit=36)


def first_backward_kernel(
    facts_ref, grad_ref, u_ref, qkv_ref, arrived_ref, vec_ref, t_o_ref, t_qkv_ref, t_in_ref,
    du_ref, d_qkv_ref, g_vec_ref,
    wide,
):
    unpack_positions(arrived_ref, wide)
    du, d_qkv, rows = attention_backward(
        facts_ref[0, COUNT], grad_ref[...], u_ref[...], qkv_ref[...], vec_ref[3:4, :], t_o_ref[0], t_qkv_ref[0]
    )
    du = to_low(du)
    du_ref[...] = du
    d_qkv_ref[...] = d_qkv
    d_inputs = dot(du, t_in_ref[...])
    top = [column_sum(d_inputs * tokens_of(wide)), column_sum(d_inputs), column_sum(du.astype(F32))]
    g_vec_ref[...] = jnp.concatenate(top + rows + [jnp.zeros((2, WIDTH), F32)], axis=0)


def first_backward(grad, facts, arrived, weights, vectors, u, qkv):
    operands = (facts, grad, u, qkv, arrived, vectors, weights["o_t"], weights["qkv_t"], weights["in_t"])
    outs = [((PIX, WIDTH), BF16), ((PIX, 3 * SLOTS), BF16), ((8, WIDTH), F32)]
    return call(
        first_backward_kernel, operands, outs, "first_backward", 17, 1, [pltpu.VMEM((CLIP, OWN, WIDTH), F32)], limit=36
    )


def attention_grads(grad, stream, d_qkv, mixture, codes, gain, offset, sel_t):
    padded = dot_tn(mixture, to_low(grad))
    w_o_grad = jnp.concatenate([padded[head * SLOT : head * SLOT + HEAD_DIM] for head in range(HEADS)], axis=0)
    a = to_low(normal_parts(stream)[0] * gain + offset + every_group(codes))
    grads = []
    for j in range(3):
        tight = to_low(dot(d_qkv[:, j * SLOTS : (j + 1) * SLOTS], sel_t))
        grads.append(dot_tn(a, tight))
    return grads + [w_o_grad]


def second_grads_kernel(grad_ref, u2_ref, d_qkv_ref, o_ref, codes_ref, vec_ref, sel_t_ref, gq_ref, gk_ref, gv_ref, go_ref):
    grads = attention_grads(
        grad_ref[...], u2_ref[...], d_qkv_ref[...], o_ref[...], codes_ref[...], vec_ref[6:7, :], vec_ref[7:8, :], sel_t_ref[...]
    )
    for ref, value in zip((gq_ref, gk_ref, gv_ref, go_ref), grads):
        ref[...] = value


def second_grads(grad, vectors, u2, d_qkv, mixture):
    operands = (grad, u2, d_qkv, mixture, frame_codes(), vectors, slot_selector().T)
    return call(second_grads_kernel, operands, [((WIDTH, WIDTH), F32)] * 4, "second_grads", 7, limit=36)


def first_grads_kernel(
    core_ref, facts_ref, loss_ref, grad_ref, u_ref, d_qkv_ref, o_ref, du_ref, arrived_ref, codes_ref, vec_ref, sel_t_ref,
    g5_ref, g6_ref, g7_ref, g8_ref, g9_ref, feed_vec_ref, second_vec_ref, first_vec_ref,
    own_ref, other_ref,
    wide,
):
    unpack_positions(arrived_ref, wide)
    grads = attention_grads(
        grad_ref[...], u_ref[...], d_qkv_ref[...], o_ref[...], codes_ref[...], vec_ref[3:4, :], vec_ref[4:5, :], sel_t_ref[...]
    )
    inputs = to_low(tokens_of(wide) * vec_ref[0:1, :] + vec_ref[1:2, :])
    later = [ref[...] for ref in (g5_ref, g6_ref, g7_ref, g8_ref, g9_ref)]
    squares = [dot_tn(inputs, du_ref[...])] + grads + later
    vector_rows = jnp.concatenate(
        [first_vec_ref[0:6, :], second_vec_ref[0:3, :], feed_vec_ref[0:4, :], jnp.full((3, WIDTH), loss_ref[0, 0] / (1024.0 * facts_ref[0, TOTAL]))], axis=0
    )
    bound = jnp.max(jnp.abs(vector_rows))
    for square in squares:
        bound = jnp.maximum(bound, jnp.max(jnp.abs(square)))
    pieces = [vector_rows[:, 64 * j : 64 * (j + 1)] for j in range(5)]
    side = jnp.concatenate(pieces + [jnp.zeros((WIDTH - 80, 64), F32)], axis=0)

    def put(ref, half):
        own = squares[5 * half : 5 * half + 5]
        for index in range(5):
            ref[tile_rows(2 * index)] = own[index][:, 0:128]
            ref[tile_rows(2 * index + 1)] = own[index][:, 128:256]
        for pair in range(2):
            ref[tile_rows(10 + pair)] = jnp.concatenate([own[2 * pair][:, 256:320], own[2 * pair + 1][:, 256:320]], axis=1)
        ref[tile_rows(12)] = jnp.concatenate([own[4][:, 256:320], side], axis=1)
        ref[13 * WIDTH :] = jnp.full((LATE_ROWS - 13 * WIDTH, 128), bound)

    for core in range(2):

        @pl.when(core_ref[0] == core)
        def _(core=core):
            put(own_ref, core)
            put(other_ref, 1 - core)


def first_grads(core, facts, loss_part, grad, arrived, vectors, u, d_qkv, mixture, du, later):
    operands = (
        core, facts, loss_part, grad, u, d_qkv, mixture, du, arrived, frame_codes(), vectors, slot_selector().T,
    ) + tuple(later)
    outs = [((LATE_ROWS, 128), F32)] * 2
    return call(first_grads_kernel, operands, outs, "first_grads", 10, 3, [pltpu.VMEM((CLIP, OWN, WIDTH), F32)], limit=44)


MUON_RATE = 0.2
ADAM_RATE = 0.4
DECAY = 0.01
AVERAGE = 0.75
STEP = 10
SHRINK = 1.0 - MUON_RATE * DECAY
SQUARE_RATE = MUON_RATE * 0.2 * math.sqrt(WIDTH)
UP_RATE = MUON_RATE * 0.2 * math.sqrt(2 * FF_INNER)
DOWN_RATE = MUON_RATE * 0.2 * math.sqrt(FF_INNER)
UP_TILES = 10
DOWN_TILES = 5
WIDE_TILES = 2 * UP_TILES
EARLY_ROWS = 4864 + 16
LATE_ROWS = 4224 + 16


def tile_rows(index):
    return slice(index * WIDTH, (index + 1) * WIDTH)


def halves(values):
    high = values.astype(BF16)
    return (high, (values - high.astype(F32)).astype(BF16))


def triple(left, right):
    stacked = jnp.concatenate([left[0], left[0], left[1]], axis=1)
    return dot(stacked, jnp.concatenate([right[0], right[1], right[0]], axis=0))


def gram_of(parts):
    high, low = parts
    half = dot_nt(jnp.concatenate([high, high], axis=1), jnp.concatenate([high * 0.5, low], axis=1))
    return half + half.T


def scaled_to_unit(matrix):
    return matrix * (1.0 / (jnp.sqrt(jnp.sum(matrix * matrix, keepdims=True)) + 1e-07))


def wide_moments_kernel(sum_ref, up_ref, down_ref, up_new_ref, down_new_ref, ahead_ref):
    for tile in range(UP_TILES):
        lanes = slice(128 * tile, 128 * (tile + 1))
        gradient = sum_ref[tile_rows(tile)]
        moment = 0.95 * up_ref[:, lanes] + gradient
        up_new_ref[:, lanes] = moment
        ahead_ref[tile] = gradient + 0.95 * moment
    for tile in range(DOWN_TILES):
        lanes = slice(128 * tile, 128 * (tile + 1))
        gradient = sum_ref[tile_rows(UP_TILES + tile)]
        moment = 0.95 * down_ref[:, lanes] + gradient
        down_new_ref[:, lanes] = moment
        ahead_ref[UP_TILES + tile] = gradient + 0.95 * moment


def wide_moments(summed, up_moment, down_moment):
    outs = [up_moment.shape, down_moment.shape, (UP_TILES + DOWN_TILES, WIDTH, 128)]
    return call(
        wide_moments_kernel, (summed, up_moment, down_moment), [(x, F32) for x in outs], "wide_moments", 4, limit=32
    )


def wide_direction_kernel(core_ref, own_ref, got_ref, o_ref, matrix):
    def put(tile, value):
        matrix[:, 128 * tile : 128 * (tile + 1)] = value

    @pl.when(core_ref[0] == 0)
    def _():
        for tile in range(UP_TILES):
            put(tile, own_ref[tile])
            put(UP_TILES + tile, got_ref[tile])

    @pl.when(core_ref[0] != 0)
    def _():
        for tile in range(DOWN_TILES):
            put(tile, got_ref[UP_TILES - DOWN_TILES + tile])
            put(DOWN_TILES + tile, own_ref[UP_TILES + tile])
        matrix[:, 128 * UP_TILES :] = jnp.zeros((WIDTH, 128 * UP_TILES), F32)

    parts = halves(scaled_to_unit(matrix[...]))
    gram = gram_of(parts)
    row = lax.broadcasted_iota(jnp.int32, (WIDTH, WIDTH), 0)
    column = lax.broadcasted_iota(jnp.int32, (WIDTH, WIDTH), 1)
    total = None
    for step in range(5):
        gram_parts = halves(gram)
        polynomial = -4.775 * gram + 2.0315 * gram_of(gram_parts)
        poly_parts = halves(polynomial)
        if total is None:
            total = polynomial + jnp.where(row == column, 3.4445, 0.0)
        else:
            total = 3.4445 * total + triple(poly_parts, halves(total))
        if step < 4:
            once = 3.4445 * gram + triple(poly_parts, gram_parts)
            gram = 3.4445 * once + triple(halves(once), poly_parts)
    direction = to_low(triple(halves(total), parts))
    for tile in range(WIDE_TILES):
        o_ref[tile] = direction[:, 128 * tile : 128 * (tile + 1)]


def wide_direction(core, own, got):
    outs = [((WIDE_TILES, WIDTH, 128), BF16)]
    return call(
        wide_direction_kernel, (core, own, got), outs, "wide_direction", 16, 1, [pltpu.VMEM((WIDTH, 128 * WIDE_TILES), F32)], limit=40
    )[0]


def wide_update_kernel(
    core_ref, own_ref, got_ref, up_ref, down_ref, up_ema_ref, down_ema_ref,
    up_new_ref, up_ema_new_ref, down_new_ref, down_ema_new_ref,
):
    def update(up_dir, down_dir):
        for tile in range(WIDE_TILES):
            lanes = slice(128 * tile, 128 * (tile + 1))
            up_new_ref[:, lanes] = up_ref[:, lanes] * SHRINK - UP_RATE * up_dir[tile].astype(F32)
        for tile in range(2 * DOWN_TILES):
            lanes = slice(128 * tile, 128 * (tile + 1))
            down_new_ref[:, lanes] = down_ref[:, lanes] * SHRINK - DOWN_RATE * down_dir[tile].astype(F32)

    def average(half):
        lanes = slice(128 * UP_TILES * half, 128 * UP_TILES * (half + 1))
        up_ema_new_ref[...] = AVERAGE * up_ema_ref[...] + (1.0 - AVERAGE) * up_new_ref[:, lanes]
        lanes = slice(128 * DOWN_TILES * half, 128 * DOWN_TILES * (half + 1))
        down_ema_new_ref[...] = AVERAGE * down_ema_ref[...] + (1.0 - AVERAGE) * down_new_ref[:, lanes]

    @pl.when(core_ref[0] == 0)
    def _():
        update(own_ref, got_ref)
        average(0)

    @pl.when(core_ref[0] != 0)
    def _():
        update(got_ref, own_ref)
        average(1)


def wide_update(core, own, got, up, down, up_ema, down_ema):
    outs = [(x.shape, F32) for x in (up, up_ema, down, down_ema)]
    return call(wide_update_kernel, (core, own, got, up, down, up_ema, down_ema), outs, "wide_update", 7, 1)


class Inward:
    def __init__(self, source, target, semaphore):
        self.copy = pltpu.make_async_copy(source, target, semaphore)
        self.target = target
        self.state = 0

    def begin(self):
        self.copy.start()
        self.state = 1

    def ready(self):
        if self.state == 1:
            self.copy.wait()
            self.state = 2
        return self.target

    def __getitem__(self, index):
        return self.ready()[index]


def squares_step(current, passes):
    def symmetric(values, count):
        if count == 1:
            low = [to_low(x) for x in values]
            return [dot_nt(x, x) for x in low]
        return [gram_of(halves(x)) for x in values]

    grams = symmetric(current, passes[0])
    squared = symmetric(grams, passes[1])
    polynomials = [-4.775 * gram + 2.0315 * square for gram, square in zip(grams, squared)]
    if passes[2] == 1:
        moved = [dot(to_low(p), to_low(x)) for p, x in zip(polynomials, current)]
    else:
        moved = [triple(halves(p), halves(x)) for p, x in zip(polynomials, current)]
    return [3.4445 * x + y for x, y in zip(current, moved)]


DIRECTION_OUTS = 7


def directions_kernel(sums, *refs):
    count = 5
    sources, refs = refs[:count], refs[count:]
    targets, refs = refs[:DIRECTION_OUTS], refs[DIRECTION_OUTS:]
    inner, refs = refs[:count], refs[count:]
    outer, refs = refs[:DIRECTION_OUTS], refs[DIRECTION_OUTS:]
    coming, going, matrix = refs
    inputs = [Inward(x, y, coming.at[i]) for i, (x, y) in enumerate(zip(sources, inner))]
    moment_ref, m1_ref, m2_ref, vec_ref, vec_ema_ref = inputs
    leaving = [pltpu.make_async_copy(x, y, going.at[i]) for i, (x, y) in enumerate(zip(outer, targets))]
    direction_ref, moment_new_ref, m1_new_ref, m2_new_ref, vec_new_ref, vec_ema_new_ref, loss_ref = outer
    for value in inputs:
        value.begin()

    side = sums[tile_rows(12)][:, 64:128]
    rows = jnp.concatenate([side[16 * j : 16 * (j + 1)] for j in range(5)], axis=1)
    loss_ref[...] = rows[13:14, 0:128]
    gradient = rows[0:13]
    first = 0.9 * m1_ref[...] + 0.1 * gradient
    second = 0.999 * m2_ref[...] + 0.001 * (gradient * gradient)
    m1_new_ref[...] = first
    m2_new_ref[...] = second
    adjusted = first * (1.0 / (1.0 - 0.9**STEP)) / (jnp.sqrt(second * (1.0 / (1.0 - 0.999**STEP))) + 1e-08)
    fresh = vec_ref[...] - ADAM_RATE * (adjusted + DECAY * vec_ref[...])
    vec_new_ref[...] = fresh
    vec_ema_new_ref[...] = AVERAGE * vec_ema_ref[...] + (1.0 - AVERAGE) * fresh
    for index in range(5):
        lanes = slice(64 * (index % 2), 64 * (index % 2) + 64)
        gradient = jnp.concatenate(
            [sums[tile_rows(2 * index)], sums[tile_rows(2 * index + 1)], sums[tile_rows(10 + index // 2)][:, lanes]], axis=1
        )
        moment = 0.95 * moment_ref[index] + gradient
        moment_new_ref[index] = moment
        matrix[index] = scaled_to_unit(gradient + 0.95 * moment)
    for copy in leaving[1:7]:
        copy.start()

    def advance(passes):
        moved = squares_step([matrix[index] for index in range(5)], passes)
        for index in range(5):
            matrix[index] = moved[index]

    advance((1, 1, 1))
    advance((1, 1, 1))
    advance((3, 1, 3))
    advance((3, 3, 3))
    advance((3, 3, 3))
    direction_ref[...] = to_low(matrix[...])
    leaving[0].start()
    for copy in leaving:
        copy.wait()


def directions(summed, moment, m1, m2, vectors, vec_ema):
    operands = (moment, m1, m2, vectors, vec_ema)
    outs = [(moment.shape, BF16), (moment.shape, F32)] + [(vectors.shape, F32)] * 4 + [((1, 128), F32)]
    return pl.pallas_call(
        directions_kernel,
        in_specs=[in_vmem()] + [anywhere()] * len(operands),
        out_specs=[anywhere()] * len(outs),
        out_shape=[jax.ShapeDtypeStruct(*out) for out in outs],
        scratch_shapes=[pltpu.VMEM(x.shape, x.dtype) for x in operands]
        + [pltpu.VMEM(*out) for out in outs]
        + [pltpu.SemaphoreType.DMA((len(operands),)), pltpu.SemaphoreType.DMA((len(outs),))]
        + [pltpu.VMEM(moment.shape, F32)],
        cost_estimate=pl.CostEstimate(flops=int(22 * 1.1e9), bytes_accessed=0, transcendentals=0),
        compiler_params=pltpu.CompilerParams(vmem_limit_bytes=46 * 2**20),
        name="directions",
    )(summed, *operands)


def own_squares_kernel(core_ref, own_ref, weight_ref, ema_ref, new_ref, ema_new_ref, own, weight, ema, new, ema_new, coming, going):
    core = core_ref[0]
    arrivals = []
    for j in range(5):
        pairs = ((weight_ref.at[core, j], weight.at[j]), (own_ref.at[j], own.at[j]), (ema_ref.at[j], ema.at[j]))
        arrivals.append([pltpu.make_async_copy(x, y, coming.at[i, j]) for i, (x, y) in enumerate(pairs)])
    for copies in arrivals:
        for copy in copies:
            copy.start()
    leaving = []
    for j in range(5):
        for copy in arrivals[j]:
            copy.wait()
        fresh = weight[j] * SHRINK - SQUARE_RATE * own[j].astype(F32)
        new[j] = fresh
        ema_new[j] = AVERAGE * ema[j] + (1.0 - AVERAGE) * fresh
        for i, (x, y) in enumerate(((new.at[j], new_ref.at[core, j]), (ema_new.at[j], ema_new_ref.at[j]))):
            leaving.append(pltpu.make_async_copy(x, y, going.at[i, j]))
            leaving[-1].start()
    for copy in leaving:
        copy.wait()


def own_squares(core, own, weights, ema):
    square = (5, WIDTH, WIDTH)
    return pl.pallas_call(
        own_squares_kernel,
        in_specs=[in_smem()] + [anywhere()] * 3,
        out_specs=[anywhere()] * 2,
        out_shape=[jax.ShapeDtypeStruct((2,) + square, F32), jax.ShapeDtypeStruct(square, F32)],
        scratch_shapes=[pltpu.VMEM(square, BF16)]
        + [pltpu.VMEM(square, F32)] * 4
        + [pltpu.SemaphoreType.DMA((3, 5)), pltpu.SemaphoreType.DMA((2, 5))],
        cost_estimate=pl.CostEstimate(flops=int(4 * 1.1e9), bytes_accessed=0, transcendentals=0),
        compiler_params=pltpu.CompilerParams(vmem_limit_bytes=60 * 2**20),
        name="own_squares",
    )(core, own, weights, ema)


def other_squares_kernel(core_ref, got_ref, weight_ref, begun_ref, new_ref, got, weight, new, coming, going):
    other = 1 - core_ref[0]
    arrivals = []
    for j in range(5):
        pairs = ((weight_ref.at[other, j], weight.at[j]), (got_ref.at[j], got.at[j]))
        arrivals.append([pltpu.make_async_copy(x, y, coming.at[i, j]) for i, (x, y) in enumerate(pairs)])
    for copies in arrivals:
        for copy in copies:
            copy.start()
    leaving = []
    for j in range(5):
        for copy in arrivals[j]:
            copy.wait()
        new[j] = weight[j] * SHRINK - SQUARE_RATE * got[j].astype(F32)
        leaving.append(pltpu.make_async_copy(new.at[j], new_ref.at[other, j], going.at[j]))
        leaving[-1].start()
    for copy in leaving:
        copy.wait()


def other_squares(core, got, weights, begun):
    square = (5, WIDTH, WIDTH)
    return pl.pallas_call(
        other_squares_kernel,
        in_specs=[in_smem()] + [anywhere()] * 3,
        out_specs=anywhere(),
        out_shape=jax.ShapeDtypeStruct(begun.shape, F32),
        input_output_aliases={3: 0},
        scratch_shapes=[pltpu.VMEM(square, BF16)]
        + [pltpu.VMEM(square, F32)] * 2
        + [pltpu.SemaphoreType.DMA((2, 5)), pltpu.SemaphoreType.DMA((5,))],
        cost_estimate=pl.CostEstimate(flops=int(3 * 1.1e9), bytes_accessed=0, transcendentals=0),
        compiler_params=pltpu.CompilerParams(vmem_limit_bytes=60 * 2**20),
        name="other_squares",
    )(core, got, weights, begun)


TAPS = 9
CHAN = 4


def group_ones():
    group = np.arange(WIDTH) // (WIDTH // GN_GROUPS)
    return jnp.asarray((group[:, None] == group[None, :]).astype(np.float32), BF16)


def group_mean(column_sums, ones):
    rest = jnp.broadcast_to(column_sums, (8, WIDTH))
    total = jnp.zeros((8, WIDTH), F32)
    for _ in range(3):
        part = to_low(rest)
        total = total + dot(part, ones)
        rest = rest - part.astype(F32)
    return total[0:1] * (1.0 / (PIX * (WIDTH // GN_GROUPS)))


def chunk_rows(index):
    return pl.ds(pl.multiple_of(index * CHUNK, CHUNK), CHUNK)


def over_chunks(body, *start):
    return lax.fori_loop(0, CHUNKS, lambda i, carry: body(i, *carry), start)


def zero_row():
    return jnp.zeros((1, WIDTH), F32)


def group_stats(ref, ones, column_sums):
    centre = group_mean(column_sums, ones)

    def squares(i, total):
        shifted = ref[chunk_rows(i), :] - centre
        return (total + column_sum(shifted * shifted),)

    (total,) = over_chunks(squares, zero_row())
    return centre, lax.rsqrt(group_mean(total, ones) + 1e-05)


def sigmoid(values):
    return 1.0 / (1.0 + jnp.exp(-values))


def shifted_lanes(values, down, right):
    lane = lax.broadcasted_iota(jnp.int32, values.shape, 1)
    line = lane // LATENT + down
    place = lane % LATENT + right
    inside = (line >= 0) & (line < LATENT) & (place >= 0) & (place < LATENT)
    offset = (down * LATENT + right) % PIX
    moved = pltpu.roll(values, (PIX - offset) % PIX, 1) if offset else values
    return jnp.where(inside, moved, 0.0)


def put_columns(cols_ref, act_ref):
    zeros = jnp.zeros((LATENT, 3 * WIDTH), BF16)
    cols_ref[0:LATENT, :] = zeros
    cols_ref[LATENT + PIX :, :] = zeros
    act_ref[0:8, :] = jnp.zeros((8, WIDTH), F32)
    act_ref[8 + PIX :, :] = jnp.zeros((8, WIDTH), F32)

    for i in range(CHUNKS):
        place = (lax.broadcasted_iota(jnp.int32, (CHUNK, WIDTH), 0)) % LATENT
        middle = act_ref[8 + i * CHUNK : 8 + (i + 1) * CHUNK, :]
        left = act_ref[7 + i * CHUNK : 7 + (i + 1) * CHUNK, :]
        right = act_ref[9 + i * CHUNK : 9 + (i + 1) * CHUNK, :]
        left = jnp.where(place == 0, 0.0, left)
        right = jnp.where(place == LATENT - 1, 0.0, right)
        cols_ref[LATENT + i * CHUNK : LATENT + (i + 1) * CHUNK, :] = jnp.concatenate(
            [to_low(left), to_low(middle), to_low(right)], axis=1
        )


def resnet_kernel(
    facts_ref, pair_ref, vec_ref, temb_ref, ones_ref, w_in_ref, w_res_ref, squares_ref,
    resnet_ref, tokens_ref,
    first, inner, act, cols,
):
    ones = ones_ref[...]

    def vec(i):
        return vec_ref[i : i + 1, :]

    pair = pair_ref[...].astype(F32)
    noisy = facts_ref[0, COS] * pair + facts_ref[0, SIN] * jnp.concatenate([pair[CHAN:], pair[:CHAN]], axis=0)
    columns = tap_rows([shifted_lanes(noisy, tap // 3 - 1, tap % 3 - 1)[:CHAN] for tap in range(TAPS)])
    w_in = tap_rows([w_in_ref[tap // 3, tap % 3] for tap in range(TAPS)])
    total = zero_row()
    for i in range(CHUNKS):
        part = dot_tn(columns[:, i * CHUNK : (i + 1) * CHUNK], w_in) + vec(0)
        first[i * CHUNK : (i + 1) * CHUNK, :] = part
        total = total + column_sum(part)

    def activate(source, total, gain, offset):
        centre, scale = group_stats(source, ones, total)

        def one(i):
            normal = (source[chunk_rows(i), :] - centre) * scale * gain + offset
            act[pl.ds(pl.multiple_of(8 + i * CHUNK, 8), CHUNK), :] = normal * sigmoid(normal)
            return ()

        over_chunks(lambda i: one(i))
        put_columns(cols, act)

    def convolve_chunk(i, which):
        out = None
        for line in range(3):
            part = cols[pl.ds(pl.multiple_of(i * CHUNK + LATENT * line, LATENT), CHUNK), :]
            term = dot(part, w_res_ref[which, line])
            out = term if out is None else out + term
        return out

    activate(first, total, vec(1), vec(2))
    shift = vec(3) + temb_ref[:, :WIDTH]

    def first_step(i, total):
        part = convolve_chunk(i, 0) + shift
        inner[chunk_rows(i), :] = part
        return (total + column_sum(part),)

    (total,) = over_chunks(first_step, zero_row())
    activate(inner, total, vec(4), vec(5))

    def second_step(i, total):
        part = first[chunk_rows(i), :] + (convolve_chunk(i, 1) + vec(6))
        resnet_ref[chunk_rows(i), :] = part
        return (total + column_sum(part),)

    (total,) = over_chunks(second_step, zero_row())
    centre, scale = group_stats(resnet_ref, ones, total)

    def token_step(i):
        normal = to_low((resnet_ref[chunk_rows(i), :] - centre) * scale * vec(7) + vec(8))
        tokens_ref[chunk_rows(i), :] = dot(normal, squares_ref[0]) + vec(9)
        return ()

    over_chunks(lambda i: token_step(i))


def resnet_block(facts, pair, vectors, w_in, w_res, squares):
    operands = (facts, pair, vectors, facts, group_ones(), w_in, w_res, squares)
    scratch = [
        pltpu.VMEM((PIX, WIDTH), F32),
        pltpu.VMEM((PIX, WIDTH), F32),
        pltpu.VMEM((PIX + 16, WIDTH), F32),
        pltpu.VMEM((PIX + 2 * LATENT, 3 * WIDTH), BF16),
    ]
    return call(resnet_kernel, operands, [((PIX, WIDTH), F32)] * 2, "resnet_block", 15, 1, scratch)


def tap_rows(pieces):
    zeros = jnp.zeros((8 - CHAN, pieces[0].shape[1]), F32)
    return to_low(jnp.concatenate([x for piece in pieces for x in (piece.astype(F32), zeros)], axis=0))


LOG2E = 1.4426950408889634
TEXT_ROWS = 128


def transformer_kernel(
    tokens_ref, resnet_ref, text_ref, vec_ref, ones_ref, sel_ref, w_kv2_ref,
    w_up_ref, t_down_ref, squares_ref,
    hidden_ref, packed_ref,
    queries, keys, values, text_kv, w_qkv_ref, w_q2_ref, w_o_ref, w_o2_ref,
):
    def vec(i):
        return vec_ref[i : i + 1, :]

    sel = sel_ref[...]
    for j in range(3):
        w_qkv_ref[:, j * SLOTS : (j + 1) * SLOTS] = to_low(dot(squares_ref[1 + j], sel))
    w_q2 = to_low(dot(squares_ref[5], sel))
    w_o = to_low(dot_tn(sel, squares_ref[4]))
    w_o2 = to_low(dot_tn(sel, squares_ref[6]))
    w_q2_ref[...] = w_q2
    w_o_ref[...] = w_o
    w_o2_ref[...] = w_o2
    lane = lax.broadcasted_iota(jnp.int32, (CHUNK, SLOTS), 1)
    counter = jnp.where(lane % SLOT == HEAD_DIM, 1.0, 0.0)

    def project(i):
        a = to_low(normal_parts(tokens_ref[chunk_rows(i), :])[0] * vec(10) + vec(11))
        qkv = dot(a, w_qkv_ref[...])
        queries[chunk_rows(i), :] = to_low(qkv[:, :SLOTS])
        keys[chunk_rows(i), :] = to_low(qkv[:, SLOTS : 2 * SLOTS])
        values[chunk_rows(i), :] = to_low(qkv[:, 2 * SLOTS :] + counter)
        return ()

    over_chunks(lambda i: project(i))
    kv = to_low(dot(text_ref[...], w_kv2_ref[...]))
    text_kv[...] = jnp.zeros_like(text_kv)
    wide_kv = jnp.concatenate(
        [dot(kv[:, :WIDTH], sel_ref[...]), dot(kv[:, WIDTH:], sel_ref[...])], axis=1
    )
    text_kv[0 : wide_kv.shape[0], :] = wide_kv
    text_lane = lax.broadcasted_iota(jnp.int32, (CHUNK, TEXT_ROWS), 1)
    text_bias = jnp.where(text_lane < TEXT_LEN, 0.0, -1e30)

    def chunk_step(i, total):
        tokens = tokens_ref[chunk_rows(i), :]
        side = lax.broadcasted_iota(jnp.int32, (CHUNK, GROUP), 1) < SLOT

        def scores_of(head):
            lanes = slice(head // 2 * GROUP, (head // 2 + 1) * GROUP)
            query = queries[chunk_rows(i), lanes]
            zero = jnp.zeros_like(query)
            own_query = jnp.where(side, query, zero) if head % 2 == 0 else jnp.where(side, zero, query)
            return dot_nt(own_query, keys[:, lanes]) * (SCALE * LOG2E)

        def mixed_of(scores, head):
            lanes = slice(head // 2 * GROUP, (head // 2 + 1) * GROUP)
            raised = jnp.exp2(scores - jnp.max(scores, axis=1, keepdims=True))
            mixed = dot(to_low(raised), values[:, lanes])
            spot = head % 2 * SLOT + HEAD_DIM
            return mixed * (1.0 / mixed[:, spot : spot + 1])

        ahead = scores_of(0)
        mixtures = []
        for head in range(HEADS):
            scores = ahead
            if head + 1 < HEADS:
                ahead = scores_of(head + 1)
            mixtures.append(mixed_of(scores, head))
        pairs = [to_low(jnp.where(side, mixtures[2 * pair], mixtures[2 * pair + 1])) for pair in range(HEADS // 2)]
        tokens = tokens + (dot(jnp.concatenate(pairs, axis=1), w_o_ref[...]) + vec(12))
        c = to_low(normal_parts(tokens)[0] * vec(13) + vec(14))
        query2 = to_low(dot(c, w_q2_ref[...]))
        pairs = []
        for pair in range(HEADS // 2):
            lanes = slice(pair * GROUP, (pair + 1) * GROUP)
            text_keys = lane_halves(to_low(text_kv[:, lanes]))
            text_values = lane_halves(to_low(text_kv[:, SLOTS + pair * GROUP : SLOTS + (pair + 1) * GROUP]))
            scores = dot_nt(query2[:, lanes], text_keys) * SCALE
            probs = []
            for part in (scores[:, :TEXT_ROWS], scores[:, TEXT_ROWS:]):
                part = part + text_bias
                raised = jnp.exp(part - jnp.max(part, axis=1, keepdims=True))
                probs.append(to_low(raised * (1.0 / jnp.sum(raised, axis=1, keepdims=True))))
            pairs.append(to_low(dot(jnp.concatenate(probs, axis=1), text_values)))
        tokens = tokens + (dot(jnp.concatenate(pairs, axis=1), w_o2_ref[...]) + vec(15))
        f = to_low(normal_parts(tokens)[0] * vec(16) + vec(17))
        fed = feed_forward(f, w_up_ref, lambda inner, units: dot_nt(inner, t_down_ref[:, units]))
        tokens = tokens + (fed + vec(18))
        hidden = resnet_ref[chunk_rows(i), :] + (dot(to_low(tokens), squares_ref[7]) + vec(19))
        hidden_ref[chunk_rows(i), :] = hidden
        return (total + column_sum(hidden),)

    (total,) = over_chunks(chunk_step, zero_row())
    centre, scale = group_stats(hidden_ref, ones_ref[...], total)
    pack_rows(packed_ref, lambda rows: (hidden_ref[rows, :] - centre) * scale)


def pack_rows(packed_ref, rows_at):
    for member in range(CLIP):
        block = to_low(rows_at(slice(member * OWN, (member + 1) * OWN)))
        packed_ref[member, 0:64, :] = block[:, 0:128]
        packed_ref[member, 64:128, :] = block[:, 128:256]
        packed_ref[member, 128:160, :] = jnp.concatenate([block[0:32, 256:320], block[32:64, 256:320]], axis=1)


def transformer_block(tokens, resnet, text, vectors, cross_kv, up, down, squares):
    operands = (
        tokens, resnet, text, vectors, group_ones(), slot_selector(), cross_kv, up, down, squares,
    )
    scratch = [pltpu.VMEM((PIX, SLOTS), BF16)] * 3 + [pltpu.VMEM((TEXT_ROWS, 2 * SLOTS), F32)]
    scratch += [pltpu.VMEM((WIDTH, 3 * SLOTS), BF16), pltpu.VMEM((WIDTH, SLOTS), BF16)] + [pltpu.VMEM((SLOTS, WIDTH), BF16)] * 2
    outs = [((PIX, WIDTH), F32), ((CLIP, 160, 128), BF16)]
    return call(transformer_kernel, operands, outs, "transformer_block", 32, 0, scratch)


def head_kernel(
    facts_ref, hidden_ref, branch_ref, pair_ref, vec_ref, ones_ref, w_ref,
    packed_ref, loss_ref,
    mixed, act, slope,
):
    ones = ones_ref[...]
    gain = vec_ref[20:21, :]
    offset = vec_ref[21:22, :]
    column_total = zero_row()
    for member in range(CLIP):
        rows = slice(member * OWN, (member + 1) * OWN)
        last = branch_ref[member, 128:160, :]
        branch = jnp.concatenate(
            [
                branch_ref[member, 0:64, :].astype(F32),
                branch_ref[member, 64:128, :].astype(F32),
                jnp.concatenate([last[:, 0:64], last[:, 64:128]], axis=0).astype(F32),
            ],
            axis=1,
        )
        part = hidden_ref[rows, :] + branch
        mixed[rows, :] = part
        column_total = column_total + column_sum(part)
    centre, scale = group_stats(mixed, ones, column_total)

    def activate(i):
        normal = (mixed[chunk_rows(i), :] - centre) * scale
        mixed[chunk_rows(i), :] = normal
        value = normal * gain + offset
        share = sigmoid(value)
        act[chunk_rows(i), :] = to_low(value * share)
        slope[chunk_rows(i), :] = share * (1.0 + value * (1.0 - share)) * gain
        return ()

    over_chunks(lambda i: activate(i))
    weight = tap_rows([w_ref[tap // 3, tap % 3] for tap in range(TAPS)])
    by_tap = dot_nt(weight, act[...])
    predicted = jnp.zeros((8, PIX), F32)
    for tap in range(TAPS):
        predicted = predicted + shifted_lanes(by_tap[8 * tap : 8 * tap + 8], tap // 3 - 1, tap % 3 - 1)
    pair = pair_ref[...].astype(F32)
    target = facts_ref[0, COS] * jnp.concatenate([pair[CHAN:], pair[:CHAN]], axis=0) - facts_ref[0, SIN] * pair
    target = jnp.where(lax.broadcasted_iota(jnp.int32, pair.shape, 0) < CHAN, target, 0.0)
    residual = (predicted - target) * facts_ref[0, VALID]
    loss_ref[...] = jnp.sum(residual * residual, keepdims=True)
    grad = to_low(2.0 * residual / facts_ref[0, TOTAL]).astype(F32)
    columns = tap_rows([shifted_lanes(grad, 1 - tap // 3, 1 - tap % 3)[:CHAN] for tap in range(TAPS)])
    total = zero_row()
    total_normal = zero_row()
    for i in range(CHUNKS):
        rows = slice(i * CHUNK, (i + 1) * CHUNK)
        part = dot_tn(columns[:, rows], weight) * slope[rows, :]
        slope[rows, :] = part
        total = total + column_sum(part)
        total_normal = total_normal + column_sum(part * mixed[rows, :])
    mean = group_mean(total, ones)
    mean_normal = group_mean(total_normal, ones)
    pack_rows(packed_ref, lambda rows: scale * (slope[rows, :] - mean - mixed[rows, :] * mean_normal))


def head_block(facts, hidden, branch, pair, vectors, weight):
    operands = (facts, hidden, branch, pair, vectors, group_ones(), weight)
    outs = [((CLIP, 160, 128), BF16), ((1, 1), F32)]
    scratch = [pltpu.VMEM((PIX, WIDTH), F32), pltpu.VMEM((PIX, WIDTH), BF16), pltpu.VMEM((PIX, WIDTH), F32)]
    return call(head_kernel, operands, outs, "head_block", 6, 1, scratch, limit=36)


def product(left, right):
    return jnp.einsum("...i,ij->...j", left, right, preferred_element_type=jnp.float32)


def time_embed(step_values, time_w1, time_w2, temb_w, temb_bias):
    half_width = WIDTH // 2
    frequency = jnp.exp(-math.log(10000.0) * jnp.arange(half_width, dtype=jnp.float32) / half_width)
    angles = step_values[..., None] * frequency
    encoding = jnp.concatenate([jnp.cos(angles), jnp.sin(angles)], axis=-1)
    hidden = product(to_low(encoding), time_w1)
    hidden = product(to_low(jax.nn.silu(hidden)), time_w2)
    return product(to_low(jax.nn.silu(hidden)), temb_w) + temb_bias


def swap_cores(values):
    return lax.ppermute(values, "dp", [(0, 1), (1, 0)])


WIRE = jnp.float16
TAIL = 16


def frame_phases():
    size = lax.axis_size("frames")
    phases = []
    shift = 0
    while (1 << shift) < size:
        group = min(4, size >> shift)
        phases.append((shift, group))
        shift += group.bit_length() - 1
    return phases


def frame_digit(shift, group):
    return (lax.axis_index("frames") >> shift) % group


def swap_frames(values, shift, distance):
    size = lax.axis_size("frames")
    return lax.ppermute(values, "frames", [(i, i ^ (distance << shift)) for i in range(size)])


def part_of(terms, start, rows):
    parts = [lax.dynamic_slice_in_dim(term, start, rows + TAIL, 0) for term in terms]
    return functools.reduce(jnp.add, parts)


def coded(terms, start, rows, bound):
    part = part_of(terms, start, rows)
    exponent = jnp.floor(14.0 - jnp.log2(jnp.maximum(bound, 1e-30)))
    place = lax.broadcasted_iota(jnp.int32, (rows + TAIL, 1), 0)
    return jnp.where(place < rows, part * jnp.exp2(exponent), exponent).astype(WIRE)


def exponent_of(message, rows):
    return message[rows : rows + 1].astype(F32)


def reduce_start(terms, bound, shift, group):
    rows = (terms[0].shape[0] - TAIL) // group
    mine = frame_digit(shift, group)
    return [coded(terms, (mine ^ d) * rows, rows, bound) for d in range(1, group)]


def reduce_send(messages, shift):
    return [swap_frames(message, shift, d + 1) for d, message in enumerate(messages)]


def reduce_end(terms, bound, got, shift, group):
    rows = (terms[0].shape[0] - TAIL) // group
    total = part_of(terms, frame_digit(shift, group) * rows, rows)
    for message in got:
        exponent = exponent_of(message, rows)
        total = total + message.astype(F32) * jnp.exp2(-exponent)
        bound = bound + jnp.exp2(15.0 - exponent)
    return [total], bound


def gather_send(block, shift, group):
    return [swap_frames(block, shift, d) for d in range(1, group)]


def gather_end(block, got, shift, group):
    rows = block.shape[0]
    mine = frame_digit(shift, group)
    total = jnp.zeros((group * rows, 128), block.dtype)
    for d, part in enumerate([block] + got):
        total = lax.dynamic_update_slice_in_dim(total, part, (mine ^ d) * rows, 0)
    return total


def decoded(block, piece):
    parts = block.reshape(-1, piece, 128)
    exponent = parts[:, piece - TAIL : piece - TAIL + 1].astype(F32)
    return (parts[:, : piece - TAIL].astype(F32) * jnp.exp2(-exponent)).reshape(-1, 128)


def first_bound(terms, used):
    return functools.reduce(jnp.add, [term[used : used + 1] for term in terms])


def fit_rows(values):
    unit = 8 * lax.axis_size("frames")
    rows = values.shape[0] - TAIL
    padded = -(-rows // unit) * unit
    return jnp.pad(values, ((0, padded - rows), (0, 0))) if padded > rows else values


def sample_groups():
    groups = []
    for block in range(lax.axis_size("frames") // CLIP):
        for half in range(2):
            groups.append(
                [
                    2 * (block * CLIP + half * HALF + place) + core
                    for core in range(2)
                    for place in range(HALF)
                ]
            )
    return groups


def swap_samples(values):
    size = lax.axis_size("frames")
    pairs = []
    for frame in range(size):
        half = (frame % CLIP) // HALF
        pairs.append((2 * frame + 1 - half, 2 * (frame ^ HALF) + half))
    return lax.ppermute(values, ("frames", "dp"), pairs)


def shards(
    latents,
    noise,
    timesteps,
    image_flags,
    frame_counts,
    text,
    conv_in,
    res_convs,
    conv_out,
    time_w1,
    time_w2,
    temb_w,
    spatial_squares,
    cross_kv,
    spatial_up,
    spatial_down,
    frozen_vectors,
    motion_squares,
    motion_up,
    motion_down,
    motion_vectors,
    square_moment,
    up_moment,
    down_moment,
    vector_moment1,
    vector_moment2,
    square_ema,
    up_ema,
    down_ema,
    vector_ema,
):
    dp_index = lax.axis_index("dp")
    place = lax.axis_index("frames")
    block = place // CLIP
    place = place % CLIP
    half = place // HALF
    stays = half == dp_index
    frame = jnp.where(stays, place, (place + HALF) % CLIP)
    pair = jnp.concatenate([latents.reshape(PIX, CHAN).T, noise.reshape(PIX, CHAN).T], axis=0)
    pair = jnp.where(stays, pair, swap_samples(pair))

    def of_block(values):
        return lax.dynamic_index_in_dim(values[0], block, 0, keepdims=False)

    text_rows = of_block(text)
    text_rows = jnp.where(stays, text_rows, swap_cores(text_rows))
    step_values = of_block(timesteps).astype(F32)[None]
    phases = (step_values / 1000.0 + 0.008) / 1.008 * (math.pi / 2)
    temb_res = time_embed(step_values, time_w1, time_w2, temb_w, frozen_vectors[22])
    flag = of_block(image_flags).astype(F32)[None]
    facts = jnp.concatenate([temb_res[0], jnp.cos(phases), jnp.sin(phases), 1.0 - flag, jnp.zeros((61,), F32)])
    facts = facts.reshape(1, 384)
    facts = jnp.where(stays, facts, swap_cores(facts))
    count = lax.dynamic_slice(frame_counts, (half, block), (1, 1)).reshape(1).astype(F32)
    total_count = 4.0 * PIX * jnp.sum(frame_counts).astype(F32)
    valid = (frame.astype(F32) < count).astype(F32)
    more = jnp.concatenate([jnp.zeros((COUNT,), F32), count, valid, total_count[None], jnp.zeros((383 - TOTAL,), F32)])
    facts = facts + more.reshape(1, 384)
    resnet, tokens = resnet_block(
        facts, pair, frozen_vectors, conv_in, res_convs.reshape(2, 3, 3 * WIDTH, WIDTH), spatial_squares
    )
    hidden, packed = transformer_block(
        tokens, resnet, text_rows, frozen_vectors, cross_kv, spatial_up, spatial_down.T, spatial_squares
    )
    groups = sample_groups()

    def exchange(values):
        return lax.all_to_all(
            values, ("frames", "dp"), split_axis=0, concat_axis=0, tiled=True, axis_index_groups=groups
        )

    arrived = exchange(packed)
    weights = prepare(motion_squares, motion_up, motion_down.T)
    branch, u, u2, u3, qkv1, qkv2, o1, o2, last = motion_forward(
        facts, arrived, weights, motion_vectors
    )
    grad, loss_part = head_block(
        facts, hidden, exchange(branch), pair, frozen_vectors, jnp.swapaxes(conv_out, 2, 3),
    )
    grad_in = exchange(grad)
    core = dp_index.reshape(1)
    dz, du4, dbranch, early, early_other = feed_backward(core, facts, grad_in, weights, motion_vectors, u3)
    phases = frame_phases()
    ordered = lax.optimization_barrier

    def gather_last(block, got, piece, rows):
        parts = [decoded(part, piece) for part in [block] + got]
        return gather_end(parts[0], parts[1:], *phases[0])[:rows]

    du4, early_other = ordered((du4, early_other))
    early_got = swap_cores(early_other)
    upper = upper_backward(dz, du4, dbranch, u3, last, motion_vectors, weights)
    early_got, du3, g9, feed_sums = ordered((early_got, *upper))

    early = [early, early_got]
    early_bound = first_bound(early, (UP_TILES + DOWN_TILES) * WIDTH)
    early = [fit_rows(term) for term in early]
    messages = reduce_start(early, early_bound, *phases[0])
    du3, *messages = ordered((du3, *messages))
    got = reduce_send(messages, phases[0][0])
    second = second_backward(du3, facts, weights, motion_vectors, u2, qkv2)
    du2, d_qkv2, second_sums, *got = ordered((*second, *got))
    early, early_bound = reduce_end(early, early_bound, got, *phases[0])

    messages = reduce_start(early, early_bound, *phases[1])
    du2, *messages = ordered((du2, *messages))
    got = reduce_send(messages, phases[1][0])
    first = first_backward(du2, facts, arrived, weights, motion_vectors, u, qkv1)
    du, d_qkv1, first_sums, du3, *got = ordered((*first, du3, *got))
    early, early_bound = reduce_end(early, early_bound, got, *phases[1])
    for shift, group in phases[2:]:
        got = reduce_send(reduce_start(early, early_bound, shift, group), shift)
        early, early_bound = reduce_end(early, early_bound, got, shift, group)
    early_block = coded(early, 0, early[0].shape[0] - TAIL, early_bound)
    early_piece = early_block.shape[0]
    for shift, group in reversed(phases[2:]):
        early_block = gather_end(early_block, gather_send(early_block, shift, group), shift, group)

    du3, early_block = ordered((du3, early_block))
    got = gather_send(early_block, *phases[1])
    later = second_grads(du3, motion_vectors, u2, d_qkv2, o2)
    du2, early_block, *more = ordered((du2, early_block, *later, *got))
    later, got = more[: len(later)], more[len(later) :]
    early_block = gather_end(early_block, got, *phases[1])

    du2, early_block = ordered((du2, early_block))
    early_got = gather_send(early_block, *phases[0])
    late, late_other = first_grads(
        core, facts, loss_part, du2, arrived, motion_vectors, u, d_qkv1, o1, du,
        (*later, g9, feed_sums, second_sums, first_sums),
    )
    late, late_other, early_block, *early_got = ordered((late, late_other, early_block, *early_got))

    late_got = swap_cores(late_other)
    early = gather_last(early_block, early_got, early_piece, EARLY_ROWS - TAIL)
    up_moment_new, down_moment_new, ahead = wide_moments(early, up_moment, down_moment.T)
    ahead, late_got = ordered((ahead, late_got))
    ahead_got = swap_cores(lax.dynamic_slice_in_dim(ahead, (1 - dp_index) * DOWN_TILES, UP_TILES, 0))
    late = [late, late_got]
    late_bound = first_bound(late, 13 * WIDTH)
    late = [fit_rows(term) for term in late]
    messages = reduce_start(late, late_bound, *phases[0])
    ahead_got, *messages = ordered((ahead_got, *messages))
    got = reduce_send(messages, phases[0][0])
    wide = wide_direction(core, ahead, ahead_got)
    wide, *got = ordered((wide, *got))
    late, late_bound = reduce_end(late, late_bound, got, *phases[0])

    wide_got = swap_cores(wide)
    for shift, group in phases[1:]:
        got = reduce_send(reduce_start(late, late_bound, shift, group), shift)
        late, late_bound = reduce_end(late, late_bound, got, shift, group)
    late_block = coded(late, 0, late[0].shape[0] - TAIL, late_bound)
    late_piece = late_block.shape[0]
    for shift, group in reversed(phases[1:]):
        late_block = gather_end(late_block, gather_send(late_block, shift, group), shift, group)
    late_block, wide_got = ordered((late_block, wide_got))
    late_got = gather_send(late_block, *phases[0])
    up_new, up_ema_new, down_new, down_ema_new = wide_update(
        core, wide, wide_got, motion_up, motion_down.T, up_ema, down_ema.T
    )
    late_block, down_ema_new, *late_got = ordered((late_block, down_ema_new, *late_got))
    late = gather_last(late_block, late_got, late_piece, LATE_ROWS - TAIL)
    square, square_moment_new, moment_first, moment_second, vector_new, vector_ema_new, loss_row = directions(
        late, square_moment, vector_moment1, vector_moment2, motion_vectors, vector_ema
    )
    square_got = swap_cores(square)
    halved = motion_squares.reshape(2, 5, WIDTH, WIDTH)
    square_new, square_ema_new = own_squares(core, square, halved, square_ema)
    square_new = other_squares(core, square_got, halved, square_new).reshape(motion_squares.shape)
    return (
        loss_row[0, 0] * (1024.0 * total_count),
        total_count,
        square_new,
        square_moment_new,
        square_ema_new,
        up_new,
        up_moment_new,
        up_ema_new,
        down_new.T,
        down_moment_new.T,
        down_ema_new.T,
        moment_first,
        moment_second,
        vector_new,
        vector_ema_new,
    )


def solution(mesh):
    return jax.shard_map(
        shards,
        mesh=mesh,
        in_specs=(
            P("dp", "frames", None, None),
            P("dp", "frames", None, None),
            P("dp", None),
            P("dp", None),
            P(),
            P("dp", None, None, None),
            P(),
            P(),
            P(),
            P(),
            P(),
            P(),
            P(),
            P(),
            P(),
            P(),
            P(),
            P(),
            P(),
            P(),
            P(),
            P("dp", None, None),
            P(None, "dp"),
            P("dp", None),
            P(),
            P(),
            P("dp", None, None),
            P(None, "dp"),
            P("dp", None),
            P(),
        ),
        out_specs=(
            P(),
            P(),
            P(),
            P("dp", None, None),
            P("dp", None, None),
            P(),
            P(None, "dp"),
            P(None, "dp"),
            P(),
            P("dp", None),
            P("dp", None),
            P(),
            P(),
            P(),
            P(),
        ),
        check_vma=False,
    )
```

```python
import functools
import math

import jax
import jax.numpy as jnp
import numpy as np
from jax import lax
from jax.experimental import pallas as pl
from jax.experimental.pallas import tpu as pltpu
from jax.sharding import PartitionSpec as P

WIDTH = 320
HEADS = 8
HEAD_DIM = 40
FF_INNER = 1280
CLIP = 16
HALF = 8
PIX = 1024
LATENT = 32
TEXT_LEN = 77
TEXT_DIM = 768
GN_GROUPS = 32
F32 = jnp.float32
BF16 = jnp.bfloat16
OWN = PIX // CLIP
SLOT = 64
SLOTS = HEADS * SLOT
CHUNK = 1024
CHUNKS = PIX // CHUNK
GROUP = 128
GROUPS = PIX // GROUP
SCALE = 1.0 / math.sqrt(HEAD_DIM)


def to_low(values):
    return values.astype(BF16)


def dot(left, right):
    return lax.dot_general(left, right, (((1,), (0,)), ((), ())), preferred_element_type=F32)


def dot_nt(left, right):
    return lax.dot_general(left, right, (((1,), (1,)), ((), ())), preferred_element_type=F32)


def dot_tn(left, right):
    return lax.dot_general(left, right, (((0,), (0,)), ((), ())), preferred_element_type=F32)


def in_vmem():
    return pl.BlockSpec(memory_space=pltpu.VMEM)


COS, SIN, KEEP, COUNT, VALID, TOTAL = range(WIDTH, WIDTH + 6)


def in_smem():
    return pl.BlockSpec(memory_space=pltpu.SMEM)


def call(kernel, operands, outs, name, micros, scalars=0, scratch=(), limit=60):
    specs = [in_smem()] * scalars + [in_vmem()] * (len(operands) - scalars)
    return pl.pallas_call(
        kernel,
        in_specs=specs,
        out_specs=[in_vmem()] * len(outs),
        out_shape=[jax.ShapeDtypeStruct(shape, kind) for shape, kind in outs],
        scratch_shapes=list(scratch),
        cost_estimate=pl.CostEstimate(flops=int(micros * 1.1e9), bytes_accessed=0, transcendentals=0),
        compiler_params=pltpu.CompilerParams(vmem_limit_bytes=limit * 2**20),
        name=name,
    )(*operands)


def slot_selector():
    out = np.zeros((WIDTH, SLOTS), np.float32)
    for head in range(HEADS):
        for j in range(HEAD_DIM):
            out[head * HEAD_DIM + j, head * SLOT + j] = 1.0
    return jnp.asarray(out, BF16)


def frame_codes():
    positions = np.arange(CLIP, dtype=np.float32)[:, None]
    column = np.arange(WIDTH)
    frequency = np.exp(np.float32(-math.log(10000.0)) * (2 * (column // 2)).astype(np.float32) / WIDTH)
    angles = positions * frequency.astype(np.float32)
    codes = np.where(column % 2 == 0, np.sin(angles), np.cos(angles)).astype(np.float32)
    return jnp.asarray(np.repeat(codes, 8, axis=0))


def unpack_positions(packed_ref, wide_ref):
    wide_ref[:, :, 0:128] = packed_ref[:, 0:64, :].astype(F32)
    wide_ref[:, :, 128:256] = packed_ref[:, 64:128, :].astype(F32)
    last = packed_ref[:, 128:160, :].astype(F32)
    wide_ref[:, 0:32, 256:320] = last[:, :, 0:64]
    wide_ref[:, 32:64, 256:320] = last[:, :, 64:128]


def pack_positions(wide_ref, packed_ref):
    packed_ref[:, 0:64, :] = to_low(wide_ref[:, :, 0:128])
    packed_ref[:, 64:128, :] = to_low(wide_ref[:, :, 128:256])
    last = jnp.concatenate([wide_ref[:, 0:32, 256:320], wide_ref[:, 32:64, 256:320]], axis=2)
    packed_ref[:, 128:160, :] = to_low(last)


def tokens_of(wide_ref):
    parts = [wide_ref[:, 8 * group : 8 * group + 8, :].reshape(GROUP, WIDTH) for group in range(GROUPS)]
    return jnp.concatenate(parts, axis=0)


def put_tokens(wide_ref, tokens):
    for group in range(GROUPS):
        part = tokens[group * GROUP : (group + 1) * GROUP].reshape(CLIP, 8, WIDTH)
        wide_ref[:, 8 * group : 8 * group + 8, :] = part


def every_group(rows):
    return jnp.concatenate([rows] * GROUPS, axis=0)


def normal_parts(values):
    centre = jnp.mean(values, axis=-1, keepdims=True)
    shifted = values - centre
    scale = lax.rsqrt(jnp.mean(shifted * shifted, axis=-1, keepdims=True) + 1e-05)
    return shifted * scale, scale


def normal_back(grad, normal, scale, gain):
    inner = grad * gain
    return scale * (
        inner
        - jnp.mean(inner, axis=-1, keepdims=True)
        - normal * jnp.mean(inner * normal, axis=-1, keepdims=True)
    )


def erf_parts(gate):
    bell = jnp.exp(-0.5 * gate * gate)
    size = jnp.abs(gate) * (1.0 / math.sqrt(2.0))
    t = 1.0 / (1.0 + 0.3275911 * size)
    poly = t * (
        0.254829592
        + t * (-0.284496736 + t * (1.421413741 + t * (-1.453152027 + t * 1.061405429)))
    )
    tail = poly * bell
    return jnp.where(gate < 0.0, tail - 1.0, 1.0 - tail), bell


def gelu_parts(gate):
    erf, bell = erf_parts(gate)
    share = 0.5 + 0.5 * erf
    return gate * share, share + gate * bell * (1.0 / math.sqrt(2.0 * math.pi))


PIECE = 256
PIECES = FF_INNER // PIECE


def feed_forward(inputs, w_up_ref, down_of):
    total = None
    for piece in range(PIECES):
        units = slice(piece * PIECE, (piece + 1) * PIECE)
        gates = slice(FF_INNER + piece * PIECE, FF_INNER + (piece + 1) * PIECE)
        value = dot(inputs, w_up_ref[:, units])
        inner = to_low(value * gelu_parts(dot(inputs, w_up_ref[:, gates]))[0])
        part = down_of(inner, units)
        total = part if total is None else total + part
    return total


def lane_halves(values):
    lane = lax.broadcasted_iota(jnp.int32, values.shape, 1)
    zero = jnp.zeros_like(values)
    return jnp.concatenate(
        [jnp.where(lane < SLOT, values, zero), jnp.where(lane < SLOT, zero, values)], axis=0
    )


def key_bias(count, queries_first):
    shape = (GROUP, 2 * GROUP) if queries_first else (2 * GROUP, GROUP)
    row = lax.broadcasted_iota(jnp.int32, shape, 0)
    column = lax.broadcasted_iota(jnp.int32, shape, 1)
    key = (column if queries_first else row) % GROUP
    valid = (row % 8 == column % 8) & ((key // 8).astype(F32) < count)
    return jnp.where(valid, 0.0, -1e30).astype(F32)


def attend_chunk(qkv, bias):
    out = []
    for group in range(GROUPS):
        rows = slice(group * GROUP, (group + 1) * GROUP)
        pairs = []
        for pair in range(HEADS // 2):
            lanes = pair * 2 * SLOT
            queries = qkv[rows, lanes : lanes + GROUP]
            keys = lane_halves(qkv[rows, SLOTS + lanes : SLOTS + lanes + GROUP])
            values = lane_halves(qkv[rows, 2 * SLOTS + lanes : 2 * SLOTS + lanes + GROUP])
            scores = dot_nt(queries, keys) * SCALE + bias
            probs = []
            for part in (scores[:, :GROUP], scores[:, GROUP:]):
                raised = jnp.exp(part - jnp.max(part, axis=1, keepdims=True))
                probs.append(raised * (1.0 / jnp.sum(raised, axis=1, keepdims=True)))
            pairs.append(to_low(dot(to_low(jnp.concatenate(probs, axis=1)), values)))
        out.append(jnp.concatenate(pairs, axis=1))
    return jnp.concatenate(out, axis=0)


def motion_forward_kernel(
    facts_ref, arrived_ref, codes_ref, vec_ref, w_in_ref, w_qkv_ref, w_o_ref, w_up_ref, w_down_ref, w_out_ref,
    branch_ref, u_ref, u2_ref, u3_ref, qkv1_ref, qkv2_ref, o1_ref, o2_ref, last_ref,
    wide,
):
    def vec(i):
        return vec_ref[i : i + 1, :]

    unpack_positions(arrived_ref, wide)
    bias = key_bias(facts_ref[0, COUNT], True)
    codes = every_group(codes_ref[...])
    inputs = to_low(tokens_of(wide) * vec(0) + vec(1))
    stream = dot(inputs, w_in_ref[...]) + vec(2)
    for index, (first, x_ref, qkv_ref, o_ref) in enumerate(
        ((3, u_ref, qkv1_ref, o1_ref), (6, u2_ref, qkv2_ref, o2_ref))
    ):
        x_ref[...] = stream
        a = to_low(normal_parts(stream)[0] * vec(first) + vec(first + 1) + codes)
        qkv = to_low(dot(a, w_qkv_ref[index]))
        qkv_ref[...] = qkv
        mixture = attend_chunk(qkv, bias)
        o_ref[...] = mixture
        stream = stream + (dot(mixture, w_o_ref[index]) + vec(first + 2))
    u3_ref[...] = stream
    c = to_low(normal_parts(stream)[0] * vec(9) + vec(10))
    fed = feed_forward(c, w_up_ref, lambda inner, units: dot(inner, w_down_ref[units, :]))
    last = to_low(stream + (fed + vec(11)))
    last_ref[...] = last
    put_tokens(wide, (dot(last, w_out_ref[...]) + vec(12)) * facts_ref[0, KEEP])
    pack_positions(wide, branch_ref)


def motion_forward(facts, arrived, weights, vectors):
    outs = [((CLIP, 160, 128), BF16)] + [((PIX, WIDTH), F32)] * 3 + [((PIX, 3 * SLOTS), BF16)] * 2
    outs = outs + [((PIX, SLOTS), BF16)] * 2 + [((PIX, WIDTH), BF16)]
    operands = (facts, arrived, frame_codes(), vectors) + tuple(
        weights[name] for name in ("in", "qkv", "o", "up", "down", "out")
    )
    return call(
        motion_forward_kernel, operands, outs, "motion_forward", 23, 1, [pltpu.VMEM((CLIP, OWN, WIDTH), F32)]
    )


def prepare_kernel(sq_ref, up_ref, down_ref, sel_ref, w_in, w_qkv, w_o, w_up, w_down, w_out, t_in, t_qkv1, t_qkv2, t_o1, t_o2, t_up, t_down, t_out):
    sel = sel_ref[...]
    low = [to_low(sq_ref[i]) for i in range(10)]
    w_in[...] = low[0]
    t_in[...] = low[0].T
    w_out[...] = low[9]
    t_out[...] = low[9].T
    for index, (first, t_qkv, t_o) in enumerate(((1, t_qkv1, t_o1), (5, t_qkv2, t_o2))):
        for j in range(3):
            padded = to_low(dot(low[first + j], sel))
            w_qkv[index, :, j * SLOTS : (j + 1) * SLOTS] = padded
            t_qkv[j * SLOTS : (j + 1) * SLOTS, :] = padded.T
        padded = to_low(dot_nt(low[first + 3].T, sel.T))
        t_o[...] = padded
        w_o[index] = padded.T
    up = to_low(up_ref[...])
    w_up[...] = up
    t_up[...] = up.T
    down = to_low(down_ref[...])
    t_down[...] = down
    w_down[...] = down.T


def prepare(squares, up, down):
    shapes = {
        "in": (WIDTH, WIDTH), "qkv": (2, WIDTH, 3 * SLOTS), "o": (2, SLOTS, WIDTH), "up": (WIDTH, 2 * FF_INNER),
        "down": (FF_INNER, WIDTH), "out": (WIDTH, WIDTH),
        "in_t": (WIDTH, WIDTH), "qkv1_t": (3 * SLOTS, WIDTH), "qkv2_t": (3 * SLOTS, WIDTH),
        "o1_t": (WIDTH, SLOTS), "o2_t": (WIDTH, SLOTS), "up_t": (2 * FF_INNER, WIDTH),
        "down_t": (WIDTH, FF_INNER), "out_t": (WIDTH, WIDTH),
    }
    made = call(
        prepare_kernel, (squares, up, down, slot_selector()), [(x, BF16) for x in shapes.values()], "motion_weights", 9
    )
    return dict(zip(shapes, made))


def column_sum(values):
    return jnp.sum(values, axis=0, keepdims=True)


def anywhere():
    return pl.BlockSpec(memory_space=pl.ANY)


def feed_backward_kernel(
    core_ref, facts_ref, grad_ref, u3_ref, vec_ref, w_up_ref, t_down_ref, t_out_ref,
    dz_ref, du4_ref, dbranch_ref, own_ref, other_ref,
    wide, dz_here, leaving,
):
    unpack_positions(grad_ref, wide)
    dbranch = to_low(tokens_of(wide) * facts_ref[0, KEEP])
    dbranch_ref[...] = dbranch
    du4 = dot(dbranch, t_out_ref[...])
    du4_ref[...] = du4
    d4 = to_low(du4)
    c = to_low(normal_parts(u3_ref[...])[0] * vec_ref[9:10, :] + vec_ref[10:11, :])
    z = dot(c, w_up_ref[...])
    value = z[:, :FF_INNER]
    gelu, slope = gelu_parts(z[:, FF_INNER:])
    inner = to_low(value * gelu)
    dinner = dot(d4, t_down_ref[...])
    dz = to_low(jnp.concatenate([dinner * gelu, dinner * value * slope], axis=1))
    dz_here[...] = dz
    copy = pltpu.make_async_copy(dz_here, dz_ref, leaving)
    copy.start()
    g_down = dot_tn(d4, inner)
    g_up = dot_tn(c, dz)
    bound = jnp.maximum(jnp.max(jnp.abs(g_up)), jnp.max(jnp.abs(g_down)))

    def put(ref, half):
        for tile in range(UP_TILES):
            start = half * FF_INNER + tile * 128
            ref[tile_rows(tile)] = g_up[:, start : start + 128]
        for tile in range(DOWN_TILES):
            start = half * (FF_INNER // 2) + tile * 128
            ref[tile_rows(UP_TILES + tile)] = g_down[:, start : start + 128]
        used = (UP_TILES + DOWN_TILES) * WIDTH
        ref[used:] = jnp.full((EARLY_ROWS - used, 128), bound)

    for core in range(2):

        @pl.when(core_ref[0] == core)
        def _(core=core):
            put(own_ref, core)
            put(other_ref, 1 - core)

    copy.wait()


def feed_backward(core, facts, grad, weights, vectors, u3):
    operands = (core, facts, grad, u3, vectors) + tuple(weights[n] for n in ("up", "down_t", "out_t"))
    outs = [((PIX, 2 * FF_INNER), BF16), ((PIX, WIDTH), F32), ((PIX, WIDTH), BF16)] + [((EARLY_ROWS, 128), F32)] * 2
    return pl.pallas_call(
        feed_backward_kernel,
        in_specs=[in_smem()] * 2 + [in_vmem()] * (len(operands) - 2),
        out_specs=[anywhere()] + [in_vmem()] * 4,
        out_shape=[jax.ShapeDtypeStruct(*out) for out in outs],
        scratch_shapes=[
            pltpu.VMEM((CLIP, OWN, WIDTH), F32),
            pltpu.VMEM((PIX, 2 * FF_INNER), BF16),
            pltpu.SemaphoreType.DMA,
        ],
        cost_estimate=pl.CostEstimate(flops=int(15 * 1.1e9), bytes_accessed=0, transcendentals=0),
        compiler_params=pltpu.CompilerParams(vmem_limit_bytes=60 * 2**20),
        name="feed_backward",
    )(*operands)


def upper_backward_kernel(
    vec_ref, t_up_at, dz_at, du4_at, u3_at, dbranch_at, last_at,
    du3_ref, g_out_ref, g_vec_ref,
    t_up, dz, du4_here, u3_here, dbranch_here, last_here, coming,
):
    size = PIX // 4
    pairs = [(t_up_at, t_up)]
    for part in range(4):
        rows = slice(part * size, (part + 1) * size)
        pairs.append((dz_at.at[rows], dz.at[rows]))
    pairs += [(du4_at, du4_here), (u3_at, u3_here), (dbranch_at, dbranch_here), (last_at, last_here)]
    arrivals = [pltpu.make_async_copy(x, y, coming.at[k]) for k, (x, y) in enumerate(pairs)]
    for copy in arrivals:
        copy.start()
    arrivals[0].wait()
    parts = []
    for part in range(4):
        arrivals[part + 1].wait()
        parts.append(dot(dz[part * size : (part + 1) * size, :], t_up[...]))
    dc = jnp.concatenate(parts, axis=0)
    for copy in arrivals[5:]:
        copy.wait()
    du4 = du4_here[...]
    dbranch = dbranch_here[...]
    normal, scale = normal_parts(u3_here[...])
    du3_ref[...] = du4 + normal_back(dc, normal, scale, vec_ref[9:10, :])
    g_out_ref[...] = dot_tn(last_here[...], dbranch)
    sums = [column_sum(dc * normal), column_sum(dc), column_sum(to_low(du4).astype(F32)), column_sum(dbranch.astype(F32))]
    g_vec_ref[...] = jnp.concatenate(sums + [jnp.zeros((4, WIDTH), F32)], axis=0)


def upper_backward(dz, du4, dbranch, u3, last, vectors, weights):
    moved = (weights["up_t"], dz, du4, u3, dbranch, last)
    outs = [((PIX, WIDTH), F32), ((WIDTH, WIDTH), F32), ((8, WIDTH), F32)]
    return pl.pallas_call(
        upper_backward_kernel,
        in_specs=[in_vmem()] + [anywhere()] * len(moved),
        out_specs=[in_vmem()] * 3,
        out_shape=[jax.ShapeDtypeStruct(*out) for out in outs],
        scratch_shapes=[pltpu.VMEM(x.shape, x.dtype) for x in moved] + [pltpu.SemaphoreType.DMA((9,))],
        cost_estimate=pl.CostEstimate(flops=int(6 * 1.1e9), bytes_accessed=0, transcendentals=0),
        compiler_params=pltpu.CompilerParams(vmem_limit_bytes=60 * 2**20),
        name="upper_backward",
    )(vectors, *moved)


def attend_back_chunk(qkv, d_mixture, bias):
    out = []
    for group in range(GROUPS):
        rows = slice(group * GROUP, (group + 1) * GROUP)
        grads = [[], [], []]
        for pair in range(HEADS // 2):
            lanes = pair * 2 * SLOT
            queries = qkv[rows, lanes : lanes + GROUP]
            keys = lane_halves(qkv[rows, SLOTS + lanes : SLOTS + lanes + GROUP])
            values = lane_halves(qkv[rows, 2 * SLOTS + lanes : 2 * SLOTS + lanes + GROUP])
            d_out = d_mixture[rows, lanes : lanes + GROUP]
            scores = dot_nt(keys, queries) * SCALE + bias
            d_probs = dot_nt(values, d_out)
            low_probs = []
            d_scores = []
            for head in range(2):
                part = scores[head * GROUP : (head + 1) * GROUP]
                d_part = d_probs[head * GROUP : (head + 1) * GROUP]
                raised = jnp.exp(part - jnp.max(part, axis=0, keepdims=True))
                probs = raised * (1.0 / jnp.sum(raised, axis=0, keepdims=True))
                low_probs.append(to_low(probs))
                d_scores.append(to_low(probs * (d_part - jnp.sum(probs * d_part, axis=0, keepdims=True))))
            low_probs = jnp.concatenate(low_probs, axis=0)
            d_scores = jnp.concatenate(d_scores, axis=0)
            d_values = dot(low_probs, d_out)
            d_keys = dot(d_scores, queries) * SCALE
            d_queries = dot_tn(d_scores, keys) * SCALE
            lane = lax.broadcasted_iota(jnp.int32, (GROUP, GROUP), 1)
            grads[0].append(to_low(d_queries))
            grads[1].append(to_low(jnp.where(lane < SLOT, d_keys[:GROUP], d_keys[GROUP:])))
            grads[2].append(to_low(jnp.where(lane < SLOT, d_values[:GROUP], d_values[GROUP:])))
        out.append(jnp.concatenate(grads[0] + grads[1] + grads[2], axis=1))
    return jnp.concatenate(out, axis=0)


def attention_backward(count, grad, stream, qkv, gain, t_o, t_qkv):
    d_out = to_low(grad)
    d_mixture = to_low(dot(d_out, t_o))
    d_qkv = attend_back_chunk(qkv, d_mixture, key_bias(count, False))
    normal, scale = normal_parts(stream)
    d_a = dot(d_qkv, t_qkv)
    rows = [column_sum(d_a * normal), column_sum(d_a), column_sum(d_out.astype(F32))]
    return grad + normal_back(d_a, normal, scale, gain), d_qkv, rows


def second_backward_kernel(
    facts_ref, grad_ref, u2_ref, qkv_ref, vec_ref, t_o_ref, t_qkv_ref,
    du2_ref, d_qkv_ref, g_vec_ref,
):
    du2, d_qkv, rows = attention_backward(
        facts_ref[0, COUNT], grad_ref[...], u2_ref[...], qkv_ref[...], vec_ref[6:7, :], t_o_ref[...], t_qkv_ref[...]
    )
    du2_ref[...] = du2
    d_qkv_ref[...] = d_qkv
    g_vec_ref[...] = jnp.concatenate(rows + [jnp.zeros((5, WIDTH), F32)], axis=0)


def second_backward(grad, facts, weights, vectors, u2, qkv):
    operands = (facts, grad, u2, qkv, vectors, weights["o2_t"], weights["qkv2_t"])
    outs = [((PIX, WIDTH), F32), ((PIX, 3 * SLOTS), BF16), ((8, WIDTH), F32)]
    return call(second_backward_kernel, operands, outs, "second_backward", 15, 1, limit=36)


def first_backward_kernel(
    facts_ref, grad_ref, u_ref, qkv_ref, arrived_ref, vec_ref, t_o_ref, t_qkv_ref, t_in_ref,
    du_ref, d_qkv_ref, g_vec_ref,
    wide,
):
    unpack_positions(arrived_ref, wide)
    du, d_qkv, rows = attention_backward(
        facts_ref[0, COUNT], grad_ref[...], u_ref[...], qkv_ref[...], vec_ref[3:4, :], t_o_ref[...], t_qkv_ref[...]
    )
    du = to_low(du)
    du_ref[...] = du
    d_qkv_ref[...] = d_qkv
    d_inputs = dot(du, t_in_ref[...])
    top = [column_sum(d_inputs * tokens_of(wide)), column_sum(d_inputs), column_sum(du.astype(F32))]
    g_vec_ref[...] = jnp.concatenate(top + rows + [jnp.zeros((2, WIDTH), F32)], axis=0)


def first_backward(grad, facts, arrived, weights, vectors, u, qkv):
    operands = (facts, grad, u, qkv, arrived, vectors, weights["o1_t"], weights["qkv1_t"], weights["in_t"])
    outs = [((PIX, WIDTH), BF16), ((PIX, 3 * SLOTS), BF16), ((8, WIDTH), F32)]
    return call(
        first_backward_kernel, operands, outs, "first_backward", 17, 1, [pltpu.VMEM((CLIP, OWN, WIDTH), F32)], limit=36
    )


def attention_grads(grad, stream, d_qkv, mixture, codes, gain, offset, sel_t):
    padded = dot_tn(mixture, to_low(grad))
    w_o_grad = jnp.concatenate([padded[head * SLOT : head * SLOT + HEAD_DIM] for head in range(HEADS)], axis=0)
    a = to_low(normal_parts(stream)[0] * gain + offset + every_group(codes))
    grads = []
    for j in range(3):
        tight = to_low(dot(d_qkv[:, j * SLOTS : (j + 1) * SLOTS], sel_t))
        grads.append(dot_tn(a, tight))
    return grads + [w_o_grad]


def second_grads_kernel(grad_ref, u2_ref, d_qkv_ref, o_ref, codes_ref, vec_ref, sel_t_ref, gq_ref, gk_ref, gv_ref, go_ref):
    grads = attention_grads(
        grad_ref[...], u2_ref[...], d_qkv_ref[...], o_ref[...], codes_ref[...], vec_ref[6:7, :], vec_ref[7:8, :], sel_t_ref[...]
    )
    for ref, value in zip((gq_ref, gk_ref, gv_ref, go_ref), grads):
        ref[...] = value


def second_grads(grad, vectors, u2, d_qkv, mixture):
    operands = (grad, u2, d_qkv, mixture, frame_codes(), vectors, slot_selector().T)
    return call(second_grads_kernel, operands, [((WIDTH, WIDTH), F32)] * 4, "second_grads", 7, limit=36)


def first_grads_kernel(
    core_ref, facts_ref, loss_ref, grad_ref, u_ref, d_qkv_ref, o_ref, du_ref, arrived_ref, codes_ref, vec_ref, sel_t_ref,
    g5_ref, g6_ref, g7_ref, g8_ref, g9_ref, feed_vec_ref, second_vec_ref, first_vec_ref,
    own_ref, other_ref,
    wide,
):
    unpack_positions(arrived_ref, wide)
    grads = attention_grads(
        grad_ref[...], u_ref[...], d_qkv_ref[...], o_ref[...], codes_ref[...], vec_ref[3:4, :], vec_ref[4:5, :], sel_t_ref[...]
    )
    inputs = to_low(tokens_of(wide) * vec_ref[0:1, :] + vec_ref[1:2, :])
    later = [ref[...] for ref in (g5_ref, g6_ref, g7_ref, g8_ref, g9_ref)]
    squares = [dot_tn(inputs, du_ref[...])] + grads + later
    vector_rows = jnp.concatenate(
        [first_vec_ref[0:6, :], second_vec_ref[0:3, :], feed_vec_ref[0:4, :], jnp.full((3, WIDTH), loss_ref[0, 0] / (1024.0 * facts_ref[0, TOTAL]))], axis=0
    )
    bound = jnp.max(jnp.abs(vector_rows))
    for square in squares:
        bound = jnp.maximum(bound, jnp.max(jnp.abs(square)))
    pieces = [vector_rows[:, 64 * j : 64 * (j + 1)] for j in range(5)]
    side = jnp.concatenate(pieces + [jnp.zeros((WIDTH - 80, 64), F32)], axis=0)

    def put(ref, half):
        own = squares[5 * half : 5 * half + 5]
        for index in range(5):
            ref[tile_rows(2 * index)] = own[index][:, 0:128]
            ref[tile_rows(2 * index + 1)] = own[index][:, 128:256]
        for pair in range(2):
            ref[tile_rows(10 + pair)] = jnp.concatenate([own[2 * pair][:, 256:320], own[2 * pair + 1][:, 256:320]], axis=1)
        ref[tile_rows(12)] = jnp.concatenate([own[4][:, 256:320], side], axis=1)
        ref[13 * WIDTH :] = jnp.full((LATE_ROWS - 13 * WIDTH, 128), bound)

    for core in range(2):

        @pl.when(core_ref[0] == core)
        def _(core=core):
            put(own_ref, core)
            put(other_ref, 1 - core)


def first_grads(core, facts, loss_part, grad, arrived, vectors, u, d_qkv, mixture, du, later):
    operands = (
        core, facts, loss_part, grad, u, d_qkv, mixture, du, arrived, frame_codes(), vectors, slot_selector().T,
    ) + tuple(later)
    outs = [((LATE_ROWS, 128), F32)] * 2
    return call(first_grads_kernel, operands, outs, "first_grads", 10, 3, [pltpu.VMEM((CLIP, OWN, WIDTH), F32)], limit=44)


MUON_RATE = 0.2
ADAM_RATE = 0.4
DECAY = 0.01
AVERAGE = 0.75
STEP = 10
SHRINK = 1.0 - MUON_RATE * DECAY
SQUARE_RATE = MUON_RATE * 0.2 * math.sqrt(WIDTH)
UP_RATE = MUON_RATE * 0.2 * math.sqrt(2 * FF_INNER)
DOWN_RATE = MUON_RATE * 0.2 * math.sqrt(FF_INNER)
UP_TILES = 10
DOWN_TILES = 5
WIDE_TILES = 2 * UP_TILES
EARLY_ROWS = 4864 + 16
LATE_ROWS = 4224 + 16


def tile_rows(index):
    return slice(index * WIDTH, (index + 1) * WIDTH)


def halves(values):
    high = values.astype(BF16)
    return (high, (values - high.astype(F32)).astype(BF16))


def triple(left, right):
    stacked = jnp.concatenate([left[0], left[0], left[1]], axis=1)
    return dot(stacked, jnp.concatenate([right[0], right[1], right[0]], axis=0))


def gram_of(parts):
    high, low = parts
    half = dot_nt(jnp.concatenate([high, high], axis=1), jnp.concatenate([high * 0.5, low], axis=1))
    return half + half.T


def scaled_to_unit(matrix):
    return matrix * (1.0 / (jnp.sqrt(jnp.sum(matrix * matrix, keepdims=True)) + 1e-07))


def wide_moments_kernel(sum_ref, up_ref, down_ref, up_new_ref, down_new_ref, ahead_ref):
    for tile in range(UP_TILES):
        lanes = slice(128 * tile, 128 * (tile + 1))
        gradient = sum_ref[tile_rows(tile)]
        moment = 0.95 * up_ref[:, lanes] + gradient
        up_new_ref[:, lanes] = moment
        ahead_ref[tile] = gradient + 0.95 * moment
    for tile in range(DOWN_TILES):
        lanes = slice(128 * tile, 128 * (tile + 1))
        gradient = sum_ref[tile_rows(UP_TILES + tile)]
        moment = 0.95 * down_ref[:, lanes] + gradient
        down_new_ref[:, lanes] = moment
        ahead_ref[UP_TILES + tile] = gradient + 0.95 * moment


def wide_moments(summed, up_moment, down_moment):
    outs = [up_moment.shape, down_moment.shape, (UP_TILES + DOWN_TILES, WIDTH, 128)]
    return call(
        wide_moments_kernel, (summed, up_moment, down_moment), [(x, F32) for x in outs], "wide_moments", 4, limit=32
    )


def wide_direction_kernel(core_ref, own_ref, got_ref, o_ref, matrix):
    def put(tile, value):
        matrix[:, 128 * tile : 128 * (tile + 1)] = value

    @pl.when(core_ref[0] == 0)
    def _():
        for tile in range(UP_TILES):
            put(tile, own_ref[tile])
            put(UP_TILES + tile, got_ref[tile])

    @pl.when(core_ref[0] != 0)
    def _():
        for tile in range(DOWN_TILES):
            put(tile, got_ref[UP_TILES - DOWN_TILES + tile])
            put(DOWN_TILES + tile, own_ref[UP_TILES + tile])
        matrix[:, 128 * UP_TILES :] = jnp.zeros((WIDTH, 128 * UP_TILES), F32)

    parts = halves(scaled_to_unit(matrix[...]))
    gram = gram_of(parts)
    row = lax.broadcasted_iota(jnp.int32, (WIDTH, WIDTH), 0)
    column = lax.broadcasted_iota(jnp.int32, (WIDTH, WIDTH), 1)
    total = None
    for step in range(5):
        gram_parts = halves(gram)
        polynomial = -4.775 * gram + 2.0315 * gram_of(gram_parts)
        poly_parts = halves(polynomial)
        if total is None:
            total = polynomial + jnp.where(row == column, 3.4445, 0.0)
        else:
            total = 3.4445 * total + triple(poly_parts, halves(total))
        if step < 4:
            once = 3.4445 * gram + triple(poly_parts, gram_parts)
            gram = 3.4445 * once + triple(halves(once), poly_parts)
    direction = to_low(triple(halves(total), parts))
    for tile in range(WIDE_TILES):
        o_ref[tile] = direction[:, 128 * tile : 128 * (tile + 1)]


def wide_direction(core, own, got):
    outs = [((WIDE_TILES, WIDTH, 128), BF16)]
    return call(
        wide_direction_kernel, (core, own, got), outs, "wide_direction", 16, 1, [pltpu.VMEM((WIDTH, 128 * WIDE_TILES), F32)], limit=40
    )[0]


def wide_update_kernel(
    core_ref, own_ref, got_ref, up_ref, down_ref, up_ema_ref, down_ema_ref,
    up_new_ref, up_ema_new_ref, down_new_ref, down_ema_new_ref,
):
    def update(up_dir, down_dir):
        for tile in range(WIDE_TILES):
            lanes = slice(128 * tile, 128 * (tile + 1))
            up_new_ref[:, lanes] = up_ref[:, lanes] * SHRINK - UP_RATE * up_dir[tile].astype(F32)
        for tile in range(2 * DOWN_TILES):
            lanes = slice(128 * tile, 128 * (tile + 1))
            down_new_ref[:, lanes] = down_ref[:, lanes] * SHRINK - DOWN_RATE * down_dir[tile].astype(F32)

    def average(half):
        lanes = slice(128 * UP_TILES * half, 128 * UP_TILES * (half + 1))
        up_ema_new_ref[...] = AVERAGE * up_ema_ref[...] + (1.0 - AVERAGE) * up_new_ref[:, lanes]
        lanes = slice(128 * DOWN_TILES * half, 128 * DOWN_TILES * (half + 1))
        down_ema_new_ref[...] = AVERAGE * down_ema_ref[...] + (1.0 - AVERAGE) * down_new_ref[:, lanes]

    @pl.when(core_ref[0] == 0)
    def _():
        update(own_ref, got_ref)
        average(0)

    @pl.when(core_ref[0] != 0)
    def _():
        update(got_ref, own_ref)
        average(1)


def wide_update(core, own, got, up, down, up_ema, down_ema):
    outs = [(x.shape, F32) for x in (up, up_ema, down, down_ema)]
    return call(wide_update_kernel, (core, own, got, up, down, up_ema, down_ema), outs, "wide_update", 7, 1)


class Inward:
    def __init__(self, source, target, semaphore):
        self.copy = pltpu.make_async_copy(source, target, semaphore)
        self.target = target
        self.state = 0

    def begin(self):
        self.copy.start()
        self.state = 1

    def ready(self):
        if self.state == 1:
            self.copy.wait()
            self.state = 2
        return self.target

    def __getitem__(self, index):
        return self.ready()[index]


def squares_step(current, passes):
    def symmetric(values, count):
        if count == 1:
            low = [to_low(x) for x in values]
            return [dot_nt(x, x) for x in low]
        return [gram_of(halves(x)) for x in values]

    grams = symmetric(current, passes[0])
    squared = symmetric(grams, passes[1])
    polynomials = [-4.775 * gram + 2.0315 * square for gram, square in zip(grams, squared)]
    if passes[2] == 1:
        moved = [dot(to_low(p), to_low(x)) for p, x in zip(polynomials, current)]
    else:
        moved = [triple(halves(p), halves(x)) for p, x in zip(polynomials, current)]
    return [3.4445 * x + y for x, y in zip(current, moved)]


DIRECTION_OUTS = 7


def directions_kernel(sums, *refs):
    count = 5
    sources, refs = refs[:count], refs[count:]
    targets, refs = refs[:DIRECTION_OUTS], refs[DIRECTION_OUTS:]
    inner, refs = refs[:count], refs[count:]
    outer, refs = refs[:DIRECTION_OUTS], refs[DIRECTION_OUTS:]
    coming, going, matrix = refs
    inputs = [Inward(x, y, coming.at[i]) for i, (x, y) in enumerate(zip(sources, inner))]
    moment_ref, m1_ref, m2_ref, vec_ref, vec_ema_ref = inputs
    leaving = [pltpu.make_async_copy(x, y, going.at[i]) for i, (x, y) in enumerate(zip(outer, targets))]
    direction_ref, moment_new_ref, m1_new_ref, m2_new_ref, vec_new_ref, vec_ema_new_ref, loss_ref = outer
    for value in inputs:
        value.begin()

    side = sums[tile_rows(12)][:, 64:128]
    rows = jnp.concatenate([side[16 * j : 16 * (j + 1)] for j in range(5)], axis=1)
    loss_ref[...] = rows[13:14, 0:128]
    gradient = rows[0:13]
    first = 0.9 * m1_ref[...] + 0.1 * gradient
    second = 0.999 * m2_ref[...] + 0.001 * (gradient * gradient)
    m1_new_ref[...] = first
    m2_new_ref[...] = second
    adjusted = first * (1.0 / (1.0 - 0.9**STEP)) / (jnp.sqrt(second * (1.0 / (1.0 - 0.999**STEP))) + 1e-08)
    fresh = vec_ref[...] - ADAM_RATE * (adjusted + DECAY * vec_ref[...])
    vec_new_ref[...] = fresh
    vec_ema_new_ref[...] = AVERAGE * vec_ema_ref[...] + (1.0 - AVERAGE) * fresh
    for index in range(5):
        lanes = slice(64 * (index % 2), 64 * (index % 2) + 64)
        gradient = jnp.concatenate(
            [sums[tile_rows(2 * index)], sums[tile_rows(2 * index + 1)], sums[tile_rows(10 + index // 2)][:, lanes]], axis=1
        )
        moment = 0.95 * moment_ref[index] + gradient
        moment_new_ref[index] = moment
        matrix[index] = scaled_to_unit(gradient + 0.95 * moment)
    for copy in leaving[1:7]:
        copy.start()

    def advance(passes):
        moved = squares_step([matrix[index] for index in range(5)], passes)
        for index in range(5):
            matrix[index] = moved[index]

    advance((1, 1, 1))
    advance((1, 1, 1))
    advance((3, 1, 3))
    advance((3, 3, 3))
    advance((3, 3, 3))
    direction_ref[...] = to_low(matrix[...])
    leaving[0].start()
    for copy in leaving:
        copy.wait()


def directions(summed, moment, m1, m2, vectors, vec_ema):
    operands = (moment, m1, m2, vectors, vec_ema)
    outs = [(moment.shape, BF16), (moment.shape, F32)] + [(vectors.shape, F32)] * 4 + [((1, 128), F32)]
    return pl.pallas_call(
        directions_kernel,
        in_specs=[in_vmem()] + [anywhere()] * len(operands),
        out_specs=[anywhere()] * len(outs),
        out_shape=[jax.ShapeDtypeStruct(*out) for out in outs],
        scratch_shapes=[pltpu.VMEM(x.shape, x.dtype) for x in operands]
        + [pltpu.VMEM(*out) for out in outs]
        + [pltpu.SemaphoreType.DMA((len(operands),)), pltpu.SemaphoreType.DMA((len(outs),))]
        + [pltpu.VMEM(moment.shape, F32)],
        cost_estimate=pl.CostEstimate(flops=int(22 * 1.1e9), bytes_accessed=0, transcendentals=0),
        compiler_params=pltpu.CompilerParams(vmem_limit_bytes=46 * 2**20),
        name="directions",
    )(summed, *operands)


def own_squares_kernel(core_ref, own_ref, weight_ref, ema_ref, new_ref, ema_new_ref, own, weight, ema, new, ema_new, coming, going):
    core = core_ref[0]
    arrivals = []
    for j in range(5):
        pairs = ((weight_ref.at[core, j], weight.at[j]), (own_ref.at[j], own.at[j]), (ema_ref.at[j], ema.at[j]))
        arrivals.append([pltpu.make_async_copy(x, y, coming.at[i, j]) for i, (x, y) in enumerate(pairs)])
    for copies in arrivals:
        for copy in copies:
            copy.start()
    leaving = []
    for j in range(5):
        for copy in arrivals[j]:
            copy.wait()
        fresh = weight[j] * SHRINK - SQUARE_RATE * own[j].astype(F32)
        new[j] = fresh
        ema_new[j] = AVERAGE * ema[j] + (1.0 - AVERAGE) * fresh
        for i, (x, y) in enumerate(((new.at[j], new_ref.at[core, j]), (ema_new.at[j], ema_new_ref.at[j]))):
            leaving.append(pltpu.make_async_copy(x, y, going.at[i, j]))
            leaving[-1].start()
    for copy in leaving:
        copy.wait()


def own_squares(core, own, weights, ema):
    square = (5, WIDTH, WIDTH)
    return pl.pallas_call(
        own_squares_kernel,
        in_specs=[in_smem()] + [anywhere()] * 3,
        out_specs=[anywhere()] * 2,
        out_shape=[jax.ShapeDtypeStruct((2,) + square, F32), jax.ShapeDtypeStruct(square, F32)],
        scratch_shapes=[pltpu.VMEM(square, BF16)]
        + [pltpu.VMEM(square, F32)] * 4
        + [pltpu.SemaphoreType.DMA((3, 5)), pltpu.SemaphoreType.DMA((2, 5))],
        cost_estimate=pl.CostEstimate(flops=int(4 * 1.1e9), bytes_accessed=0, transcendentals=0),
        compiler_params=pltpu.CompilerParams(vmem_limit_bytes=60 * 2**20),
        name="own_squares",
    )(core, own, weights, ema)


def other_squares_kernel(core_ref, got_ref, weight_ref, begun_ref, new_ref, got, weight, new, coming, going):
    other = 1 - core_ref[0]
    arrivals = []
    for j in range(5):
        pairs = ((weight_ref.at[other, j], weight.at[j]), (got_ref.at[j], got.at[j]))
        arrivals.append([pltpu.make_async_copy(x, y, coming.at[i, j]) for i, (x, y) in enumerate(pairs)])
    for copies in arrivals:
        for copy in copies:
            copy.start()
    leaving = []
    for j in range(5):
        for copy in arrivals[j]:
            copy.wait()
        new[j] = weight[j] * SHRINK - SQUARE_RATE * got[j].astype(F32)
        leaving.append(pltpu.make_async_copy(new.at[j], new_ref.at[other, j], going.at[j]))
        leaving[-1].start()
    for copy in leaving:
        copy.wait()


def other_squares(core, got, weights, begun):
    square = (5, WIDTH, WIDTH)
    return pl.pallas_call(
        other_squares_kernel,
        in_specs=[in_smem()] + [anywhere()] * 3,
        out_specs=anywhere(),
        out_shape=jax.ShapeDtypeStruct(begun.shape, F32),
        input_output_aliases={3: 0},
        scratch_shapes=[pltpu.VMEM(square, BF16)]
        + [pltpu.VMEM(square, F32)] * 2
        + [pltpu.SemaphoreType.DMA((2, 5)), pltpu.SemaphoreType.DMA((5,))],
        cost_estimate=pl.CostEstimate(flops=int(3 * 1.1e9), bytes_accessed=0, transcendentals=0),
        compiler_params=pltpu.CompilerParams(vmem_limit_bytes=60 * 2**20),
        name="other_squares",
    )(core, got, weights, begun)


TAPS = 9
CHAN = 4


def group_ones():
    group = np.arange(WIDTH) // (WIDTH // GN_GROUPS)
    return jnp.asarray((group[:, None] == group[None, :]).astype(np.float32), BF16)


def group_mean(column_sums, ones):
    rest = jnp.broadcast_to(column_sums, (8, WIDTH))
    total = jnp.zeros((8, WIDTH), F32)
    for _ in range(3):
        part = to_low(rest)
        total = total + dot(part, ones)
        rest = rest - part.astype(F32)
    return total[0:1] * (1.0 / (PIX * (WIDTH // GN_GROUPS)))


def chunk_rows(index):
    return pl.ds(pl.multiple_of(index * CHUNK, CHUNK), CHUNK)


def over_chunks(body, *start):
    return lax.fori_loop(0, CHUNKS, lambda i, carry: body(i, *carry), start)


def zero_row():
    return jnp.zeros((1, WIDTH), F32)


def group_stats(ref, ones, column_sums):
    centre = group_mean(column_sums, ones)

    def squares(i, total):
        shifted = ref[chunk_rows(i), :] - centre
        return (total + column_sum(shifted * shifted),)

    (total,) = over_chunks(squares, zero_row())
    return centre, lax.rsqrt(group_mean(total, ones) + 1e-05)


def sigmoid(values):
    return 1.0 / (1.0 + jnp.exp(-values))


def shifted_lanes(values, down, right):
    lane = lax.broadcasted_iota(jnp.int32, values.shape, 1)
    line = lane // LATENT + down
    place = lane % LATENT + right
    inside = (line >= 0) & (line < LATENT) & (place >= 0) & (place < LATENT)
    offset = (down * LATENT + right) % PIX
    moved = pltpu.roll(values, (PIX - offset) % PIX, 1) if offset else values
    return jnp.where(inside, moved, 0.0)


def put_columns(cols_ref, act_ref):
    zeros = jnp.zeros((LATENT, 3 * WIDTH), BF16)
    cols_ref[0:LATENT, :] = zeros
    cols_ref[LATENT + PIX :, :] = zeros
    act_ref[0:8, :] = jnp.zeros((8, WIDTH), F32)
    act_ref[8 + PIX :, :] = jnp.zeros((8, WIDTH), F32)

    for i in range(CHUNKS):
        place = (lax.broadcasted_iota(jnp.int32, (CHUNK, WIDTH), 0)) % LATENT
        middle = act_ref[8 + i * CHUNK : 8 + (i + 1) * CHUNK, :]
        left = act_ref[7 + i * CHUNK : 7 + (i + 1) * CHUNK, :]
        right = act_ref[9 + i * CHUNK : 9 + (i + 1) * CHUNK, :]
        left = jnp.where(place == 0, 0.0, left)
        right = jnp.where(place == LATENT - 1, 0.0, right)
        cols_ref[LATENT + i * CHUNK : LATENT + (i + 1) * CHUNK, :] = jnp.concatenate(
            [to_low(left), to_low(middle), to_low(right)], axis=1
        )


def resnet_kernel(
    facts_ref, pair_ref, vec_ref, temb_ref, ones_ref, w_in_ref, w_res_ref, squares_ref,
    resnet_ref, tokens_ref,
    first, inner, act, cols,
):
    ones = ones_ref[...]

    def vec(i):
        return vec_ref[i : i + 1, :]

    pair = pair_ref[...].astype(F32)
    noisy = facts_ref[0, COS] * pair + facts_ref[0, SIN] * jnp.concatenate([pair[CHAN:], pair[:CHAN]], axis=0)
    columns = tap_rows([shifted_lanes(noisy, tap // 3 - 1, tap % 3 - 1)[:CHAN] for tap in range(TAPS)])
    w_in = tap_rows([w_in_ref[tap // 3, tap % 3] for tap in range(TAPS)])
    total = zero_row()
    for i in range(CHUNKS):
        part = dot_tn(columns[:, i * CHUNK : (i + 1) * CHUNK], w_in) + vec(0)
        first[i * CHUNK : (i + 1) * CHUNK, :] = part
        total = total + column_sum(part)

    def activate(source, total, gain, offset):
        centre, scale = group_stats(source, ones, total)

        def one(i):
            normal = (source[chunk_rows(i), :] - centre) * scale * gain + offset
            act[pl.ds(pl.multiple_of(8 + i * CHUNK, 8), CHUNK), :] = normal * sigmoid(normal)
            return ()

        over_chunks(lambda i: one(i))
        put_columns(cols, act)

    def convolve_chunk(i, which):
        out = None
        for line in range(3):
            part = cols[pl.ds(pl.multiple_of(i * CHUNK + LATENT * line, LATENT), CHUNK), :]
            term = dot(part, w_res_ref[which, line])
            out = term if out is None else out + term
        return out

    activate(first, total, vec(1), vec(2))
    shift = vec(3) + temb_ref[:, :WIDTH]

    def first_step(i, total):
        part = convolve_chunk(i, 0) + shift
        inner[chunk_rows(i), :] = part
        return (total + column_sum(part),)

    (total,) = over_chunks(first_step, zero_row())
    activate(inner, total, vec(4), vec(5))

    def second_step(i, total):
        part = first[chunk_rows(i), :] + (convolve_chunk(i, 1) + vec(6))
        resnet_ref[chunk_rows(i), :] = part
        return (total + column_sum(part),)

    (total,) = over_chunks(second_step, zero_row())
    centre, scale = group_stats(resnet_ref, ones, total)

    def token_step(i):
        normal = to_low((resnet_ref[chunk_rows(i), :] - centre) * scale * vec(7) + vec(8))
        tokens_ref[chunk_rows(i), :] = dot(normal, squares_ref[0]) + vec(9)
        return ()

    over_chunks(lambda i: token_step(i))


def resnet_block(facts, pair, vectors, w_in, w_res, squares):
    operands = (facts, pair, vectors, facts, group_ones(), w_in, w_res, squares)
    scratch = [
        pltpu.VMEM((PIX, WIDTH), F32),
        pltpu.VMEM((PIX, WIDTH), F32),
        pltpu.VMEM((PIX + 16, WIDTH), F32),
        pltpu.VMEM((PIX + 2 * LATENT, 3 * WIDTH), BF16),
    ]
    return call(resnet_kernel, operands, [((PIX, WIDTH), F32)] * 2, "resnet_block", 15, 1, scratch)


def tap_rows(pieces):
    zeros = jnp.zeros((8 - CHAN, pieces[0].shape[1]), F32)
    return to_low(jnp.concatenate([x for piece in pieces for x in (piece.astype(F32), zeros)], axis=0))


LOG2E = 1.4426950408889634
TEXT_ROWS = 128


def transformer_kernel(
    tokens_ref, resnet_ref, text_ref, vec_ref, ones_ref, sel_ref, w_kv2_ref,
    w_up_ref, t_down_ref, squares_ref,
    hidden_ref, packed_ref,
    queries, keys, values, text_kv, w_qkv_ref, w_q2_ref, w_o_ref, w_o2_ref,
):
    def vec(i):
        return vec_ref[i : i + 1, :]

    sel = sel_ref[...]
    for j in range(3):
        w_qkv_ref[:, j * SLOTS : (j + 1) * SLOTS] = to_low(dot(squares_ref[1 + j], sel))
    w_q2 = to_low(dot(squares_ref[5], sel))
    w_o = to_low(dot_tn(sel, squares_ref[4]))
    w_o2 = to_low(dot_tn(sel, squares_ref[6]))
    w_q2_ref[...] = w_q2
    w_o_ref[...] = w_o
    w_o2_ref[...] = w_o2
    lane = lax.broadcasted_iota(jnp.int32, (CHUNK, SLOTS), 1)
    counter = jnp.where(lane % SLOT == HEAD_DIM, 1.0, 0.0)

    def project(i):
        a = to_low(normal_parts(tokens_ref[chunk_rows(i), :])[0] * vec(10) + vec(11))
        qkv = dot(a, w_qkv_ref[...])
        queries[chunk_rows(i), :] = to_low(qkv[:, :SLOTS])
        keys[chunk_rows(i), :] = to_low(qkv[:, SLOTS : 2 * SLOTS])
        values[chunk_rows(i), :] = to_low(qkv[:, 2 * SLOTS :] + counter)
        return ()

    over_chunks(lambda i: project(i))
    kv = to_low(dot(text_ref[...], w_kv2_ref[...]))
    text_kv[...] = jnp.zeros_like(text_kv)
    wide_kv = jnp.concatenate(
        [dot(kv[:, :WIDTH], sel_ref[...]), dot(kv[:, WIDTH:], sel_ref[...])], axis=1
    )
    text_kv[0 : wide_kv.shape[0], :] = wide_kv
    text_lane = lax.broadcasted_iota(jnp.int32, (CHUNK, TEXT_ROWS), 1)
    text_bias = jnp.where(text_lane < TEXT_LEN, 0.0, -1e30)

    def chunk_step(i, total):
        tokens = tokens_ref[chunk_rows(i), :]
        side = lax.broadcasted_iota(jnp.int32, (CHUNK, GROUP), 1) < SLOT

        def scores_of(head):
            lanes = slice(head // 2 * GROUP, (head // 2 + 1) * GROUP)
            query = queries[chunk_rows(i), lanes]
            zero = jnp.zeros_like(query)
            own_query = jnp.where(side, query, zero) if head % 2 == 0 else jnp.where(side, zero, query)
            return dot_nt(own_query, keys[:, lanes]) * (SCALE * LOG2E)

        def mixed_of(scores, head):
            lanes = slice(head // 2 * GROUP, (head // 2 + 1) * GROUP)
            raised = jnp.exp2(scores - jnp.max(scores, axis=1, keepdims=True))
            mixed = dot(to_low(raised), values[:, lanes])
            spot = head % 2 * SLOT + HEAD_DIM
            return mixed * (1.0 / mixed[:, spot : spot + 1])

        ahead = scores_of(0)
        mixtures = []
        for head in range(HEADS):
            scores = ahead
            if head + 1 < HEADS:
                ahead = scores_of(head + 1)
            mixtures.append(mixed_of(scores, head))
        pairs = [to_low(jnp.where(side, mixtures[2 * pair], mixtures[2 * pair + 1])) for pair in range(HEADS // 2)]
        tokens = tokens + (dot(jnp.concatenate(pairs, axis=1), w_o_ref[...]) + vec(12))
        c = to_low(normal_parts(tokens)[0] * vec(13) + vec(14))
        query2 = to_low(dot(c, w_q2_ref[...]))
        pairs = []
        for pair in range(HEADS // 2):
            lanes = slice(pair * GROUP, (pair + 1) * GROUP)
            text_keys = lane_halves(to_low(text_kv[:, lanes]))
            text_values = lane_halves(to_low(text_kv[:, SLOTS + pair * GROUP : SLOTS + (pair + 1) * GROUP]))
            scores = dot_nt(query2[:, lanes], text_keys) * SCALE
            probs = []
            for part in (scores[:, :TEXT_ROWS], scores[:, TEXT_ROWS:]):
                part = part + text_bias
                raised = jnp.exp(part - jnp.max(part, axis=1, keepdims=True))
                probs.append(to_low(raised * (1.0 / jnp.sum(raised, axis=1, keepdims=True))))
            pairs.append(to_low(dot(jnp.concatenate(probs, axis=1), text_values)))
        tokens = tokens + (dot(jnp.concatenate(pairs, axis=1), w_o2_ref[...]) + vec(15))
        f = to_low(normal_parts(tokens)[0] * vec(16) + vec(17))
        fed = feed_forward(f, w_up_ref, lambda inner, units: dot_nt(inner, t_down_ref[:, units]))
        tokens = tokens + (fed + vec(18))
        hidden = resnet_ref[chunk_rows(i), :] + (dot(to_low(tokens), squares_ref[7]) + vec(19))
        hidden_ref[chunk_rows(i), :] = hidden
        return (total + column_sum(hidden),)

    (total,) = over_chunks(chunk_step, zero_row())
    centre, scale = group_stats(hidden_ref, ones_ref[...], total)
    pack_rows(packed_ref, lambda rows: (hidden_ref[rows, :] - centre) * scale)


def pack_rows(packed_ref, rows_at):
    for member in range(CLIP):
        block = to_low(rows_at(slice(member * OWN, (member + 1) * OWN)))
        packed_ref[member, 0:64, :] = block[:, 0:128]
        packed_ref[member, 64:128, :] = block[:, 128:256]
        packed_ref[member, 128:160, :] = jnp.concatenate([block[0:32, 256:320], block[32:64, 256:320]], axis=1)


def transformer_block(tokens, resnet, text, vectors, cross_kv, up, down, squares):
    operands = (
        tokens, resnet, text, vectors, group_ones(), slot_selector(), cross_kv, up, down, squares,
    )
    scratch = [pltpu.VMEM((PIX, SLOTS), BF16)] * 3 + [pltpu.VMEM((TEXT_ROWS, 2 * SLOTS), F32)]
    scratch += [pltpu.VMEM((WIDTH, 3 * SLOTS), BF16), pltpu.VMEM((WIDTH, SLOTS), BF16)] + [pltpu.VMEM((SLOTS, WIDTH), BF16)] * 2
    outs = [((PIX, WIDTH), F32), ((CLIP, 160, 128), BF16)]
    return call(transformer_kernel, operands, outs, "transformer_block", 32, 0, scratch)


def head_kernel(
    facts_ref, hidden_ref, branch_ref, pair_ref, vec_ref, ones_ref, w_ref,
    packed_ref, loss_ref,
    mixed, act, slope,
):
    ones = ones_ref[...]
    gain = vec_ref[20:21, :]
    offset = vec_ref[21:22, :]
    column_total = zero_row()
    for member in range(CLIP):
        rows = slice(member * OWN, (member + 1) * OWN)
        last = branch_ref[member, 128:160, :]
        branch = jnp.concatenate(
            [
                branch_ref[member, 0:64, :].astype(F32),
                branch_ref[member, 64:128, :].astype(F32),
                jnp.concatenate([last[:, 0:64], last[:, 64:128]], axis=0).astype(F32),
            ],
            axis=1,
        )
        part = hidden_ref[rows, :] + branch
        mixed[rows, :] = part
        column_total = column_total + column_sum(part)
    centre, scale = group_stats(mixed, ones, column_total)

    def activate(i):
        normal = (mixed[chunk_rows(i), :] - centre) * scale
        mixed[chunk_rows(i), :] = normal
        value = normal * gain + offset
        share = sigmoid(value)
        act[chunk_rows(i), :] = to_low(value * share)
        slope[chunk_rows(i), :] = share * (1.0 + value * (1.0 - share)) * gain
        return ()

    over_chunks(lambda i: activate(i))
    weight = tap_rows([w_ref[tap // 3, tap % 3] for tap in range(TAPS)])
    by_tap = dot_nt(weight, act[...])
    predicted = jnp.zeros((8, PIX), F32)
    for tap in range(TAPS):
        predicted = predicted + shifted_lanes(by_tap[8 * tap : 8 * tap + 8], tap // 3 - 1, tap % 3 - 1)
    pair = pair_ref[...].astype(F32)
    target = facts_ref[0, COS] * jnp.concatenate([pair[CHAN:], pair[:CHAN]], axis=0) - facts_ref[0, SIN] * pair
    target = jnp.where(lax.broadcasted_iota(jnp.int32, pair.shape, 0) < CHAN, target, 0.0)
    residual = (predicted - target) * facts_ref[0, VALID]
    loss_ref[...] = jnp.sum(residual * residual, keepdims=True)
    grad = to_low(2.0 * residual / facts_ref[0, TOTAL]).astype(F32)
    columns = tap_rows([shifted_lanes(grad, 1 - tap // 3, 1 - tap % 3)[:CHAN] for tap in range(TAPS)])
    total = zero_row()
    total_normal = zero_row()
    for i in range(CHUNKS):
        rows = slice(i * CHUNK, (i + 1) * CHUNK)
        part = dot_tn(columns[:, rows], weight) * slope[rows, :]
        slope[rows, :] = part
        total = total + column_sum(part)
        total_normal = total_normal + column_sum(part * mixed[rows, :])
    mean = group_mean(total, ones)
    mean_normal = group_mean(total_normal, ones)
    pack_rows(packed_ref, lambda rows: scale * (slope[rows, :] - mean - mixed[rows, :] * mean_normal))


def head_block(facts, hidden, branch, pair, vectors, weight):
    operands = (facts, hidden, branch, pair, vectors, group_ones(), weight)
    outs = [((CLIP, 160, 128), BF16), ((1, 1), F32)]
    scratch = [pltpu.VMEM((PIX, WIDTH), F32), pltpu.VMEM((PIX, WIDTH), BF16), pltpu.VMEM((PIX, WIDTH), F32)]
    return call(head_kernel, operands, outs, "head_block", 6, 1, scratch, limit=36)


def product(left, right):
    return jnp.einsum("...i,ij->...j", left, right, preferred_element_type=jnp.float32)


def time_embed(step_values, time_w1, time_w2, temb_w, temb_bias):
    half_width = WIDTH // 2
    frequency = jnp.exp(-math.log(10000.0) * jnp.arange(half_width, dtype=jnp.float32) / half_width)
    angles = step_values[..., None] * frequency
    encoding = jnp.concatenate([jnp.cos(angles), jnp.sin(angles)], axis=-1)
    hidden = product(to_low(encoding), time_w1)
    hidden = product(to_low(jax.nn.silu(hidden)), time_w2)
    return product(to_low(jax.nn.silu(hidden)), temb_w) + temb_bias


def swap_cores(values):
    return lax.ppermute(values, "dp", [(0, 1), (1, 0)])


WIRE = jnp.float16
TAIL = 16


def frame_phases():
    size = lax.axis_size("frames")
    phases = []
    shift = 0
    while (1 << shift) < size:
        group = min(4, size >> shift)
        phases.append((shift, group))
        shift += group.bit_length() - 1
    return phases


def frame_digit(shift, group):
    return (lax.axis_index("frames") >> shift) % group


def swap_frames(values, shift, distance):
    size = lax.axis_size("frames")
    return lax.ppermute(values, "frames", [(i, i ^ (distance << shift)) for i in range(size)])


def part_of(terms, start, rows):
    parts = [lax.dynamic_slice_in_dim(term, start, rows + TAIL, 0) for term in terms]
    return functools.reduce(jnp.add, parts)


def coded(terms, start, rows, bound):
    part = part_of(terms, start, rows)
    exponent = jnp.floor(14.0 - jnp.log2(jnp.maximum(bound, 1e-30)))
    place = lax.broadcasted_iota(jnp.int32, (rows + TAIL, 1), 0)
    return jnp.where(place < rows, part * jnp.exp2(exponent), exponent).astype(WIRE)


def exponent_of(message, rows):
    return message[rows : rows + 1].astype(F32)


def reduce_start(terms, bound, shift, group):
    rows = (terms[0].shape[0] - TAIL) // group
    mine = frame_digit(shift, group)
    return [coded(terms, (mine ^ d) * rows, rows, bound) for d in range(1, group)]


def reduce_send(messages, shift):
    return [swap_frames(message, shift, d + 1) for d, message in enumerate(messages)]


def reduce_end(terms, bound, got, shift, group):
    rows = (terms[0].shape[0] - TAIL) // group
    total = part_of(terms, frame_digit(shift, group) * rows, rows)
    for message in got:
        exponent = exponent_of(message, rows)
        total = total + message.astype(F32) * jnp.exp2(-exponent)
        bound = bound + jnp.exp2(15.0 - exponent)
    return [total], bound


def gather_send(block, shift, group):
    return [swap_frames(block, shift, d) for d in range(1, group)]


def gather_end(block, got, shift, group):
    rows = block.shape[0]
    mine = frame_digit(shift, group)
    total = jnp.zeros((group * rows, 128), block.dtype)
    for d, part in enumerate([block] + got):
        total = lax.dynamic_update_slice_in_dim(total, part, (mine ^ d) * rows, 0)
    return total


def decoded(block, piece):
    parts = block.reshape(-1, piece, 128)
    exponent = parts[:, piece - TAIL : piece - TAIL + 1].astype(F32)
    return (parts[:, : piece - TAIL].astype(F32) * jnp.exp2(-exponent)).reshape(-1, 128)


def first_bound(terms, used):
    return functools.reduce(jnp.add, [term[used : used + 1] for term in terms])


def fit_rows(values):
    unit = 8 * lax.axis_size("frames")
    rows = values.shape[0] - TAIL
    padded = -(-rows // unit) * unit
    return jnp.pad(values, ((0, padded - rows), (0, 0))) if padded > rows else values


def sample_groups():
    groups = []
    for block in range(lax.axis_size("frames") // CLIP):
        for half in range(2):
            groups.append(
                [
                    2 * (block * CLIP + half * HALF + place) + core
                    for core in range(2)
                    for place in range(HALF)
                ]
            )
    return groups


def swap_samples(values):
    size = lax.axis_size("frames")
    pairs = []
    for frame in range(size):
        half = (frame % CLIP) // HALF
        pairs.append((2 * frame + 1 - half, 2 * (frame ^ HALF) + half))
    return lax.ppermute(values, ("frames", "dp"), pairs)


def shards(
    latents,
    noise,
    timesteps,
    image_flags,
    frame_counts,
    text,
    conv_in,
    res_convs,
    conv_out,
    time_w1,
    time_w2,
    temb_w,
    spatial_squares,
    cross_kv,
    spatial_up,
    spatial_down,
    frozen_vectors,
    motion_squares,
    motion_up,
    motion_down,
    motion_vectors,
    square_moment,
    up_moment,
    down_moment,
    vector_moment1,
    vector_moment2,
    square_ema,
    up_ema,
    down_ema,
    vector_ema,
):
    dp_index = lax.axis_index("dp")
    place = lax.axis_index("frames")
    block = place // CLIP
    place = place % CLIP
    half = place // HALF
    stays = half == dp_index
    frame = jnp.where(stays, place, (place + HALF) % CLIP)
    pair = jnp.concatenate([latents.reshape(PIX, CHAN).T, noise.reshape(PIX, CHAN).T], axis=0)
    pair = jnp.where(stays, pair, swap_samples(pair))

    def of_block(values):
        return lax.dynamic_index_in_dim(values[0], block, 0, keepdims=False)

    text_rows = of_block(text)
    text_rows = jnp.where(stays, text_rows, swap_cores(text_rows))
    step_values = of_block(timesteps).astype(F32)[None]
    phases = (step_values / 1000.0 + 0.008) / 1.008 * (math.pi / 2)
    temb_res = time_embed(step_values, time_w1, time_w2, temb_w, frozen_vectors[22])
    flag = of_block(image_flags).astype(F32)[None]
    facts = jnp.concatenate([temb_res[0], jnp.cos(phases), jnp.sin(phases), 1.0 - flag, jnp.zeros((61,), F32)])
    facts = facts.reshape(1, 384)
    facts = jnp.where(stays, facts, swap_cores(facts))
    count = lax.dynamic_slice(frame_counts, (half, block), (1, 1)).reshape(1).astype(F32)
    total_count = 4.0 * PIX * jnp.sum(frame_counts).astype(F32)
    valid = (frame.astype(F32) < count).astype(F32)
    more = jnp.concatenate([jnp.zeros((COUNT,), F32), count, valid, total_count[None], jnp.zeros((383 - TOTAL,), F32)])
    facts = facts + more.reshape(1, 384)
    resnet, tokens = resnet_block(
        facts, pair, frozen_vectors, conv_in, res_convs.reshape(2, 3, 3 * WIDTH, WIDTH), spatial_squares
    )
    hidden, packed = transformer_block(
        tokens, resnet, text_rows, frozen_vectors, cross_kv, spatial_up, spatial_down.T, spatial_squares
    )
    groups = sample_groups()

    def exchange(values):
        return lax.all_to_all(
            values, ("frames", "dp"), split_axis=0, concat_axis=0, tiled=True, axis_index_groups=groups
        )

    arrived = exchange(packed)
    weights = prepare(motion_squares, motion_up, motion_down.T)
    branch, u, u2, u3, qkv1, qkv2, o1, o2, last = motion_forward(
        facts, arrived, weights, motion_vectors
    )
    grad, loss_part = head_block(
        facts, hidden, exchange(branch), pair, frozen_vectors, jnp.swapaxes(conv_out, 2, 3),
    )
    grad_in = exchange(grad)
    core = dp_index.reshape(1)
    dz, du4, dbranch, early, early_other = feed_backward(core, facts, grad_in, weights, motion_vectors, u3)
    phases = frame_phases()
    ordered = lax.optimization_barrier

    def gather_last(block, got, piece, rows):
        parts = [decoded(part, piece) for part in [block] + got]
        return gather_end(parts[0], parts[1:], *phases[0])[:rows]

    du4, early_other = ordered((du4, early_other))
    early_got = swap_cores(early_other)
    upper = upper_backward(dz, du4, dbranch, u3, last, motion_vectors, weights)
    early_got, du3, g9, feed_sums = ordered((early_got, *upper))

    early = [early, early_got]
    early_bound = first_bound(early, (UP_TILES + DOWN_TILES) * WIDTH)
    early = [fit_rows(term) for term in early]
    messages = reduce_start(early, early_bound, *phases[0])
    du3, *messages = ordered((du3, *messages))
    got = reduce_send(messages, phases[0][0])
    second = second_backward(du3, facts, weights, motion_vectors, u2, qkv2)
    du2, d_qkv2, second_sums, *got = ordered((*second, *got))
    early, early_bound = reduce_end(early, early_bound, got, *phases[0])

    messages = reduce_start(early, early_bound, *phases[1])
    du2, *messages = ordered((du2, *messages))
    got = reduce_send(messages, phases[1][0])
    first = first_backward(du2, facts, arrived, weights, motion_vectors, u, qkv1)
    du, d_qkv1, first_sums, du3, *got = ordered((*first, du3, *got))
    early, early_bound = reduce_end(early, early_bound, got, *phases[1])
    for shift, group in phases[2:]:
        got = reduce_send(reduce_start(early, early_bound, shift, group), shift)
        early, early_bound = reduce_end(early, early_bound, got, shift, group)
    early_block = coded(early, 0, early[0].shape[0] - TAIL, early_bound)
    early_piece = early_block.shape[0]
    for shift, group in reversed(phases[2:]):
        early_block = gather_end(early_block, gather_send(early_block, shift, group), shift, group)

    du3, early_block = ordered((du3, early_block))
    got = gather_send(early_block, *phases[1])
    later = second_grads(du3, motion_vectors, u2, d_qkv2, o2)
    du2, early_block, *more = ordered((du2, early_block, *later, *got))
    later, got = more[: len(later)], more[len(later) :]
    early_block = gather_end(early_block, got, *phases[1])

    du2, early_block = ordered((du2, early_block))
    early_got = gather_send(early_block, *phases[0])
    late, late_other = first_grads(
        core, facts, loss_part, du2, arrived, motion_vectors, u, d_qkv1, o1, du,
        (*later, g9, feed_sums, second_sums, first_sums),
    )
    late, late_other, early_block, *early_got = ordered((late, late_other, early_block, *early_got))

    late_got = swap_cores(late_other)
    early = gather_last(early_block, early_got, early_piece, EARLY_ROWS - TAIL)
    up_moment_new, down_moment_new, ahead = wide_moments(early, up_moment, down_moment.T)
    ahead, late_got = ordered((ahead, late_got))
    ahead_got = swap_cores(lax.dynamic_slice_in_dim(ahead, (1 - dp_index) * DOWN_TILES, UP_TILES, 0))
    late = [late, late_got]
    late_bound = first_bound(late, 13 * WIDTH)
    late = [fit_rows(term) for term in late]
    messages = reduce_start(late, late_bound, *phases[0])
    ahead_got, *messages = ordered((ahead_got, *messages))
    got = reduce_send(messages, phases[0][0])
    wide = wide_direction(core, ahead, ahead_got)
    wide, *got = ordered((wide, *got))
    late, late_bound = reduce_end(late, late_bound, got, *phases[0])

    wide_got = swap_cores(wide)
    for shift, group in phases[1:]:
        got = reduce_send(reduce_start(late, late_bound, shift, group), shift)
        late, late_bound = reduce_end(late, late_bound, got, shift, group)
    late_block = coded(late, 0, late[0].shape[0] - TAIL, late_bound)
    late_piece = late_block.shape[0]
    for shift, group in reversed(phases[1:]):
        late_block = gather_end(late_block, gather_send(late_block, shift, group), shift, group)
    late_block, wide_got = ordered((late_block, wide_got))
    late_got = gather_send(late_block, *phases[0])
    up_new, up_ema_new, down_new, down_ema_new = wide_update(
        core, wide, wide_got, motion_up, motion_down.T, up_ema, down_ema.T
    )
    late_block, down_ema_new, *late_got = ordered((late_block, down_ema_new, *late_got))
    late = gather_last(late_block, late_got, late_piece, LATE_ROWS - TAIL)
    square, square_moment_new, moment_first, moment_second, vector_new, vector_ema_new, loss_row = directions(
        late, square_moment, vector_moment1, vector_moment2, motion_vectors, vector_ema
    )
    square_got = swap_cores(square)
    halved = motion_squares.reshape(2, 5, WIDTH, WIDTH)
    square_new, square_ema_new = own_squares(core, square, halved, square_ema)
    square_new = other_squares(core, square_got, halved, square_new).reshape(motion_squares.shape)
    return (
        loss_row[0, 0] * (1024.0 * total_count),
        total_count,
        square_new,
        square_moment_new,
        square_ema_new,
        up_new,
        up_moment_new,
        up_ema_new,
        down_new.T,
        down_moment_new.T,
        down_ema_new.T,
        moment_first,
        moment_second,
        vector_new,
        vector_ema_new,
    )


def solution(mesh):
    return jax.shard_map(
        shards,
        mesh=mesh,
        in_specs=(
            P("dp", "frames", None, None),
            P("dp", "frames", None, None),
            P("dp", None),
            P("dp", None),
            P(),
            P("dp", None, None, None),
            P(),
            P(),
            P(),
            P(),
            P(),
            P(),
            P(),
            P(),
            P(),
            P(),
            P(),
            P(),
            P(),
            P(),
            P(),
            P("dp", None, None),
            P(None, "dp"),
            P("dp", None),
            P(),
            P(),
            P("dp", None, None),
            P(None, "dp"),
            P("dp", None),
            P(),
        ),
        out_specs=(
            P(),
            P(),
            P(),
            P("dp", None, None),
            P("dp", None, None),
            P(),
            P(None, "dp"),
            P(None, "dp"),
            P(),
            P("dp", None),
            P("dp", None),
            P(),
            P(),
            P(),
            P(),
        ),
        check_vma=False,
    )
```
